32 devices in a mesh: dp: 8 (over y, x, core), fsdp: 4 (over z).
Axes of the slice: x: 2, y: 2, z: 4, core: 2. Of those that a mesh axis runs over, the one named last changes fastest.
Arguments:
- hidden_in: bfloat16 [32, 128, 960], P(('dp', 'fsdp')), may hold values from -6 to 6
- segment_ids: int32 [32, 128], P(('dp', 'fsdp')), may hold values from 0 to 3, as said below
- positions: int32 [32, 128], P(('dp', 'fsdp')), may hold values from 0 to 2047, as said below
- query_weight: bfloat16 [960, 960], P('fsdp', 'dp'), may hold values from -0.1875 to 0.1875
- key_weight: bfloat16 [960, 320], P('fsdp', 'dp'), may hold values from -0.1875 to 0.1875
- value_weight: bfloat16 [960, 320], P('fsdp', 'dp'), may hold values from -0.1875 to 0.1875
- output_weight: bfloat16 [960, 960], P('fsdp', 'dp'), may hold values from -0.75 to 0.75
- attention_gain: bfloat16 [960], P('dp'), may hold values from 0.099609375 to 1.8984375
- gate_weight: bfloat16 [960, 2560], P('fsdp', 'dp'), may hold values from -0.1875 to 0.1875
- up_weight: bfloat16 [960, 2560], P('fsdp', 'dp'), may hold values from -0.1875 to 0.1875
- down_weight: bfloat16 [2560, 960], P('fsdp', 'dp'), may hold values from -0.125 to 0.125
- feedforward_gain: bfloat16 [960], P('dp'), may hold values from 0.099609375 to 1.8984375
- output_cotangent: bfloat16 [32, 128, 960], P(('dp', 'fsdp')), may hold values from -6 to 6
Outputs:
- block_output: bfloat16 [32, 128, 960], P(('dp', 'fsdp'))
- input_grad: float32 [32, 128, 960], P(('dp', 'fsdp'))
- query_grad: float32 [960, 960], P('fsdp', 'dp')
- key_grad: float32 [960, 320], P('fsdp', 'dp')
- value_grad: float32 [960, 320], P('fsdp', 'dp')
- output_grad: float32 [960, 960], P('fsdp', 'dp')
- attention_gain_grad: float32 [960], P('dp')
- gate_grad: float32 [960, 2560], P('fsdp', 'dp')
- up_grad: float32 [960, 2560], P('fsdp', 'dp')
- down_grad: float32 [2560, 960], P('fsdp', 'dp')
- feedforward_gain_grad: float32 [960], P('dp')
The draws below stay inside these ranges and needn't reach their ends.
Inputs may be any that keep to these rules, and one draw needn't show every extreme that they name: `segment_ids`: each row of 128 tokens holds exactly 4 documents of consecutive tokens, numbered in order from 0. Within a document positions rise by one from token to token; the first document of every row starts at position 0.
All inputs are finite; a program needn't handle non-finite values.
Results may differ from the reference program's by a relative error of at most 0.013.
Values may be sent and summed in bfloat16 or wider, within the bound.
No kernel may reach another device: no remote copies, remote signals or barrier semaphores. Data moves between devices by JAX's collectives and lax.ppermute only.
A program may use at most 192 MiB of HBM per device.

```python
import jax
import jax.numpy as jnp
from jax import lax

D = 960
HEADS = 15
KV_HEADS = 5
HD = 64
FF = 2560
TOK_DEV = 128
DOCS = 4
MAXPOS = 2048
KVD = 320
SEQS = 32


def one_row(row_key):
    key_cuts = jax.random.fold_in(row_key, 1)
    key_offsets = jax.random.fold_in(row_key, 2)
    picked = jax.random.permutation(key_cuts, TOK_DEV - 1)[:DOCS - 1] + 1
    cut_points = jnp.sort(picked).astype(jnp.int32)
    places = jnp.arange(TOK_DEV).astype(jnp.int32)
    segment = jnp.sum((places[:, None] >= cut_points[None, :]).astype(jnp.int32), axis=1).astype(jnp.int32)
    starts = jnp.concatenate([jnp.zeros((1,), jnp.int32), cut_points])
    finishes = jnp.concatenate([cut_points, jnp.full((1,), TOK_DEV, jnp.int32)])
    lengths = finishes - starts
    upper_bound = MAXPOS - lengths + 1
    offsets = jax.random.randint(key_offsets, (DOCS,), 0, upper_bound).astype(jnp.int32)
    offsets = offsets.at[0].set(0)
    offsets = offsets.at[DOCS - 1].set(MAXPOS - lengths[DOCS - 1])
    chosen = (segment[:, None] == jnp.arange(DOCS).astype(jnp.int32)[None, :]).astype(jnp.int32)
    start_here = jnp.sum(chosen * starts[None, :], axis=1)
    offset_here = jnp.sum(chosen * offsets[None, :], axis=1)
    position = places - start_here + offset_here
    return (segment, position.astype(jnp.int32))


def document_layout(key):
    base_key = jax.random.fold_in(key, 17)
    row_keys = jax.random.split(base_key, SEQS)
    return jax.vmap(one_row)(row_keys)


def draw_segment_ids(key, part):
    return document_layout(key)[0]


def draw_positions(key, part):
    return document_layout(key)[1]


def level_of(own_key, dims, cuts, least, top_value):
    loudness = 1.0
    for dim, parts in cuts:
        heights = jax.random.uniform(jax.random.fold_in(jax.random.fold_in(own_key, 6), dim), (parts,), jnp.float32, least / len(cuts), top_value / len(cuts))
        loudness = loudness * jnp.repeat(jnp.exp(heights), dims[dim] // parts).reshape((-1,) + (1,) * (len(dims) - 1 - dim))
    return loudness


def scatter_about(own_key, dims, scale, limit, pieces=(), held_as=jnp.bfloat16):
    values = jax.random.normal(own_key, dims, jnp.float32) * scale
    if len(pieces) > 0:
        values = level_of(own_key, dims, pieces, -0.22, 0.18) * values
    return jnp.clip(values, min=-limit, max=limit).astype(held_as)


def setup_inputs(seed: int = 0) -> dict:
    key_list = jax.random.split(jax.random.key(seed), 14)
    hidden_in = scatter_about(key_list[0], (SEQS, TOK_DEV, D), 1.0, 6.0, ((0, 32),))
    segment_ids = draw_segment_ids(jax.random.fold_in(key_list[13], 71), 0)
    positions = draw_positions(jax.random.fold_in(key_list[13], 71), 0)
    query_weight = scatter_about(key_list[3], (D, D), D ** -0.5, 0.1875, ((0, 4), (1, 8)))
    key_weight = scatter_about(key_list[4], (D, KVD), D ** -0.5, 0.1875, ((0, 4), (1, 8)))
    value_weight = scatter_about(key_list[5], (D, KVD), D ** -0.5, 0.1875, ((0, 4), (1, 8)))
    output_weight = scatter_about(key_list[6], (D, D), (D // 16) ** -0.5, 0.75, ((0, 4), (1, 8)))
    attention_gain = jnp.clip(1.0 + 0.18 * jax.random.normal(key_list[7], (D,), jnp.float32), 0.099609375, 1.8984375).astype(jnp.bfloat16)
    gate_weight = scatter_about(key_list[8], (D, FF), D ** -0.5, 0.1875, ((0, 4), (1, 8)))
    up_weight = scatter_about(key_list[9], (D, FF), D ** -0.5, 0.1875, ((0, 4), (1, 8)))
    down_weight = scatter_about(key_list[10], (FF, D), FF ** -0.5, 0.125, ((0, 4), (1, 8)))
    feedforward_gain = jnp.clip(1.0 + 0.18 * jax.random.normal(key_list[11], (D,), jnp.float32), 0.099609375, 1.8984375).astype(jnp.bfloat16)
    output_cotangent = scatter_about(key_list[12], (SEQS, TOK_DEV, D), 1.0, 6.0, ((0, 32),))
    return dict(hidden_in=hidden_in, segment_ids=segment_ids, positions=positions, query_weight=query_weight, key_weight=key_weight, value_weight=value_weight, output_weight=output_weight, attention_gain=attention_gain, gate_weight=gate_weight, up_weight=up_weight, down_weight=down_weight, feedforward_gain=feedforward_gain, output_cotangent=output_cotangent)


EPS = 1e-05
THETA = 100000.0
NEGATIVE = -1e+30

def rotary_tables(position, head_dim):
    inverse = THETA ** (-jnp.arange(0, head_dim, 2).astype(jnp.float32) / head_dim)
    angles = position.astype(jnp.float32)[:, None] * inverse[None, :]
    cosines = jnp.cos(angles)
    sine_values = jnp.sin(angles)
    return (jnp.concatenate([cosines, cosines], -1), jnp.concatenate([sine_values, sine_values], -1))

def rotate(values, cosines, sine_values):
    half_dim = values.shape[-1] // 2
    turned = jnp.concatenate([-values[..., half_dim:], values[..., :half_dim]], -1)
    return values * cosines[:, None, :] + turned * sine_values[:, None, :]

def rotate_back(gradient, cosines, sine_values):
    half_dim = gradient.shape[-1] // 2
    sine_scaled = gradient * sine_values[:, None, :]
    turned = jnp.concatenate([-sine_scaled[..., half_dim:], sine_scaled[..., :half_dim]], -1)
    return gradient * cosines[:, None, :] - turned

def norm_forward(values, gain):
    row_scale = lax.rsqrt(lax.optimization_barrier(jnp.mean(values * values, -1, keepdims=True)) + EPS)
    return (row_scale, (values * row_scale * gain.astype(jnp.float32)).astype(jnp.bfloat16))

def norm_backward(values, row_scale, gain, upstream):
    unit_rows = values * row_scale
    scaled = upstream * gain.astype(jnp.float32)
    gain_grad = lax.optimization_barrier(jnp.sum(upstream * unit_rows, 0))
    result = row_scale * (scaled - unit_rows * lax.optimization_barrier(jnp.mean(scaled * unit_rows, -1, keepdims=True)))
    return (result, gain_grad)

def contract_first(left, right):
    return jnp.dot(left.T, right, preferred_element_type=jnp.float32)

def contract_last(left, right):
    return jnp.dot(left, right.T, preferred_element_type=jnp.float32)

def masked_scores(grouped, key_turned, segment, head_dim):
    length = grouped.shape[0]
    scores = jnp.einsum('qkgd,tkd->kgqt', grouped.astype(jnp.float32), key_turned.astype(jnp.float32)) * head_dim ** (-0.5)
    index_rows = jnp.arange(length)
    allowed = (segment[:, None] == segment[None, :]) & (index_rows[:, None] >= index_rows[None, :])
    return jnp.where(allowed, scores, NEGATIVE)

def layer_pass(hidden_row, segment, position, cotangent, weights):
    query_weight, key_weight, value_weight, output_weight, attention_gain, gate_weight, up_weight, down_weight, feedforward_gain = weights
    length = hidden_row.shape[0]
    kv_heads = KV_HEADS
    group = HEADS // KV_HEADS
    head_dim = HD
    hidden_rows = hidden_row.astype(jnp.float32)
    scale_one, normed_one = norm_forward(hidden_rows, attention_gain)
    cosines, sine_values = rotary_tables(position, head_dim)
    query_proj = jnp.dot(normed_one, query_weight, preferred_element_type=jnp.float32).reshape(length, HEADS, head_dim)
    key_proj = jnp.dot(normed_one, key_weight, preferred_element_type=jnp.float32).reshape(length, kv_heads, head_dim)
    value_proj = jnp.dot(normed_one, value_weight, preferred_element_type=jnp.float32).reshape(length, kv_heads, head_dim)
    query_turned = rotate(query_proj, cosines, sine_values).astype(jnp.bfloat16)
    key_turned = rotate(key_proj, cosines, sine_values).astype(jnp.bfloat16)
    value_rounded = value_proj.astype(jnp.bfloat16)
    grouped = query_turned.reshape(length, kv_heads, group, head_dim)
    scores = masked_scores(grouped, key_turned, segment, head_dim)
    row_max = lax.optimization_barrier(jnp.max(scores, -1, keepdims=True))
    exponentials = jnp.exp(scores - row_max)
    totals = lax.optimization_barrier(jnp.sum(exponentials, -1, keepdims=True))
    log_total = row_max + jnp.log(totals)
    probs_rounded = (exponentials / totals).astype(jnp.bfloat16)
    attended = jnp.einsum('kgqt,tkd->qkgd', probs_rounded.astype(jnp.float32), value_rounded.astype(jnp.float32))
    attended = attended.reshape(length, HEADS * head_dim).astype(jnp.bfloat16)
    residual = hidden_rows + jnp.dot(attended, output_weight, preferred_element_type=jnp.float32)
    scale_two, normed_two = norm_forward(residual, feedforward_gain)
    gate_proj = jnp.dot(normed_two, gate_weight, preferred_element_type=jnp.float32)
    up_proj = jnp.dot(normed_two, up_weight, preferred_element_type=jnp.float32)
    sigmoid_gate = jax.nn.sigmoid(gate_proj)
    silu_gate = gate_proj * sigmoid_gate
    mixed = (silu_gate * up_proj).astype(jnp.bfloat16)
    block_output = (residual + jnp.dot(mixed, down_weight, preferred_element_type=jnp.float32)).astype(jnp.bfloat16)
    down_grad = contract_first(mixed, cotangent)
    mixed_grad = contract_last(cotangent, down_weight)
    gate_delta = (mixed_grad * up_proj * sigmoid_gate * (1.0 + gate_proj * (1.0 - sigmoid_gate))).astype(jnp.bfloat16)
    up_delta = (mixed_grad * silu_gate).astype(jnp.bfloat16)
    gate_grad = contract_first(normed_two, gate_delta)
    up_grad = contract_first(normed_two, up_delta)
    normed_two_grad = contract_last(gate_delta, gate_weight) + contract_last(up_delta, up_weight)
    residual_part, feedforward_gain_grad = norm_backward(residual, scale_two, feedforward_gain, normed_two_grad)
    residual_grad = cotangent.astype(jnp.float32) + residual_part
    residual_rounded = residual_grad.astype(jnp.bfloat16)
    output_grad = contract_first(attended, residual_rounded)
    attended_grad = contract_last(residual_rounded, output_weight).astype(jnp.bfloat16)
    grad_grouped = attended_grad.reshape(length, kv_heads, group, head_dim).astype(jnp.float32)
    probs_again = jnp.exp(scores - log_total)
    probs_again_rounded = probs_again.astype(jnp.bfloat16)
    value_sum = jnp.einsum('kgqt,qkgd->tkd', probs_again_rounded.astype(jnp.float32), grad_grouped)
    prob_grad = jnp.einsum('qkgd,tkd->kgqt', grad_grouped, value_rounded.astype(jnp.float32))
    inner_rows = lax.optimization_barrier(jnp.sum(probs_again * prob_grad, -1, keepdims=True))
    score_grad = (probs_again * (prob_grad - inner_rows) * head_dim ** (-0.5)).astype(jnp.bfloat16)
    query_delta_raw = jnp.einsum('kgqt,tkd->qkgd', score_grad.astype(jnp.float32), key_turned.astype(jnp.float32)).reshape(length, HEADS, head_dim)
    key_sum = jnp.einsum('kgqt,qkgd->tkd', score_grad.astype(jnp.float32), grouped.astype(jnp.float32))
    query_delta = rotate_back(query_delta_raw, cosines, sine_values).reshape(length, HEADS * head_dim).astype(jnp.bfloat16)
    key_delta = rotate_back(key_sum, cosines, sine_values).reshape(length, kv_heads * head_dim).astype(jnp.bfloat16)
    value_delta = value_sum.reshape(length, kv_heads * head_dim).astype(jnp.bfloat16)
    query_grad = contract_first(normed_one, query_delta)
    key_grad = contract_first(normed_one, key_delta)
    value_grad = contract_first(normed_one, value_delta)
    normed_one_grad = contract_last(query_delta, query_weight) + contract_last(key_delta, key_weight) + contract_last(value_delta, value_weight)
    input_part, attention_gain_grad = norm_backward(hidden_rows, scale_one, attention_gain, normed_one_grad)
    input_grad = residual_grad + input_part
    gradients = (query_grad, key_grad, value_grad, output_grad, attention_gain_grad, gate_grad, up_grad, down_grad, feedforward_gain_grad)
    return (block_output, input_grad, gradients)

def reference(hidden_in, segment_ids, positions, query_weight, key_weight, value_weight, output_weight, attention_gain, gate_weight, up_weight, down_weight, feedforward_gain, output_cotangent):
    weights = (query_weight, key_weight, value_weight, output_weight, attention_gain, gate_weight, up_weight, down_weight, feedforward_gain)

    def one_sequence(running, inputs):
        hidden_row, segment, position, cotangent = inputs
        block_output, input_grad, gradients = layer_pass(hidden_row, segment, position, cotangent, weights)
        running = tuple((summed + gradient for summed, gradient in zip(running, gradients)))
        return (running, (block_output, input_grad))
    initial = tuple((jnp.zeros(weight_array.shape, jnp.float32) for weight_array in weights))
    totals, stacked = lax.scan(one_sequence, initial, (hidden_in, segment_ids, positions, output_cotangent))
    return (stacked[0], stacked[1], totals[0], totals[1], totals[2], totals[3], totals[4], totals[5], totals[6], totals[7], totals[8])
```

```python
import jax
import jax.numpy as jnp
from jax import lax
from jax.sharding import PartitionSpec as P

HEADS = 15
KV_HEADS = 5
HD = 64
GROUP = HEADS // KV_HEADS


EPS = 1e-05
THETA = 100000.0
NEGATIVE = -1e30
F32 = jnp.float32
BF16 = jnp.bfloat16


def rotary_tables(position, head_dim):
    inverse = THETA ** (-jnp.arange(0, head_dim, 2).astype(F32) / head_dim)
    angles = position.astype(F32)[:, None] * inverse[None, :]
    cosines = jnp.cos(angles)
    sine_values = jnp.sin(angles)
    return (
        jnp.concatenate([cosines, cosines], -1),
        jnp.concatenate([sine_values, sine_values], -1),
    )


def rotate(values, cosines, sine_values):
    half_dim = values.shape[-1] // 2
    turned = jnp.concatenate([-values[..., half_dim:], values[..., :half_dim]], -1)
    return values * cosines[:, None, :] + turned * sine_values[:, None, :]


def rotate_back(gradient, cosines, sine_values):
    half_dim = gradient.shape[-1] // 2
    sine_scaled = gradient * sine_values[:, None, :]
    turned = jnp.concatenate([-sine_scaled[..., half_dim:], sine_scaled[..., :half_dim]], -1)
    return gradient * cosines[:, None, :] - turned


def row_scale_of(values):
    return lax.rsqrt(jnp.mean(values * values, -1, keepdims=True) + EPS)


def norm_backward(values, row_scale, gain, upstream):
    unit_rows = values * row_scale
    scaled = upstream * gain
    gain_grad = jnp.sum(upstream * unit_rows, 0)
    result = row_scale * (scaled - unit_rows * jnp.mean(scaled * unit_rows, -1, keepdims=True))
    return (result, gain_grad)


def dot(left, right):
    return jnp.dot(left, right, preferred_element_type=F32)


def contract_first(left, right):
    return lax.dot_general(left, right, (((0,), (0,)), ((), ())), preferred_element_type=F32)


def contract_last(left, right):
    return lax.dot_general(left, right, (((1,), (1,)), ((), ())), preferred_element_type=F32)


def send(values, axis, distance):
    count = lax.axis_size(axis)
    return lax.ppermute(values, axis, [(i, i ^ distance) for i in range(count)])


def pick(blocks, index):
    return lax.dynamic_index_in_dim(blocks, index, 0, keepdims=False)


def reorder(blocks, me):
    return jnp.stack([pick(blocks, me ^ s) for s in range(blocks.shape[0])])


def plane_gather(values):
    count = lax.axis_size("dp")
    if count != 8:
        return reorder(lax.all_gather(values, "dp"), lax.axis_index("dp"))
    slots = [values, send(values, "dp", 1)] + [None] * 6
    for s in (2, 4, 6):
        slots[s] = send(values, "dp", s)
        slots[s + 1] = send(slots[s], "dp", 1)
    return jnp.stack(slots)


def plane_exchange(blocks):
    count = lax.axis_size("dp")
    if count != 8:
        me = lax.axis_index("dp")
        return reorder(lax.all_to_all(reorder(blocks, me), "dp", 0, 0), me)
    return jnp.stack([blocks[0]] + [send(blocks[s], "dp", s) for s in range(1, 8)])


def plane_sum(blocks):
    count = lax.axis_size("dp")
    if count != 8:
        return jnp.sum(plane_exchange(blocks.astype(BF16)).astype(F32), 0)
    odd = send(jnp.stack([blocks[s] for s in (1, 3, 5, 7)]).astype(BF16), "dp", 1)
    pair = [blocks[2 * i] + odd[i].astype(F32) for i in range(4)]
    total = pair[0]
    for i in range(1, 4):
        total = total + send(pair[i].astype(BF16), "dp", 2 * i).astype(F32)
    return total


def line_gather(values):
    me = lax.axis_index("fsdp")
    count = lax.axis_size("fsdp")
    out = jnp.zeros((count,) + values.shape, values.dtype)
    out = lax.dynamic_update_index_in_dim(out, values, me, 0)
    for s in range(1, count):
        out = lax.dynamic_update_index_in_dim(out, send(values, "fsdp", s), me ^ s, 0)
    return out


def line_sum(blocks):
    me = lax.axis_index("fsdp")
    total = pick(blocks, me)
    for s in range(1, lax.axis_size("fsdp")):
        total = total + send(pick(blocks, me ^ s).astype(BF16), "fsdp", s).astype(F32)
    return total


def down_routes(dp_count, fsdp_count):
    ratio = dp_count // fsdp_count
    routes = []
    for m in range(ratio):
        pairs = []
        for d in range(dp_count):
            for f in range(fsdp_count):
                target = (ratio * f + (m + d) % ratio) * fsdp_count + d // ratio
                pairs.append((d * fsdp_count + f, target))
        routes.append(pairs)
    return routes


def down_pieces(down_turned, dp_count, fsdp_count):
    ratio = dp_count // fsdp_count
    d = lax.axis_index("dp")
    width = down_turned.shape[1] // ratio
    halves = jnp.stack([down_turned[:, h * width : (h + 1) * width] for h in range(ratio)])
    got = [
        lax.ppermute(pick(halves, (m + d) % ratio), ("dp", "fsdp"), pairs)
        for m, pairs in enumerate(down_routes(dp_count, fsdp_count))
    ]
    stacked = jnp.stack(got)
    ordered = [pick(stacked, (d - j) % ratio) for j in range(ratio)]
    return jnp.concatenate(ordered, 0)


def down_return(grad_turned, dp_count, fsdp_count):
    ratio = dp_count // fsdp_count
    d = lax.axis_index("dp")
    height = grad_turned.shape[0] // ratio
    pieces = grad_turned.reshape(ratio, height, grad_turned.shape[1])
    got = []
    for m, pairs in enumerate(down_routes(dp_count, fsdp_count)):
        back = [(target, source) for source, target in pairs]
        got.append(lax.ppermute(pick(pieces, (d - m) % ratio), ("dp", "fsdp"), back))
    stacked = jnp.stack(got)
    return jnp.concatenate([pick(stacked, (h - d) % ratio) for h in range(ratio)], 1)


def masked_scores(query_turned, key_turned, segment):
    length = query_turned.shape[0]
    grouped = query_turned.reshape(length, KV_HEADS, GROUP, HD)
    scores = jnp.einsum("qkgd,tkd->kgqt", grouped, key_turned, preferred_element_type=F32)
    index = jnp.arange(length)
    allowed = (segment[:, None] == segment[None, :]) & (index[:, None] >= index[None, :])
    return jnp.where(allowed, scores * HD ** (-0.5), NEGATIVE)


def attend_forward(query_turned, key_turned, value_rounded, segment):
    length = query_turned.shape[0]
    scores = masked_scores(query_turned, key_turned, segment)
    row_max = jnp.max(scores, -1, keepdims=True)
    exponentials = jnp.exp(scores - row_max)
    totals = jnp.sum(exponentials, -1, keepdims=True)
    probs_rounded = (exponentials / totals).astype(BF16)
    attended = jnp.einsum("kgqt,tkd->qkgd", probs_rounded, value_rounded, preferred_element_type=F32)
    return (attended.reshape(length, HEADS * HD).astype(BF16), row_max + jnp.log(totals))


def attend_backward(query_turned, key_turned, value_rounded, segment, log_totals, attended_grad):
    length = query_turned.shape[0]
    grouped = query_turned.reshape(length, KV_HEADS, GROUP, HD)
    grad_grouped = attended_grad.reshape(length, KV_HEADS, GROUP, HD)
    scores = masked_scores(query_turned, key_turned, segment)
    probs_again = jnp.exp(scores - log_totals)
    value_sum = jnp.einsum(
        "kgqt,qkgd->tkd", probs_again.astype(BF16), grad_grouped, preferred_element_type=F32
    )
    prob_grad = jnp.einsum(
        "qkgd,tkd->kgqt", grad_grouped, value_rounded, preferred_element_type=F32
    )
    inner_rows = jnp.sum(probs_again * prob_grad, -1, keepdims=True)
    score_grad = (probs_again * (prob_grad - inner_rows) * HD ** (-0.5)).astype(BF16)
    query_part = jnp.einsum("kgqt,tkd->qkgd", score_grad, key_turned, preferred_element_type=F32)
    key_sum = jnp.einsum("kgqt,qkgd->tkd", score_grad, grouped, preferred_element_type=F32)
    return (query_part.reshape(length, HEADS, HD), key_sum, value_sum)


def local(
    hidden_in,
    segment_ids,
    positions,
    query_weight,
    key_weight,
    value_weight,
    output_weight,
    attention_gain,
    gate_weight,
    up_weight,
    down_weight,
    feedforward_gain,
    output_cotangent,
):
    hidden = hidden_in[0]
    hidden_rows = hidden.astype(F32)
    segment = segment_ids[0]
    cotangent = output_cotangent[0]
    length, features = hidden.shape
    width = HEADS * HD
    kv_width = KV_HEADS * HD
    dp_count = lax.axis_size("dp")
    fsdp_count = lax.axis_size("fsdp")
    d = lax.axis_index("dp")
    f = lax.axis_index("fsdp")
    q_cols = width // dp_count
    kv_cols = kv_width // dp_count
    x_cols = features // dp_count
    own_rows = features // fsdp_count
    qkv_cols = q_cols + 2 * kv_cols
    all_cols = qkv_cols + x_cols
    hidden_units = gate_weight.shape[1]

    attention_block = jnp.concatenate(
        [query_weight, key_weight, value_weight, output_weight], 1
    )
    attention_rows = line_gather(attention_block).reshape(features, all_cols)
    gains = jnp.concatenate(
        [attention_gain, feedforward_gain, jnp.zeros((all_cols - 2 * x_cols,), BF16)]
    )
    gains = jnp.concatenate([gains[None], jnp.zeros((15, all_cols), BF16)])
    slots = plane_gather(jnp.concatenate([attention_rows, gains], 0))
    gains_ordered = reorder(slots[:, features, :], d)
    attention_gain_full = gains_ordered[:, :x_cols].reshape(features).astype(F32)
    feed_gain_full = gains_ordered[:, x_cols : 2 * x_cols].reshape(features).astype(F32)
    qkv_slots = slots[:, :features, :qkv_cols]
    output_slots = slots[:, :features, qkv_cols:]

    down_block = down_pieces(down_weight.T, dp_count, fsdp_count)
    feed_block = jnp.concatenate([gate_weight, up_weight, down_block], 1)
    feed = line_gather(feed_block).reshape(features, 3 * hidden_units)

    tokens = plane_gather(jnp.stack([hidden, cotangent]))
    hidden_all = tokens[:, 0].reshape(dp_count * length, features)
    cotangent_all = tokens[:, 1].reshape(dp_count * length, features)

    scale_one = row_scale_of(hidden_rows)
    normed_one = (hidden_rows * scale_one * attention_gain_full).astype(BF16)
    cosines, sine_values = rotary_tables(positions[0], HD)
    qkv = reorder(jnp.einsum("td,sdc->stc", normed_one, qkv_slots, preferred_element_type=F32), d)

    def columns(start, count):
        part = qkv[:, :, start : start + count]
        return part.transpose(1, 0, 2).reshape(length, dp_count * count)

    query_proj = columns(0, q_cols).reshape(length, HEADS, HD)
    key_proj = columns(q_cols, kv_cols).reshape(length, KV_HEADS, HD)
    value_proj = columns(q_cols + kv_cols, kv_cols).reshape(length, KV_HEADS, HD)
    query_turned = rotate(query_proj, cosines, sine_values).astype(BF16)
    key_turned = rotate(key_proj, cosines, sine_values).astype(BF16)
    value_rounded = value_proj.astype(BF16)
    attended, log_totals = attend_forward(query_turned, key_turned, value_rounded, segment)
    added = reorder(jnp.einsum("td,sdc->stc", attended, output_slots, preferred_element_type=F32), d)
    residual = hidden_rows + added.transpose(1, 0, 2).reshape(length, features)

    scale_two = row_scale_of(residual)
    normed_two = (residual * scale_two * feed_gain_full).astype(BF16)
    normed_two_all = plane_gather(normed_two).reshape(dp_count * length, features)
    gate_up = feed[:, : 2 * hidden_units]
    down_turned = feed[:, 2 * hidden_units :]
    both = dot(normed_two_all, gate_up)
    gate_proj = both[:, :hidden_units]
    up_proj = both[:, hidden_units:]
    mixed_grad = dot(cotangent_all, down_turned)
    sigmoid_gate = jax.nn.sigmoid(gate_proj)
    silu_gate = gate_proj * sigmoid_gate
    mixed = (silu_gate * up_proj).astype(BF16)
    gate_delta = (
        mixed_grad * up_proj * sigmoid_gate * (1.0 + gate_proj * (1.0 - sigmoid_gate))
    ).astype(BF16)
    up_delta = (mixed_grad * silu_gate).astype(BF16)
    deltas = jnp.concatenate([gate_delta, up_delta], 1)
    normed_two_grad = plane_sum(
        contract_last(deltas, gate_up).reshape(dp_count, length, features)
    )
    gate_up_grad = contract_first(normed_two_all, deltas)
    down_grad = contract_first(cotangent_all, mixed)
    feed_grad = jnp.concatenate([gate_up_grad, down_grad], 1).reshape(
        fsdp_count, own_rows, 3 * hidden_units
    )
    fed = plane_sum(contract_last(mixed, down_turned).reshape(dp_count, length, features))
    block_output = (residual + fed).astype(BF16)
    attended_all = plane_gather(attended).reshape(dp_count * length, width)

    residual_part, feed_gain_grad = norm_backward(
        residual, scale_two, feed_gain_full, normed_two_grad
    )
    residual_grad = cotangent.astype(F32) + residual_part
    feed_sum = line_sum(feed_grad)

    residual_rounded = residual_grad.astype(BF16)
    residual_blocks = residual_rounded.reshape(length, dp_count, x_cols).transpose(1, 0, 2)
    residual_slots = reorder(residual_blocks, d)
    attended_grad = jnp.einsum(
        "stc,sdc->td", residual_slots, output_slots, preferred_element_type=F32
    ).astype(BF16)
    query_raw, key_raw, value_raw = attend_backward(
        query_turned, key_turned, value_rounded, segment, log_totals, attended_grad
    )
    query_delta = rotate_back(query_raw, cosines, sine_values).astype(BF16)
    key_delta = rotate_back(key_raw, cosines, sine_values).astype(BF16)
    value_delta = value_raw.astype(BF16)
    qkv_delta = jnp.concatenate(
        [
            part.reshape(length, dp_count, -1).transpose(1, 0, 2)
            for part in (query_delta, key_delta, value_delta)
        ],
        2,
    )
    delta_slots = reorder(qkv_delta, d)
    normed_one_grad = jnp.einsum(
        "stc,sdc->td", delta_slots, qkv_slots, preferred_element_type=F32
    )
    input_part, attention_gain_grad = norm_backward(
        hidden_rows, scale_one, attention_gain_full, normed_one_grad
    )
    input_grad = residual_grad + input_part

    gain_rows = jnp.concatenate(
        [
            feed_gain_grad.reshape(dp_count, 1, x_cols),
            attention_gain_grad.reshape(dp_count, 1, x_cols),
            jnp.zeros((dp_count, 1, all_cols - 2 * x_cols), F32),
        ],
        2,
    ).astype(BF16)
    gain_rows = jnp.pad(reorder(gain_rows, d), ((0, 0), (0, 15), (0, 0)))
    outgoing = jnp.concatenate(
        [jnp.concatenate([delta_slots, residual_slots], 2), gain_rows], 1
    )
    arrived = plane_exchange(outgoing)
    deltas_all = arrived[:, :length].reshape(dp_count * length, all_cols)
    gain_sums = jnp.sum(arrived[:, length].astype(F32), 0)
    hidden_all_rows = hidden_all.astype(F32)
    normed_one_all = (
        hidden_all_rows * row_scale_of(hidden_all_rows) * attention_gain_full
    ).astype(BF16)
    qkv_grad = contract_first(normed_one_all, deltas_all[:, :qkv_cols])
    output_grad = contract_first(attended_all, deltas_all[:, qkv_cols:])
    attention_grad = jnp.concatenate([qkv_grad, output_grad], 1).reshape(
        fsdp_count, own_rows, all_cols
    )
    gain_block = jnp.broadcast_to(
        jnp.pad(gain_sums[None], ((0, 15), (0, 0)))[None], (fsdp_count, 16, all_cols)
    )
    attention_sum = line_sum(jnp.concatenate([attention_grad, gain_block], 1))
    down_out = down_return(feed_sum[:, 2 * hidden_units :], dp_count, fsdp_count).T

    ends = (q_cols, q_cols + kv_cols, qkv_cols)
    return (
        block_output[None],
        input_grad[None],
        attention_sum[:own_rows, : ends[0]],
        attention_sum[:own_rows, ends[0] : ends[1]],
        attention_sum[:own_rows, ends[1] : ends[2]],
        attention_sum[:own_rows, ends[2] :],
        attention_sum[own_rows, x_cols : 2 * x_cols],
        feed_sum[:, :hidden_units],
        feed_sum[:, hidden_units : 2 * hidden_units],
        down_out,
        attention_sum[own_rows, :x_cols],
    )


def solution(mesh):
    in_specs = (
        P(("dp", "fsdp"), None, None),
        P(("dp", "fsdp"), None),
        P(("dp", "fsdp"), None),
        P("fsdp", "dp"),
        P("fsdp", "dp"),
        P("fsdp", "dp"),
        P("fsdp", "dp"),
        P("dp"),
        P("fsdp", "dp"),
        P("fsdp", "dp"),
        P("fsdp", "dp"),
        P("dp"),
        P(("dp", "fsdp"), None, None),
    )
    out_specs = (
        P(("dp", "fsdp"), None, None),
        P(("dp", "fsdp"), None, None),
        P("fsdp", "dp"),
        P("fsdp", "dp"),
        P("fsdp", "dp"),
        P("fsdp", "dp"),
        P("dp"),
        P("fsdp", "dp"),
        P("fsdp", "dp"),
        P("fsdp", "dp"),
        P("dp"),
    )
    return jax.shard_map(local, mesh=mesh, in_specs=in_specs, out_specs=out_specs, check_vma=False)
```

```python
import jax
import jax.numpy as jnp
from jax import lax
from jax.experimental import pallas as pl
from jax.experimental.pallas import tpu as pltpu
from jax.sharding import PartitionSpec as P

HEADS = 15
KV_HEADS = 5
HD = 64
GROUP = HEADS // KV_HEADS


EPS = 1e-05
THETA = 100000.0
NEGATIVE = -1e30
F32 = jnp.float32
BF16 = jnp.bfloat16


def rotary_tables(position, head_dim):
    inverse = THETA ** (-jnp.arange(0, head_dim, 2).astype(F32) / head_dim)
    angles = position.astype(F32)[:, None] * inverse[None, :]
    cosines = jnp.cos(angles)
    sine_values = jnp.sin(angles)
    return (
        jnp.concatenate([cosines, cosines], -1),
        jnp.concatenate([sine_values, sine_values], -1),
    )


def rotate(values, cosines, sine_values):
    half_dim = values.shape[-1] // 2
    turned = jnp.concatenate([-values[..., half_dim:], values[..., :half_dim]], -1)
    return values * cosines[:, None, :] + turned * sine_values[:, None, :]


def rotate_back(gradient, cosines, sine_values):
    half_dim = gradient.shape[-1] // 2
    sine_scaled = gradient * sine_values[:, None, :]
    turned = jnp.concatenate([-sine_scaled[..., half_dim:], sine_scaled[..., :half_dim]], -1)
    return gradient * cosines[:, None, :] - turned


def row_scale_of(values):
    return lax.rsqrt(jnp.mean(values * values, -1, keepdims=True) + EPS)


def norm_backward(values, row_scale, gain, upstream):
    unit_rows = values * row_scale
    scaled = upstream * gain
    gain_grad = jnp.sum(upstream * unit_rows, 0)
    result = row_scale * (scaled - unit_rows * jnp.mean(scaled * unit_rows, -1, keepdims=True))
    return (result, gain_grad)


def dot(left, right):
    return jnp.dot(left, right, preferred_element_type=F32)


def contract_first(left, right):
    return lax.dot_general(left, right, (((0,), (0,)), ((), ())), preferred_element_type=F32)


def contract_last(left, right):
    return lax.dot_general(left, right, (((1,), (1,)), ((), ())), preferred_element_type=F32)


def send(values, axis, distance):
    count = lax.axis_size(axis)
    return lax.ppermute(values, axis, [(i, i ^ distance) for i in range(count)])


def pick(blocks, index):
    return lax.dynamic_index_in_dim(blocks, index, 0, keepdims=False)


def reorder(blocks, me):
    return jnp.stack([pick(blocks, me ^ s) for s in range(blocks.shape[0])])


def plane_gather(values):
    count = lax.axis_size("dp")
    if count != 8:
        return reorder(lax.all_gather(values, "dp"), lax.axis_index("dp"))
    slots = [values, send(values, "dp", 1)] + [None] * 6
    for s in (2, 4, 6):
        slots[s] = send(values, "dp", s)
        slots[s + 1] = send(slots[s], "dp", 1)
    return jnp.stack(slots)


def plane_exchange(blocks):
    count = lax.axis_size("dp")
    if count != 8:
        me = lax.axis_index("dp")
        return reorder(lax.all_to_all(reorder(blocks, me), "dp", 0, 0), me)
    return jnp.stack([blocks[0]] + [send(blocks[s], "dp", s) for s in range(1, 8)])


def plane_sum(blocks):
    count = lax.axis_size("dp")
    if count != 8:
        return jnp.sum(plane_exchange(blocks.astype(BF16)).astype(F32), 0)
    odd = send(jnp.stack([blocks[s] for s in (1, 3, 5, 7)]).astype(BF16), "dp", 1)
    pair = [blocks[2 * i] + odd[i].astype(F32) for i in range(4)]
    total = pair[0]
    for i in range(1, 4):
        total = total + send(pair[i].astype(BF16), "dp", 2 * i).astype(F32)
    return total


def line_gather(values):
    me = lax.axis_index("fsdp")
    count = lax.axis_size("fsdp")
    out = jnp.zeros((count,) + values.shape, values.dtype)
    out = lax.dynamic_update_index_in_dim(out, values, me, 0)
    for s in range(1, count):
        out = lax.dynamic_update_index_in_dim(out, send(values, "fsdp", s), me ^ s, 0)
    return out


def line_sum(blocks):
    me = lax.axis_index("fsdp")
    total = pick(blocks, me)
    for s in range(1, lax.axis_size("fsdp")):
        total = total + send(pick(blocks, me ^ s).astype(BF16), "fsdp", s).astype(F32)
    return total


def down_routes(dp_count, fsdp_count):
    ratio = dp_count // fsdp_count
    routes = []
    for m in range(ratio):
        pairs = []
        for d in range(dp_count):
            for f in range(fsdp_count):
                target = (ratio * f + (m + d) % ratio) * fsdp_count + d // ratio
                pairs.append((d * fsdp_count + f, target))
        routes.append(pairs)
    return routes


def down_pieces(down_turned, dp_count, fsdp_count):
    ratio = dp_count // fsdp_count
    d = lax.axis_index("dp")
    width = down_turned.shape[1] // ratio
    halves = jnp.stack([down_turned[:, h * width : (h + 1) * width] for h in range(ratio)])
    got = [
        lax.ppermute(pick(halves, (m + d) % ratio), ("dp", "fsdp"), pairs)
        for m, pairs in enumerate(down_routes(dp_count, fsdp_count))
    ]
    stacked = jnp.stack(got)
    ordered = [pick(stacked, (d - j) % ratio) for j in range(ratio)]
    return jnp.concatenate(ordered, 0)


def down_return(grad_turned, dp_count, fsdp_count):
    ratio = dp_count // fsdp_count
    d = lax.axis_index("dp")
    height = grad_turned.shape[0] // ratio
    pieces = grad_turned.reshape(ratio, height, grad_turned.shape[1])
    got = []
    for m, pairs in enumerate(down_routes(dp_count, fsdp_count)):
        back = [(target, source) for source, target in pairs]
        got.append(lax.ppermute(pick(pieces, (d - m) % ratio), ("dp", "fsdp"), back))
    stacked = jnp.stack(got)
    return jnp.concatenate([pick(stacked, (h - d) % ratio) for h in range(ratio)], 1)


def masked_scores(query_turned, key_turned, segment):
    length = query_turned.shape[0]
    grouped = query_turned.reshape(length, KV_HEADS, GROUP, HD)
    scores = jnp.einsum("qkgd,tkd->kgqt", grouped, key_turned, preferred_element_type=F32)
    index = jnp.arange(length)
    allowed = (segment[:, None] == segment[None, :]) & (index[:, None] >= index[None, :])
    return jnp.where(allowed, scores * HD ** (-0.5), NEGATIVE)


def attend_forward(query_turned, key_turned, value_rounded, segment):
    length = query_turned.shape[0]
    scores = masked_scores(query_turned, key_turned, segment)
    row_max = jnp.max(scores, -1, keepdims=True)
    exponentials = jnp.exp(scores - row_max)
    totals = jnp.sum(exponentials, -1, keepdims=True)
    probs_rounded = (exponentials / totals).astype(BF16)
    attended = jnp.einsum("kgqt,tkd->qkgd", probs_rounded, value_rounded, preferred_element_type=F32)
    return (attended.reshape(length, HEADS * HD).astype(BF16), row_max + jnp.log(totals))


def attend_backward(query_turned, key_turned, value_rounded, segment, log_totals, attended_grad):
    length = query_turned.shape[0]
    grouped = query_turned.reshape(length, KV_HEADS, GROUP, HD)
    grad_grouped = attended_grad.reshape(length, KV_HEADS, GROUP, HD)
    scores = masked_scores(query_turned, key_turned, segment)
    probs_again = jnp.exp(scores - log_totals)
    value_sum = jnp.einsum(
        "kgqt,qkgd->tkd", probs_again.astype(BF16), grad_grouped, preferred_element_type=F32
    )
    prob_grad = jnp.einsum(
        "qkgd,tkd->kgqt", grad_grouped, value_rounded, preferred_element_type=F32
    )
    inner_rows = jnp.sum(probs_again * prob_grad, -1, keepdims=True)
    score_grad = (probs_again * (prob_grad - inner_rows) * HD ** (-0.5)).astype(BF16)
    query_part = jnp.einsum("kgqt,tkd->qkgd", score_grad, key_turned, preferred_element_type=F32)
    key_sum = jnp.einsum("kgqt,qkgd->tkd", score_grad, grouped, preferred_element_type=F32)
    return (query_part.reshape(length, HEADS, HD), key_sum, value_sum)


def local(
    hidden_in,
    segment_ids,
    positions,
    query_weight,
    key_weight,
    value_weight,
    output_weight,
    attention_gain,
    gate_weight,
    up_weight,
    down_weight,
    feedforward_gain,
    output_cotangent,
):
    hidden = hidden_in[0]
    hidden_rows = hidden.astype(F32)
    segment = segment_ids[0]
    cotangent = output_cotangent[0]
    length, features = hidden.shape
    width = HEADS * HD
    kv_width = KV_HEADS * HD
    dp_count = lax.axis_size("dp")
    fsdp_count = lax.axis_size("fsdp")
    d = lax.axis_index("dp")
    f = lax.axis_index("fsdp")
    q_cols = width // dp_count
    kv_cols = kv_width // dp_count
    x_cols = features // dp_count
    own_rows = features // fsdp_count
    qkv_cols = q_cols + 2 * kv_cols
    all_cols = qkv_cols + x_cols
    hidden_units = gate_weight.shape[1]

    attention_block = jnp.concatenate(
        [query_weight, key_weight, value_weight, output_weight], 1
    )
    attention_rows = line_gather(attention_block).reshape(features, all_cols)
    gains = jnp.concatenate(
        [attention_gain, feedforward_gain, jnp.zeros((all_cols - 2 * x_cols,), BF16)]
    )
    gains = jnp.concatenate([gains[None], jnp.zeros((15, all_cols), BF16)])
    slots = plane_gather(jnp.concatenate([attention_rows, gains], 0))
    gains_ordered = reorder(slots[:, features, :], d)
    attention_gain_full = gains_ordered[:, :x_cols].reshape(features).astype(F32)
    feed_gain_full = gains_ordered[:, x_cols : 2 * x_cols].reshape(features).astype(F32)
    qkv_slots = slots[:, :features, :qkv_cols]
    output_slots = slots[:, :features, qkv_cols:]

    down_block = down_pieces(down_weight.T, dp_count, fsdp_count)
    feed_block = jnp.concatenate([gate_weight, up_weight, down_block], 1)
    feed = line_gather(feed_block).reshape(features, 3 * hidden_units)

    tokens = plane_gather(jnp.stack([hidden, cotangent]))
    hidden_all = tokens[:, 0].reshape(dp_count * length, features)
    cotangent_all = tokens[:, 1].reshape(dp_count * length, features)

    scale_one = row_scale_of(hidden_rows)
    normed_one = (hidden_rows * scale_one * attention_gain_full).astype(BF16)
    cosines, sine_values = rotary_tables(positions[0], HD)
    qkv = reorder(jnp.einsum("td,sdc->stc", normed_one, qkv_slots, preferred_element_type=F32), d)

    def columns(start, count):
        part = qkv[:, :, start : start + count]
        return part.transpose(1, 0, 2).reshape(length, dp_count * count)

    query_proj = columns(0, q_cols).reshape(length, HEADS, HD)
    key_proj = columns(q_cols, kv_cols).reshape(length, KV_HEADS, HD)
    value_proj = columns(q_cols + kv_cols, kv_cols).reshape(length, KV_HEADS, HD)
    query_turned = rotate(query_proj, cosines, sine_values).astype(BF16)
    key_turned = rotate(key_proj, cosines, sine_values).astype(BF16)
    value_rounded = value_proj.astype(BF16)
    attended, log_totals = attend_forward(query_turned, key_turned, value_rounded, segment)
    added = reorder(jnp.einsum("td,sdc->stc", attended, output_slots, preferred_element_type=F32), d)
    residual = hidden_rows + added.transpose(1, 0, 2).reshape(length, features)

    scale_two = row_scale_of(residual)
    normed_two = (residual * scale_two * feed_gain_full).astype(BF16)
    normed_two_all = plane_gather(normed_two).reshape(dp_count * length, features)
    gate_up = feed[:, : 2 * hidden_units]
    down_turned = feed[:, 2 * hidden_units :]
    both = dot(normed_two_all, gate_up)
    gate_proj = both[:, :hidden_units]
    up_proj = both[:, hidden_units:]
    mixed_grad = dot(cotangent_all, down_turned)
    sigmoid_gate = jax.nn.sigmoid(gate_proj)
    silu_gate = gate_proj * sigmoid_gate
    mixed = (silu_gate * up_proj).astype(BF16)
    gate_delta = (
        mixed_grad * up_proj * sigmoid_gate * (1.0 + gate_proj * (1.0 - sigmoid_gate))
    ).astype(BF16)
    up_delta = (mixed_grad * silu_gate).astype(BF16)
    deltas = jnp.concatenate([gate_delta, up_delta], 1)
    normed_two_grad = plane_sum(
        contract_last(deltas, gate_up).reshape(dp_count, length, features)
    )
    gate_up_grad = contract_first(normed_two_all, deltas)
    down_grad = contract_first(cotangent_all, mixed)
    feed_grad = jnp.concatenate([gate_up_grad, down_grad], 1).reshape(
        fsdp_count, own_rows, 3 * hidden_units
    )
    fed = plane_sum(contract_last(mixed, down_turned).reshape(dp_count, length, features))
    block_output = (residual + fed).astype(BF16)
    attended_all = plane_gather(attended).reshape(dp_count * length, width)

    residual_part, feed_gain_grad = norm_backward(
        residual, scale_two, feed_gain_full, normed_two_grad
    )
    residual_grad = cotangent.astype(F32) + residual_part
    feed_sum = line_sum(feed_grad)

    residual_rounded = residual_grad.astype(BF16)
    residual_blocks = residual_rounded.reshape(length, dp_count, x_cols).transpose(1, 0, 2)
    residual_slots = reorder(residual_blocks, d)
    attended_grad = jnp.einsum(
        "stc,sdc->td", residual_slots, output_slots, preferred_element_type=F32
    ).astype(BF16)
    query_raw, key_raw, value_raw = attend_backward(
        query_turned, key_turned, value_rounded, segment, log_totals, attended_grad
    )
    query_delta = rotate_back(query_raw, cosines, sine_values).astype(BF16)
    key_delta = rotate_back(key_raw, cosines, sine_values).astype(BF16)
    value_delta = value_raw.astype(BF16)
    qkv_delta = jnp.concatenate(
        [
            part.reshape(length, dp_count, -1).transpose(1, 0, 2)
            for part in (query_delta, key_delta, value_delta)
        ],
        2,
    )
    delta_slots = reorder(qkv_delta, d)
    normed_one_grad = jnp.einsum(
        "stc,sdc->td", delta_slots, qkv_slots, preferred_element_type=F32
    )
    input_part, attention_gain_grad = norm_backward(
        hidden_rows, scale_one, attention_gain_full, normed_one_grad
    )
    input_grad = residual_grad + input_part

    gain_rows = jnp.concatenate(
        [
            feed_gain_grad.reshape(dp_count, 1, x_cols),
            attention_gain_grad.reshape(dp_count, 1, x_cols),
            jnp.zeros((dp_count, 1, all_cols - 2 * x_cols), F32),
        ],
        2,
    ).astype(BF16)
    gain_rows = jnp.pad(reorder(gain_rows, d), ((0, 0), (0, 15), (0, 0)))
    outgoing = jnp.concatenate(
        [jnp.concatenate([delta_slots, residual_slots], 2), gain_rows], 1
    )
    arrived = plane_exchange(outgoing)
    deltas_all = arrived[:, :length].reshape(dp_count * length, all_cols)
    gain_sums = jnp.sum(arrived[:, length].astype(F32), 0)
    hidden_all_rows = hidden_all.astype(F32)
    normed_one_all = (
        hidden_all_rows * row_scale_of(hidden_all_rows) * attention_gain_full
    ).astype(BF16)
    qkv_grad = contract_first(normed_one_all, deltas_all[:, :qkv_cols])
    output_grad = contract_first(attended_all, deltas_all[:, qkv_cols:])
    attention_grad = jnp.concatenate([qkv_grad, output_grad], 1).reshape(
        fsdp_count, own_rows, all_cols
    )
    gain_block = jnp.broadcast_to(
        jnp.pad(gain_sums[None], ((0, 15), (0, 0)))[None], (fsdp_count, 16, all_cols)
    )
    attention_sum = line_sum(jnp.concatenate([attention_grad, gain_block], 1))
    down_out = down_return(feed_sum[:, 2 * hidden_units :], dp_count, fsdp_count).T

    ends = (q_cols, q_cols + kv_cols, qkv_cols)
    return (
        block_output[None],
        input_grad[None],
        attention_sum[:own_rows, : ends[0]],
        attention_sum[:own_rows, ends[0] : ends[1]],
        attention_sum[:own_rows, ends[1] : ends[2]],
        attention_sum[:own_rows, ends[2] :],
        attention_sum[own_rows, x_cols : 2 * x_cols],
        feed_sum[:, :hidden_units],
        feed_sum[:, hidden_units : 2 * hidden_units],
        down_out,
        attention_sum[own_rows, :x_cols],
    )


def vspec():
    return pl.BlockSpec(memory_space=pltpu.VMEM)


def kernel_call(body, outs, args, specs=None, scratch=(), megabytes=8, micros=1.0):
    if specs is None:
        specs = [None] * len(args)
    kinds = {
        None: pltpu.VMEM,
        "any": pl.ANY,
        "smem": pltpu.SMEM,
    }
    return pl.pallas_call(
        body,
        out_shape=outs,
        in_specs=[pl.BlockSpec(memory_space=kinds[s]) for s in specs],
        out_specs=[pl.BlockSpec(memory_space=pltpu.VMEM) for _ in outs],
        scratch_shapes=list(scratch),
        compiler_params=pltpu.CompilerParams(vmem_limit_bytes=63 * 2**20),
        cost_estimate=pl.CostEstimate(
            flops=0, bytes_accessed=int(micros * 3.0e6), transcendentals=0
        ),
    )(*args)


def shape(dims, dtype):
    return jax.ShapeDtypeStruct(dims, dtype)


def blocks_of(values, width):
    return [values[:, i : i + width] for i in range(0, values.shape[1], width)]


def turn(values):
    half = values.shape[-1] // 2
    return jnp.concatenate([-values[:, half:], values[:, :half]], 1)


def pad_lanes(values, before, total):
    rows, count = values.shape
    parts = []
    if before:
        parts.append(jnp.zeros((rows, before), values.dtype))
    parts.append(values)
    if total - before - count:
        parts.append(jnp.zeros((rows, total - before - count), values.dtype))
    return jnp.concatenate(parts, 1)


def pack_attention(q_ref, k_ref, v_ref, o_ref, out_ref):
    kv = jnp.concatenate([k_ref[...], v_ref[...]], 0).astype(F32).T.astype(BF16)
    qkv = jnp.concatenate([q_ref[...], kv], 1)
    o = o_ref[...]
    half = o.shape[0] // 2
    out_ref[...] = jnp.concatenate([qkv[:half], o[:half], o[half:], qkv[half:]], 1)


def pack_down(ids, down_ref, _, p0_ref, p1_ref):
    down = down_ref[...]
    units = down.shape[1] // 2
    first = down[:, :units].astype(F32)
    second = down[:, units:].astype(F32)
    even = (ids[0] % 2) == 0
    p0_ref[...] = jnp.where(even, first, second).astype(BF16)
    p1_ref[...] = jnp.where(even, second, first).astype(BF16)


def pack_feed(ids, gate_ref, up_ref, r0_ref, r1_ref, _, out_ref):
    gate_up = jnp.concatenate([gate_ref[...], up_ref[...]], 0).astype(F32).T
    even = (ids[0] % 2) == 0
    r0 = r0_ref[...].astype(F32)
    r1 = r1_ref[...].astype(F32)
    joined = jnp.concatenate([jnp.where(even, r0, r1), jnp.where(even, r1, r0)], 1)
    rows = gate_up.shape[0]
    out_ref[:rows] = gate_up.astype(BF16)
    out_ref[rows:] = joined.astype(BF16)


def join_first(own_ref, got_ref, ag_ref, fg_ref, out_ref):
    half = own_ref.shape[0]
    out_ref[: 2 * half] = jnp.concatenate([own_ref[...], got_ref[...]], 0)
    gains = jnp.concatenate([ag_ref[...], fg_ref[...]], 1)
    row = pad_lanes(gains, 0, out_ref.shape[1])
    out_ref[2 * half :] = jnp.broadcast_to(row, (16, out_ref.shape[1]))


def join_second(a_ref, b_ref, _, out_ref):
    out_ref[...] = jnp.concatenate([a_ref[...], b_ref[...]], 0)


def line_blocks(buffer, f, offset):
    return [
        jnp.concatenate(
            [buffer[2 * (f ^ j) + offset][:, :120], buffer[2 * (f ^ (j + 1)) + offset][:, :120]], 1
        )
        for j in (0, 2)
    ]


def attention_forward(
    ids, x_ref, cos_ref, sin_ref, segc_ref, segr_ref, *rest
):
    first = rest[:8]
    second = rest[8:16]
    (
        x2_ref, h2_ref, att_ref, qr_ref, kr_ref, vr_ref, lse_ref, gains_ref,
        hb, tb, gb,
    ) = rest[16:]
    d = ids[0]
    f = ids[1]
    length = x_ref.shape[0]
    for s in range(8):
        gb[d ^ s] = first[s][240:248, :256].astype(F32)
    gain_one = jnp.concatenate([gb[i][:, :120] for i in range(8)], 1)
    gain_two = jnp.concatenate([gb[i][:, 120:240] for i in range(8)], 1)
    gains_ref[0] = gain_one
    gains_ref[1] = gain_two
    x = x_ref[...].astype(F32)
    scale = lax.rsqrt(jnp.mean(x * x, -1, keepdims=True) + EPS)
    h1 = (x * scale * gain_one[:1]).astype(BF16)
    for i, block in enumerate(blocks_of(h1, 120)):
        hb[i, :, :120] = block
    left = line_blocks(hb, f, 0)
    right = line_blocks(hb, f, 1)
    for s in range(8):
        a = dot(left[0], first[s][:240, 0:256]) + dot(left[1], second[s][:, 0:256])
        b = dot(right[0], first[s][:240, 384:640]) + dot(right[1], second[s][:, 384:640])
        tb[d ^ s, :, :200] = a[:, :200] + b[:, 56:256]
    parts = [tb[i] for i in range(8)]
    q = jnp.concatenate([p[:, :120] for p in parts], 1)
    k = jnp.concatenate([p[:, 120:160] for p in parts], 1)
    v = jnp.concatenate([p[:, 160:200] for p in parts], 1)
    cosines = cos_ref[...]
    sines = sin_ref[...]
    index_q = lax.broadcasted_iota(jnp.int32, (length, length), 0)
    index_k = lax.broadcasted_iota(jnp.int32, (length, length), 1)
    allowed = (segc_ref[...] == segr_ref[...]) & (index_q >= index_k)
    bias = jnp.where(allowed, 0.0, NEGATIVE)
    bias = jnp.concatenate([bias] * GROUP, 0)
    heads = []
    for g in range(KV_HEADS):
        kg = k[:, g * HD : (g + 1) * HD]
        kr = (kg * cosines + turn(kg) * sines).astype(BF16)
        vr = v[:, g * HD : (g + 1) * HD].astype(BF16)
        rows = []
        for h in range(g * GROUP, (g + 1) * GROUP):
            qh = q[:, h * HD : (h + 1) * HD]
            rows.append((qh * cosines + turn(qh) * sines).astype(BF16))
        qr = jnp.concatenate(rows, 0)
        qr_ref[g] = qr
        kr_ref[g] = kr
        vr_ref[g] = vr
        scores = contract_last(qr, kr) * HD ** (-0.5) + bias
        top = jnp.max(scores, -1, keepdims=True)
        exps = jnp.exp(scores - top)
        totals = jnp.sum(exps, -1, keepdims=True)
        lse_ref[g] = top + jnp.log(totals)
        probs = (exps / totals).astype(BF16)
        out = dot(probs, vr).astype(BF16)
        heads += [out[i * length : (i + 1) * length] for i in range(GROUP)]
    attended = jnp.concatenate(heads, 1)
    att_ref[...] = attended
    for i, block in enumerate(blocks_of(attended, 120)):
        hb[i, :, :120] = block
    left = line_blocks(hb, f, 0)
    right = line_blocks(hb, f, 1)
    for s in range(8):
        a = dot(left[0], first[s][:240, 128:384]) + dot(left[1], second[s][:, 128:384])
        b = dot(right[0], first[s][:240, 256:512]) + dot(right[1], second[s][:, 256:512])
        tb[d ^ s, :, :120] = a[:, 72:192] + b[:, 64:184]
    x2 = x + jnp.concatenate([tb[i][:, :120] for i in range(8)], 1)
    x2_ref[...] = x2
    scale_two = lax.rsqrt(jnp.mean(x2 * x2, -1, keepdims=True) + EPS)
    h2_ref[...] = (x2 * scale_two * gain_two[:1]).astype(BF16)


def start_stack(refs, buffer, sems):
    copies = []
    for s, ref in enumerate(refs):
        rows = ref.shape[0]
        copy = pltpu.make_async_copy(ref, buffer.at[pl.ds(s * rows, rows)], sems.at[s])
        copy.start()
        copies.append(copy)
    return copies


def place_feed(feed_ref, gu, dt):
    for j in range(4):
        gu[240 * j : 240 * (j + 1), :] = feed_ref[360 * j : 360 * j + 240, :]
        dt[240 * j : 240 * (j + 1), :] = unfold_down(feed_ref[360 * j + 240 : 360 * (j + 1), :])


def unfold_down(both):
    half = both.shape[1] // 2
    return jnp.concatenate([both[:, :half], both[:, half:]], 0)


def feed_critical(*rest):
    h_refs, c_refs, feed_ref = rest[:8], rest[8:16], rest[16]
    even_ref, odd_ref, delta_ref, mixed_ref, hs, cs, gu, dt, h_sems, c_sems = rest[17:]
    c_copies = start_stack(c_refs, cs, c_sems)
    h_copies = start_stack(h_refs, hs, h_sems)
    place_feed(feed_ref, gu, dt)
    for copy in c_copies + h_copies:
        copy.wait()
    units = dt.shape[1]

    def step(c, carry):
        rows = pl.ds(pl.multiple_of(c * 256, 256), 256)
        both = dot(hs[rows, :], gu[...])
        mixed_grad = dot(cs[rows, :], dt[...])
        gate = both[:, :units]
        up = both[:, units:]
        sig = 1.0 / (1.0 + jnp.exp(-gate))
        silu = gate * sig
        mixed_ref[rows, :] = (silu * up).astype(BF16)
        gate_delta = (mixed_grad * up * sig * (1.0 + gate * (1.0 - sig))).astype(BF16)
        up_delta = (mixed_grad * silu).astype(BF16)
        deltas = jnp.concatenate([gate_delta, up_delta], 1)
        delta_ref[rows, :] = deltas
        back = contract_last(deltas, gu[...])
        even_ref[c] = back[:128]
        odd_ref[pl.ds(pl.multiple_of(c * 128, 128), 128), :] = back[128:].astype(BF16)
        return carry

    lax.fori_loop(0, 4, step, 0)


def pair_sum(even_ref, odd_ref, *rest):
    own_ref, a_ref, b_ref, c_ref = rest[-4:]
    rows = own_ref.shape[0]
    own_ref[...] = even_ref[0] + odd_ref[:rows].astype(F32)
    for i, ref in ((1, a_ref), (2, b_ref), (3, c_ref)):
        ref[...] = (even_ref[i] + odd_ref[rows * i : rows * (i + 1)].astype(F32)).astype(BF16)


def feed_rest(*rest):
    h_refs, c_refs, feed_ref = rest[:8], rest[8:16], rest[16]
    delta_ref, mixed_ref = rest[17:19]
    grad_ref, even_ref, odd_ref, hs, cs, h_sems, c_sems = rest[20:]
    h_copies = start_stack(h_refs, hs, h_sems)
    c_copies = start_stack(c_refs, cs, c_sems)
    for copy in h_copies + c_copies:
        copy.wait()
    for j in range(4):
        part = contract_first(hs[:, 240 * j : 240 * (j + 1)], delta_ref[...])
        grad_ref[360 * j : 360 * j + 240, :] = part.astype(BF16)
        part = contract_first(cs[:, 240 * j : 240 * (j + 1)], mixed_ref[...])
        part = jnp.concatenate([part[:120], part[120:]], 1)
        grad_ref[360 * j + 240 : 360 * (j + 1), :] = part.astype(BF16)
    turned = [unfold_down(feed_ref[360 * j + 240 : 360 * (j + 1), :]) for j in range(4)]
    down = jnp.concatenate(turned, 0)
    for c in range(4):
        part = contract_last(mixed_ref[256 * c : 256 * (c + 1), :], down)
        even_ref[c] = part[:128]
        odd_ref[128 * c : 128 * (c + 1), :] = part[128:].astype(BF16)


def spread_line(buffer, parts, f, offset):
    for j, part in enumerate(parts):
        buffer[2 * (f ^ (2 * j)) + offset, :, :120] = part[:, :120]
        buffer[2 * (f ^ (2 * j + 1)) + offset, :, :120] = part[:, 120:240]


def attention_backward(ids, *rest):
    own_ref, a_ref, b_ref, c_ref, cot_ref, x2_ref, x_ref, gains_ref = rest[:8]
    cos_ref, sin_ref, segc_ref, segr_ref, qr_ref, kr_ref, vr_ref, lse_ref = rest[8:16]
    first, second = rest[16:24], rest[24:32]
    outs = rest[32:40]
    grad_ref, fb, db, eb, gb = rest[40:]
    d = ids[0]
    f = ids[1]
    length = x_ref.shape[0]
    gain_one = gains_ref[0, :1]
    gain_two = gains_ref[1, :1]
    dh2 = (
        own_ref[...] + a_ref[...].astype(F32) + b_ref[...].astype(F32) + c_ref[...].astype(F32)
    )
    x2 = x2_ref[...]
    scale_two = lax.rsqrt(jnp.mean(x2 * x2, -1, keepdims=True) + EPS)
    unit = x2 * scale_two
    feed_gain_grad = jnp.sum(dh2 * unit, 0, keepdims=True)
    scaled = dh2 * gain_two
    dx2 = cot_ref[...].astype(F32) + scale_two * (
        scaled - unit * jnp.mean(scaled * unit, -1, keepdims=True)
    )
    rounded = dx2.astype(BF16)
    for i, block in enumerate(blocks_of(rounded, 120)):
        db[i, :, :120] = block
    left = [jnp.zeros((length, 240), F32)] * 2
    right = [jnp.zeros((length, 240), F32)] * 2
    for s in range(8):
        mine = db[d ^ s][:, :120]
        for_left = pad_lanes(mine, 72, 256)
        for_right = pad_lanes(mine, 64, 256)
        left[0] = left[0] + contract_last(for_left, first[s][:240, 128:384])
        left[1] = left[1] + contract_last(for_left, second[s][:, 128:384])
        right[0] = right[0] + contract_last(for_right, first[s][:240, 256:512])
        right[1] = right[1] + contract_last(for_right, second[s][:, 256:512])
    spread_line(fb, left, f, 0)
    spread_line(fb, right, f, 1)
    grad = jnp.concatenate([fb[i][:, :120] for i in range(8)], 1).astype(BF16)
    cosines = cos_ref[...]
    sines = sin_ref[...]
    index_q = lax.broadcasted_iota(jnp.int32, (length, length), 0)
    index_k = lax.broadcasted_iota(jnp.int32, (length, length), 1)
    allowed = (segc_ref[...] == segr_ref[...]) & (index_q >= index_k)
    bias = jnp.where(allowed, 0.0, NEGATIVE)
    bias = jnp.concatenate([bias] * GROUP, 0)
    dq, dk, dv = [], [], []
    for g in range(KV_HEADS):
        qr = qr_ref[g]
        kr = kr_ref[g]
        vr = vr_ref[g]
        grads = jnp.concatenate(
            [grad[:, h * HD : (h + 1) * HD] for h in range(g * GROUP, (g + 1) * GROUP)], 0
        )
        probs = jnp.exp(contract_last(qr, kr) * HD ** (-0.5) + bias - lse_ref[g])
        dv.append(contract_first(probs.astype(BF16), grads).astype(BF16))
        dprob = contract_last(grads, vr)
        inner = jnp.sum(probs * dprob, -1, keepdims=True)
        ds = (probs * (dprob - inner) * HD ** (-0.5)).astype(BF16)
        dqg = dot(ds, kr)
        dkg = contract_first(ds, qr)
        dk.append((dkg * cosines - turn(dkg * sines)).astype(BF16))
        for i in range(GROUP):
            part = dqg[i * length : (i + 1) * length]
            dq.append((part * cosines - turn(part * sines)).astype(BF16))
    dq = blocks_of(jnp.concatenate(dq, 1), 120)
    dk = blocks_of(jnp.concatenate(dk, 1), 40)
    dv = blocks_of(jnp.concatenate(dv, 1), 40)
    for i in range(8):
        eb[i, :, :200] = jnp.concatenate([dq[i], dk[i], dv[i]], 1)
    left = [jnp.zeros((length, 240), F32)] * 2
    right = [jnp.zeros((length, 240), F32)] * 2
    for s in range(8):
        mine = eb[d ^ s][:, :200]
        for_left = pad_lanes(mine, 0, 256)
        for_right = pad_lanes(mine, 56, 256)
        left[0] = left[0] + contract_last(for_left, first[s][:240, 0:256])
        left[1] = left[1] + contract_last(for_left, second[s][:, 0:256])
        right[0] = right[0] + contract_last(for_right, first[s][:240, 384:640])
        right[1] = right[1] + contract_last(for_right, second[s][:, 384:640])
    spread_line(fb, left, f, 0)
    spread_line(fb, right, f, 1)
    dh1 = jnp.concatenate([fb[i][:, :120] for i in range(8)], 1)
    x = x_ref[...].astype(F32)
    scale_one = lax.rsqrt(jnp.mean(x * x, -1, keepdims=True) + EPS)
    unit = x * scale_one
    attention_gain_grad = jnp.sum(dh1 * unit, 0, keepdims=True)
    scaled = dh1 * gain_one
    input_grad = dx2 + scale_one * (
        scaled - unit * jnp.mean(scaled * unit, -1, keepdims=True)
    )
    grad_ref[...] = input_grad.T
    for i in range(8):
        row = jnp.concatenate(
            [feed_gain_grad[:, 120 * i : 120 * (i + 1)], attention_gain_grad[:, 120 * i : 120 * (i + 1)]], 1
        )
        gb[i] = jnp.broadcast_to(pad_lanes(row, 0, 640), (16, 640))
    half = length // 2
    for s in range(8):
        delta = eb[d ^ s][:, :200]
        mine = db[d ^ s][:, :120]
        outs[s][:half] = jnp.concatenate(
            [delta[:half], mine[:half], mine[half:], delta[half:]], 1
        )
        outs[s][half:] = gb[d ^ s].astype(BF16)


def attention_weights(ids, *rest):
    x_refs, att_refs, got, gains_ref = rest[:8], rest[8:16], rest[16:24], rest[24]
    own_ref, g1_ref, g2_ref, g3_ref, hs, at, dl, acc, x_sems, a_sems = rest[25:]
    f = ids[1]
    length = 128
    half = 64
    x_copies = start_stack(x_refs, hs, x_sems)
    a_copies = start_stack(att_refs, at, a_sems)
    gain_sum = jnp.zeros((8, 640), F32)
    for s in range(8):
        block = got[s][:half]
        dl[s * length : s * length + half, 0:320] = block[:, :320]
        dl[s * length + half : (s + 1) * length, 0:320] = jnp.concatenate(
            [block[:, 440:], block[:, 320:440]], 1
        )
        gain_sum = gain_sum + got[s][half : half + 8].astype(F32)
    gain_one = gains_ref[0, :1]
    for copy in x_copies + a_copies:
        copy.wait()
    for s in range(8):
        x = hs[length * s : length * (s + 1)].astype(F32)
        scale = lax.rsqrt(jnp.mean(x * x, -1, keepdims=True) + EPS)
        hs[s * length : (s + 1) * length] = (x * scale * gain_one).astype(BF16)
    qkv = contract_first(dl[:, :200], hs[...])
    out = contract_first(dl[:, 200:320], at[...])
    both = jnp.concatenate([qkv, out], 0)
    for i in range(4):
        acc[i, :320, :240] = both[:, 240 * i : 240 * (i + 1)]
        acc[i, 320:, :240] = jnp.concatenate([gain_sum[:, :240]] * 2, 0)
    own_ref[...] = acc[f][:, :240]
    for j, ref in ((1, g1_ref), (2, g2_ref), (3, g3_ref)):
        ref[...] = acc[f ^ j][:, :240].astype(BF16)


def finish_feed(ids, sum_ref, gate_ref, up_ref, a_ref, b_ref):
    total = sum_ref[:240].astype(F32).T
    gate_ref[...] = total[:320]
    up_ref[...] = total[320:]
    even = (ids[0] % 2) == 0
    down = sum_ref[240:].astype(F32)
    left = down[:, :320]
    right = down[:, 320:]
    a_ref[...] = jnp.where(even, left, right).astype(BF16)
    b_ref[...] = jnp.where(even, right, left).astype(BF16)


def finish_down(ids, a_ref, b_ref, out_ref):
    even = (ids[0] % 2) == 0
    a = a_ref[...].astype(F32)
    b = b_ref[...].astype(F32)
    out_ref[...] = jnp.concatenate([jnp.where(even, a, b), jnp.where(even, b, a)], 1)


def finish_output(x2_ref, own_ref, a_ref, b_ref, c_ref, out_ref):
    total = (
        x2_ref[...]
        + own_ref[...]
        + a_ref[...].astype(F32)
        + b_ref[...].astype(F32)
        + c_ref[...].astype(F32)
    )
    out_ref[...] = total.T.astype(BF16)


def finish_attention(own_ref, a_ref, b_ref, c_ref, q_ref, k_ref, v_ref, o_ref, ag_ref, fg_ref):
    total = (
        own_ref[...] + a_ref[...].astype(F32) + b_ref[...].astype(F32) + c_ref[...].astype(F32)
    )
    q_ref[...] = total[:120].T
    k_ref[...] = total[120:160]
    v_ref[...] = total[160:200]
    o_ref[...] = total[200:320].T
    fg_ref[...] = total[320:328, :120]
    ag_ref[...] = total[320:328, 120:240]


def fast(
    hidden_in,
    segment_ids,
    positions,
    query_weight,
    key_weight,
    value_weight,
    output_weight,
    attention_gain,
    gate_weight,
    up_weight,
    down_weight,
    feedforward_gain,
    output_cotangent,
):
    hidden = hidden_in[0]
    cotangent = output_cotangent[0]
    length, features = hidden.shape
    d = lax.axis_index("dp")
    f = lax.axis_index("fsdp")
    ids = jnp.stack([d, f]).astype(jnp.int32)
    tokens = 8 * length

    (block,) = kernel_call(
        pack_attention,
        [shape((120, 640), BF16)],
        [query_weight, key_weight.T, value_weight.T, output_weight],
    )
    line = [block] + [send(block, "fsdp", j) for j in (1, 2, 3)]
    (chunk_a,) = kernel_call(
        join_first,
        [shape((256, 640), BF16)],
        [line[0], line[1], attention_gain[None], feedforward_gain[None]],
    )
    (chunk_b,) = kernel_call(join_second, [shape((240, 640), BF16)], [line[2], line[3], chunk_a], [None, None, "any"])

    def spread(chunk, near, far):
        slots = [chunk, send(chunk, "dp", 1)] + [None] * 6
        slots[near] = send(chunk, "dp", near)
        slots[far] = send(chunk, "dp", far)
        slots[6] = send(slots[near], "dp", far)
        for s in (near, far, 6):
            slots[s + 1] = send(slots[s], "dp", 1)
        return slots

    first = spread(chunk_a, 2, 4)
    second = spread(chunk_b, 4, 2)

    piece_a, piece_b = kernel_call(
        pack_down,
        [shape((120, 320), BF16), shape((120, 320), BF16)],
        [ids, down_weight.T, block],
        ["smem", None, "any"],
    )
    routes = down_routes(8, 4)
    piece_a = lax.ppermute(piece_a, ("dp", "fsdp"), routes[0])
    piece_b = lax.ppermute(piece_b, ("dp", "fsdp"), routes[1])
    (feed_block,) = kernel_call(
        pack_feed,
        [shape((360, 640), BF16)],
        [ids, gate_weight.T, up_weight.T, piece_a, piece_b, chunk_b],
        ["smem"] + [None] * 4 + ["any"],
    )
    feed = lax.all_gather(feed_block, "fsdp", axis=0, tiled=True)

    def gather(values):
        slots = [values, send(values, "dp", 1)] + [None] * 6
        for s in (2, 4, 6):
            slots[s] = send(values, "dp", s)
            slots[s + 1] = send(slots[s], "dp", 1)
        return slots

    cotangent_slots = gather(cotangent)

    cosines, sines = rotary_tables(positions[0], HD)
    seg_column = segment_ids[0][:, None]
    seg_row = segment_ids
    x2, h2, attended, qr, kr, vr, lse, gains = kernel_call(
        attention_forward,
        [
            shape((length, features), F32),
            shape((length, features), BF16),
            shape((length, features), BF16),
            shape((KV_HEADS, GROUP * length, HD), BF16),
            shape((KV_HEADS, length, HD), BF16),
            shape((KV_HEADS, length, HD), BF16),
            shape((KV_HEADS, GROUP * length, 1), F32),
            shape((2, 8, features), F32),
        ],
        [ids, hidden, cosines, sines, seg_column, seg_row, *first, *second],
        ["smem"] + [None] * 21,
        [
            pltpu.VMEM((8, length, 128), BF16),
            pltpu.VMEM((8, length, 256), F32),
            pltpu.VMEM((8, 8, 256), F32),
        ],
        16,
        8.5,
    )
    h2_slots = gather(h2)
    even, odd, deltas, mixed = kernel_call(
        feed_critical,
        [
            shape((4, length, features), F32),
            shape((4 * length, features), BF16),
            shape((tokens, 640), BF16),
            shape((tokens, 320), BF16),
        ],
        [*h2_slots, *cotangent_slots, feed],
        ["any"] * 16 + [None],
        [
            pltpu.VMEM((tokens, features), BF16),
            pltpu.VMEM((tokens, features), BF16),
            pltpu.VMEM((features, 640), BF16),
            pltpu.VMEM((features, 320), BF16),
            pltpu.SemaphoreType.DMA((8,)),
            pltpu.SemaphoreType.DMA((8,)),
        ],
        24,
        9.0,
    )

    def scatter_sum(even, odd, *after):
        odd = send(odd, "dp", 1)
        own, a, b, c = kernel_call(
            pair_sum,
            [shape((length, features), F32)] + [shape((length, features), BF16)] * 3,
            [even, odd, *after],
            [None, None] + ["any"] * len(after),
            (),
            12,
        )
        return own, send(a, "dp", 2), send(b, "dp", 4), send(c, "dp", 6)

    back_own, back_a, back_b, back_c = scatter_sum(even, odd)
    feed_grad, f_even, f_odd = kernel_call(
        feed_rest,
        [
            shape((4 * 360, 640), BF16),
            shape((4, length, features), F32),
            shape((4 * length, features), BF16),
        ],
        [*h2_slots, *cotangent_slots, feed, deltas, mixed, back_own],
        ["any"] * 16 + [None] * 3 + ["any"],
        [
            pltpu.VMEM((tokens, features), BF16),
            pltpu.VMEM((tokens, features), BF16),
            pltpu.SemaphoreType.DMA((8,)),
            pltpu.SemaphoreType.DMA((8,)),
        ],
        24,
        9.0,
    )
    feed_sum = lax.psum_scatter(feed_grad, "fsdp", scatter_dimension=0, tiled=True)
    attended_slots = gather(attended)
    hidden_slots = gather(hidden)
    *outgoing, input_grad = kernel_call(
        attention_backward,
        [shape((80, 640), BF16)] * 8 + [shape((features, length), F32)],
        [
            ids, back_own, back_a, back_b, back_c, cotangent, x2, hidden, gains,
            cosines, sines, seg_column, seg_row, qr, kr, vr, lse, *first, *second,
        ],
        ["smem"] + [None] * 32,
        [
            pltpu.VMEM((8, length, 128), F32),
            pltpu.VMEM((8, length, 128), BF16),
            pltpu.VMEM((8, length, 256), BF16),
            pltpu.VMEM((8, 16, 640), F32),
        ],
        18,
        10.5,
    )
    arrived = [outgoing[0]] + [send(outgoing[s], "dp", s) for s in range(1, 8)]
    w0, w1, w2, w3 = kernel_call(
        attention_weights,
        [shape((336, 240), F32)] + [shape((336, 240), BF16)] * 3,
        [ids, *hidden_slots, *attended_slots, *arrived, gains],
        ["smem"] + ["any"] * 16 + [None] * 9,
        [
            pltpu.VMEM((tokens, features), BF16),
            pltpu.VMEM((tokens, features), BF16),
            pltpu.VMEM((tokens, 320), BF16),
            pltpu.VMEM((4, 336, 256), F32),
            pltpu.SemaphoreType.DMA((8,)),
            pltpu.SemaphoreType.DMA((8,)),
        ],
        20,
        4.5,
    )

    gate_out, up_out, piece_a, piece_b = kernel_call(
        finish_feed,
        [shape((320, 240), F32)] * 2 + [shape((120, 320), BF16)] * 2,
        [ids, feed_sum],
        ["smem", None],
    )
    back = [[(t, s) for s, t in pairs] for pairs in routes]
    piece_a = lax.ppermute(piece_a, ("dp", "fsdp"), back[0])
    piece_b = lax.ppermute(piece_b, ("dp", "fsdp"), back[1])
    (down_out,) = kernel_call(
        finish_down, [shape((120, 640), F32)], [ids, piece_a, piece_b], ["smem", None, None]
    )
    sums = scatter_sum(f_even, f_odd, w0)
    (block_output,) = kernel_call(
        finish_output, [shape((features, length), BF16)], [x2, *sums]
    )
    parts = [send(w, "fsdp", j) for j, w in ((1, w1), (2, w2), (3, w3))]
    q_out, k_out, v_out, o_out, ag_out, fg_out = kernel_call(
        finish_attention,
        [
            shape((240, 120), F32),
            shape((40, 240), F32),
            shape((40, 240), F32),
            shape((240, 120), F32),
            shape((8, 120), F32),
            shape((8, 120), F32),
        ],
        [w0, *parts],
    )
    return (
        block_output.T[None],
        input_grad.T[None],
        q_out,
        k_out.T,
        v_out.T,
        o_out,
        ag_out[0],
        gate_out.T,
        up_out.T,
        down_out.T,
        fg_out[0],
    )


def fits(mesh_shape):
    return mesh_shape["dp"] == 8 and mesh_shape["fsdp"] == 4


def solution(mesh):
    in_specs = (
        P(("dp", "fsdp"), None, None),
        P(("dp", "fsdp"), None),
        P(("dp", "fsdp"), None),
        P("fsdp", "dp"),
        P("fsdp", "dp"),
        P("fsdp", "dp"),
        P("fsdp", "dp"),
        P("dp"),
        P("fsdp", "dp"),
        P("fsdp", "dp"),
        P("fsdp", "dp"),
        P("dp"),
        P(("dp", "fsdp"), None, None),
    )
    out_specs = (
        P(("dp", "fsdp"), None, None),
        P(("dp", "fsdp"), None, None),
        P("fsdp", "dp"),
        P("fsdp", "dp"),
        P("fsdp", "dp"),
        P("fsdp", "dp"),
        P("dp"),
        P("fsdp", "dp"),
        P("fsdp", "dp"),
        P("fsdp", "dp"),
        P("dp"),
    )
    body = fast if fits(mesh.shape) else local
    return jax.shard_map(body, mesh=mesh, in_specs=in_specs, out_specs=out_specs, check_vma=False)
```

```python
import jax
import jax.numpy as jnp
from jax import lax
from jax.experimental import pallas as pl
from jax.experimental.pallas import tpu as pltpu
from jax.sharding import PartitionSpec as P

HEADS = 15
KV_HEADS = 5
HD = 64
GROUP = HEADS // KV_HEADS


EPS = 1e-05
THETA = 100000.0
NEGATIVE = -1e30
F32 = jnp.float32
BF16 = jnp.bfloat16


def rotary_tables(position, head_dim):
    inverse = THETA ** (-jnp.arange(0, head_dim, 2).astype(F32) / head_dim)
    angles = position.astype(F32)[:, None] * inverse[None, :]
    cosines = jnp.cos(angles)
    sine_values = jnp.sin(angles)
    return (
        jnp.concatenate([cosines, cosines], -1),
        jnp.concatenate([sine_values, sine_values], -1),
    )


def rotate(values, cosines, sine_values):
    half_dim = values.shape[-1] // 2
    turned = jnp.concatenate([-values[..., half_dim:], values[..., :half_dim]], -1)
    return values * cosines[:, None, :] + turned * sine_values[:, None, :]


def rotate_back(gradient, cosines, sine_values):
    half_dim = gradient.shape[-1] // 2
    sine_scaled = gradient * sine_values[:, None, :]
    turned = jnp.concatenate([-sine_scaled[..., half_dim:], sine_scaled[..., :half_dim]], -1)
    return gradient * cosines[:, None, :] - turned


def row_scale_of(values):
    return lax.rsqrt(jnp.mean(values * values, -1, keepdims=True) + EPS)


def norm_backward(values, row_scale, gain, upstream):
    unit_rows = values * row_scale
    scaled = upstream * gain
    gain_grad = jnp.sum(upstream * unit_rows, 0)
    result = row_scale * (scaled - unit_rows * jnp.mean(scaled * unit_rows, -1, keepdims=True))
    return (result, gain_grad)


def dot(left, right):
    return jnp.dot(left, right, preferred_element_type=F32)


def contract_first(left, right):
    return lax.dot_general(left, right, (((0,), (0,)), ((), ())), preferred_element_type=F32)


def contract_last(left, right):
    return lax.dot_general(left, right, (((1,), (1,)), ((), ())), preferred_element_type=F32)


def send(values, axis, distance):
    count = lax.axis_size(axis)
    return lax.ppermute(values, axis, [(i, i ^ distance) for i in range(count)])


def pick(blocks, index):
    return lax.dynamic_index_in_dim(blocks, index, 0, keepdims=False)


def reorder(blocks, me):
    return jnp.stack([pick(blocks, me ^ s) for s in range(blocks.shape[0])])


def plane_gather(values):
    count = lax.axis_size("dp")
    if count != 8:
        return reorder(lax.all_gather(values, "dp"), lax.axis_index("dp"))
    slots = [values, send(values, "dp", 1)] + [None] * 6
    for s in (2, 4, 6):
        slots[s] = send(values, "dp", s)
        slots[s + 1] = send(slots[s], "dp", 1)
    return jnp.stack(slots)


def plane_exchange(blocks):
    count = lax.axis_size("dp")
    if count != 8:
        me = lax.axis_index("dp")
        return reorder(lax.all_to_all(reorder(blocks, me), "dp", 0, 0), me)
    return jnp.stack([blocks[0]] + [send(blocks[s], "dp", s) for s in range(1, 8)])


def plane_sum(blocks):
    count = lax.axis_size("dp")
    if count != 8:
        return jnp.sum(plane_exchange(blocks.astype(BF16)).astype(F32), 0)
    odd = send(jnp.stack([blocks[s] for s in (1, 3, 5, 7)]).astype(BF16), "dp", 1)
    pair = [blocks[2 * i] + odd[i].astype(F32) for i in range(4)]
    total = pair[0]
    for i in range(1, 4):
        total = total + send(pair[i].astype(BF16), "dp", 2 * i).astype(F32)
    return total


def line_gather(values):
    me = lax.axis_index("fsdp")
    count = lax.axis_size("fsdp")
    out = jnp.zeros((count,) + values.shape, values.dtype)
    out = lax.dynamic_update_index_in_dim(out, values, me, 0)
    for s in range(1, count):
        out = lax.dynamic_update_index_in_dim(out, send(values, "fsdp", s), me ^ s, 0)
    return out


def line_sum(blocks):
    me = lax.axis_index("fsdp")
    total = pick(blocks, me)
    for s in range(1, lax.axis_size("fsdp")):
        total = total + send(pick(blocks, me ^ s).astype(BF16), "fsdp", s).astype(F32)
    return total


def down_routes(dp_count, fsdp_count):
    ratio = dp_count // fsdp_count
    routes = []
    for m in range(ratio):
        pairs = []
        for d in range(dp_count):
            for f in range(fsdp_count):
                target = (ratio * f + (m + d) % ratio) * fsdp_count + d // ratio
                pairs.append((d * fsdp_count + f, target))
        routes.append(pairs)
    return routes


def down_pieces(down_turned, dp_count, fsdp_count):
    ratio = dp_count // fsdp_count
    d = lax.axis_index("dp")
    width = down_turned.shape[1] // ratio
    halves = jnp.stack([down_turned[:, h * width : (h + 1) * width] for h in range(ratio)])
    got = [
        lax.ppermute(pick(halves, (m + d) % ratio), ("dp", "fsdp"), pairs)
        for m, pairs in enumerate(down_routes(dp_count, fsdp_count))
    ]
    stacked = jnp.stack(got)
    ordered = [pick(stacked, (d - j) % ratio) for j in range(ratio)]
    return jnp.concatenate(ordered, 0)


def down_return(grad_turned, dp_count, fsdp_count):
    ratio = dp_count // fsdp_count
    d = lax.axis_index("dp")
    height = grad_turned.shape[0] // ratio
    pieces = grad_turned.reshape(ratio, height, grad_turned.shape[1])
    got = []
    for m, pairs in enumerate(down_routes(dp_count, fsdp_count)):
        back = [(target, source) for source, target in pairs]
        got.append(lax.ppermute(pick(pieces, (d - m) % ratio), ("dp", "fsdp"), back))
    stacked = jnp.stack(got)
    return jnp.concatenate([pick(stacked, (h - d) % ratio) for h in range(ratio)], 1)


def masked_scores(query_turned, key_turned, segment):
    length = query_turned.shape[0]
    grouped = query_turned.reshape(length, KV_HEADS, GROUP, HD)
    scores = jnp.einsum("qkgd,tkd->kgqt", grouped, key_turned, preferred_element_type=F32)
    index = jnp.arange(length)
    allowed = (segment[:, None] == segment[None, :]) & (index[:, None] >= index[None, :])
    return jnp.where(allowed, scores * HD ** (-0.5), NEGATIVE)


def attend_forward(query_turned, key_turned, value_rounded, segment):
    length = query_turned.shape[0]
    scores = masked_scores(query_turned, key_turned, segment)
    row_max = jnp.max(scores, -1, keepdims=True)
    exponentials = jnp.exp(scores - row_max)
    totals = jnp.sum(exponentials, -1, keepdims=True)
    probs_rounded = (exponentials / totals).astype(BF16)
    attended = jnp.einsum("kgqt,tkd->qkgd", probs_rounded, value_rounded, preferred_element_type=F32)
    return (attended.reshape(length, HEADS * HD).astype(BF16), row_max + jnp.log(totals))


def attend_backward(query_turned, key_turned, value_rounded, segment, log_totals, attended_grad):
    length = query_turned.shape[0]
    grouped = query_turned.reshape(length, KV_HEADS, GROUP, HD)
    grad_grouped = attended_grad.reshape(length, KV_HEADS, GROUP, HD)
    scores = masked_scores(query_turned, key_turned, segment)
    probs_again = jnp.exp(scores - log_totals)
    value_sum = jnp.einsum(
        "kgqt,qkgd->tkd", probs_again.astype(BF16), grad_grouped, preferred_element_type=F32
    )
    prob_grad = jnp.einsum(
        "qkgd,tkd->kgqt", grad_grouped, value_rounded, preferred_element_type=F32
    )
    inner_rows = jnp.sum(probs_again * prob_grad, -1, keepdims=True)
    score_grad = (probs_again * (prob_grad - inner_rows) * HD ** (-0.5)).astype(BF16)
    query_part = jnp.einsum("kgqt,tkd->qkgd", score_grad, key_turned, preferred_element_type=F32)
    key_sum = jnp.einsum("kgqt,qkgd->tkd", score_grad, grouped, preferred_element_type=F32)
    return (query_part.reshape(length, HEADS, HD), key_sum, value_sum)


def local(
    hidden_in,
    segment_ids,
    positions,
    query_weight,
    key_weight,
    value_weight,
    output_weight,
    attention_gain,
    gate_weight,
    up_weight,
    down_weight,
    feedforward_gain,
    output_cotangent,
):
    hidden = hidden_in[0]
    hidden_rows = hidden.astype(F32)
    segment = segment_ids[0]
    cotangent = output_cotangent[0]
    length, features = hidden.shape
    width = HEADS * HD
    kv_width = KV_HEADS * HD
    dp_count = lax.axis_size("dp")
    fsdp_count = lax.axis_size("fsdp")
    d = lax.axis_index("dp")
    f = lax.axis_index("fsdp")
    q_cols = width // dp_count
    kv_cols = kv_width // dp_count
    x_cols = features // dp_count
    own_rows = features // fsdp_count
    qkv_cols = q_cols + 2 * kv_cols
    all_cols = qkv_cols + x_cols
    hidden_units = gate_weight.shape[1]

    attention_block = jnp.concatenate(
        [query_weight, key_weight, value_weight, output_weight], 1
    )
    attention_rows = line_gather(attention_block).reshape(features, all_cols)
    gains = jnp.concatenate(
        [attention_gain, feedforward_gain, jnp.zeros((all_cols - 2 * x_cols,), BF16)]
    )
    gains = jnp.concatenate([gains[None], jnp.zeros((15, all_cols), BF16)])
    slots = plane_gather(jnp.concatenate([attention_rows, gains], 0))
    gains_ordered = reorder(slots[:, features, :], d)
    attention_gain_full = gains_ordered[:, :x_cols].reshape(features).astype(F32)
    feed_gain_full = gains_ordered[:, x_cols : 2 * x_cols].reshape(features).astype(F32)
    qkv_slots = slots[:, :features, :qkv_cols]
    output_slots = slots[:, :features, qkv_cols:]

    down_block = down_pieces(down_weight.T, dp_count, fsdp_count)
    feed_block = jnp.concatenate([gate_weight, up_weight, down_block], 1)
    feed = line_gather(feed_block).reshape(features, 3 * hidden_units)

    tokens = plane_gather(jnp.stack([hidden, cotangent]))
    hidden_all = tokens[:, 0].reshape(dp_count * length, features)
    cotangent_all = tokens[:, 1].reshape(dp_count * length, features)

    scale_one = row_scale_of(hidden_rows)
    normed_one = (hidden_rows * scale_one * attention_gain_full).astype(BF16)
    cosines, sine_values = rotary_tables(positions[0], HD)
    qkv = reorder(jnp.einsum("td,sdc->stc", normed_one, qkv_slots, preferred_element_type=F32), d)

    def columns(start, count):
        part = qkv[:, :, start : start + count]
        return part.transpose(1, 0, 2).reshape(length, dp_count * count)

    query_proj = columns(0, q_cols).reshape(length, HEADS, HD)
    key_proj = columns(q_cols, kv_cols).reshape(length, KV_HEADS, HD)
    value_proj = columns(q_cols + kv_cols, kv_cols).reshape(length, KV_HEADS, HD)
    query_turned = rotate(query_proj, cosines, sine_values).astype(BF16)
    key_turned = rotate(key_proj, cosines, sine_values).astype(BF16)
    value_rounded = value_proj.astype(BF16)
    attended, log_totals = attend_forward(query_turned, key_turned, value_rounded, segment)
    added = reorder(jnp.einsum("td,sdc->stc", attended, output_slots, preferred_element_type=F32), d)
    residual = hidden_rows + added.transpose(1, 0, 2).reshape(length, features)

    scale_two = row_scale_of(residual)
    normed_two = (residual * scale_two * feed_gain_full).astype(BF16)
    normed_two_all = plane_gather(normed_two).reshape(dp_count * length, features)
    gate_up = feed[:, : 2 * hidden_units]
    down_turned = feed[:, 2 * hidden_units :]
    both = dot(normed_two_all, gate_up)
    gate_proj = both[:, :hidden_units]
    up_proj = both[:, hidden_units:]
    mixed_grad = dot(cotangent_all, down_turned)
    sigmoid_gate = jax.nn.sigmoid(gate_proj)
    silu_gate = gate_proj * sigmoid_gate
    mixed = (silu_gate * up_proj).astype(BF16)
    gate_delta = (
        mixed_grad * up_proj * sigmoid_gate * (1.0 + gate_proj * (1.0 - sigmoid_gate))
    ).astype(BF16)
    up_delta = (mixed_grad * silu_gate).astype(BF16)
    deltas = jnp.concatenate([gate_delta, up_delta], 1)
    normed_two_grad = plane_sum(
        contract_last(deltas, gate_up).reshape(dp_count, length, features)
    )
    gate_up_grad = contract_first(normed_two_all, deltas)
    down_grad = contract_first(cotangent_all, mixed)
    feed_grad = jnp.concatenate([gate_up_grad, down_grad], 1).reshape(
        fsdp_count, own_rows, 3 * hidden_units
    )
    fed = plane_sum(contract_last(mixed, down_turned).reshape(dp_count, length, features))
    block_output = (residual + fed).astype(BF16)
    attended_all = plane_gather(attended).reshape(dp_count * length, width)

    residual_part, feed_gain_grad = norm_backward(
        residual, scale_two, feed_gain_full, normed_two_grad
    )
    residual_grad = cotangent.astype(F32) + residual_part
    feed_sum = line_sum(feed_grad)

    residual_rounded = residual_grad.astype(BF16)
    residual_blocks = residual_rounded.reshape(length, dp_count, x_cols).transpose(1, 0, 2)
    residual_slots = reorder(residual_blocks, d)
    attended_grad = jnp.einsum(
        "stc,sdc->td", residual_slots, output_slots, preferred_element_type=F32
    ).astype(BF16)
    query_raw, key_raw, value_raw = attend_backward(
        query_turned, key_turned, value_rounded, segment, log_totals, attended_grad
    )
    query_delta = rotate_back(query_raw, cosines, sine_values).astype(BF16)
    key_delta = rotate_back(key_raw, cosines, sine_values).astype(BF16)
    value_delta = value_raw.astype(BF16)
    qkv_delta = jnp.concatenate(
        [
            part.reshape(length, dp_count, -1).transpose(1, 0, 2)
            for part in (query_delta, key_delta, value_delta)
        ],
        2,
    )
    delta_slots = reorder(qkv_delta, d)
    normed_one_grad = jnp.einsum(
        "stc,sdc->td", delta_slots, qkv_slots, preferred_element_type=F32
    )
    input_part, attention_gain_grad = norm_backward(
        hidden_rows, scale_one, attention_gain_full, normed_one_grad
    )
    input_grad = residual_grad + input_part

    gain_rows = jnp.concatenate(
        [
            feed_gain_grad.reshape(dp_count, 1, x_cols),
            attention_gain_grad.reshape(dp_count, 1, x_cols),
            jnp.zeros((dp_count, 1, all_cols - 2 * x_cols), F32),
        ],
        2,
    ).astype(BF16)
    gain_rows = jnp.pad(reorder(gain_rows, d), ((0, 0), (0, 15), (0, 0)))
    outgoing = jnp.concatenate(
        [jnp.concatenate([delta_slots, residual_slots], 2), gain_rows], 1
    )
    arrived = plane_exchange(outgoing)
    deltas_all = arrived[:, :length].reshape(dp_count * length, all_cols)
    gain_sums = jnp.sum(arrived[:, length].astype(F32), 0)
    hidden_all_rows = hidden_all.astype(F32)
    normed_one_all = (
        hidden_all_rows * row_scale_of(hidden_all_rows) * attention_gain_full
    ).astype(BF16)
    qkv_grad = contract_first(normed_one_all, deltas_all[:, :qkv_cols])
    output_grad = contract_first(attended_all, deltas_all[:, qkv_cols:])
    attention_grad = jnp.concatenate([qkv_grad, output_grad], 1).reshape(
        fsdp_count, own_rows, all_cols
    )
    gain_block = jnp.broadcast_to(
        jnp.pad(gain_sums[None], ((0, 15), (0, 0)))[None], (fsdp_count, 16, all_cols)
    )
    attention_sum = line_sum(jnp.concatenate([attention_grad, gain_block], 1))
    down_out = down_return(feed_sum[:, 2 * hidden_units :], dp_count, fsdp_count).T

    ends = (q_cols, q_cols + kv_cols, qkv_cols)
    return (
        block_output[None],
        input_grad[None],
        attention_sum[:own_rows, : ends[0]],
        attention_sum[:own_rows, ends[0] : ends[1]],
        attention_sum[:own_rows, ends[1] : ends[2]],
        attention_sum[:own_rows, ends[2] :],
        attention_sum[own_rows, x_cols : 2 * x_cols],
        feed_sum[:, :hidden_units],
        feed_sum[:, hidden_units : 2 * hidden_units],
        down_out,
        attention_sum[own_rows, :x_cols],
    )


def vspec():
    return pl.BlockSpec(memory_space=pltpu.VMEM)


def kernel_call(body, outs, args, specs=None, scratch=(), megabytes=8, micros=1.0):
    if specs is None:
        specs = [None] * len(args)
    kinds = {
        None: pltpu.VMEM,
        "any": pl.ANY,
        "smem": pltpu.SMEM,
    }
    return pl.pallas_call(
        body,
        out_shape=outs,
        in_specs=[pl.BlockSpec(memory_space=kinds[s]) for s in specs],
        out_specs=[pl.BlockSpec(memory_space=pltpu.VMEM) for _ in outs],
        scratch_shapes=list(scratch),
        compiler_params=pltpu.CompilerParams(vmem_limit_bytes=63 * 2**20),
        cost_estimate=pl.CostEstimate(
            flops=int(micros * 1.1e9), bytes_accessed=int(micros * 3.0e6), transcendentals=0
        ),
    )(*args)


def after_all(values, *others):
    count = len(values)
    return pl.pallas_call(
        lambda *refs: None,
        out_shape=[shape(value.shape, value.dtype) for value in values],
        in_specs=[pl.BlockSpec(memory_space=pl.ANY)] * (count + len(others)),
        out_specs=[pl.BlockSpec(memory_space=pl.ANY)] * count,
        input_output_aliases={i: i for i in range(count)},
    )(*values, *others)


def after(value, *others):
    return after_all([value], *others)[0]


def shape(dims, dtype):
    return jax.ShapeDtypeStruct(dims, dtype)


def blocks_of(values, width):
    return [values[:, i : i + width] for i in range(0, values.shape[1], width)]


def turn(values):
    half = values.shape[-1] // 2
    return jnp.concatenate([-values[:, half:], values[:, :half]], 1)


def pad_lanes(values, before, total):
    rows, count = values.shape
    parts = []
    if before:
        parts.append(jnp.zeros((rows, before), values.dtype))
    parts.append(values)
    if total - before - count:
        parts.append(jnp.zeros((rows, total - before - count), values.dtype))
    return jnp.concatenate(parts, 1)


def pack_attention(q_ref, k_ref, v_ref, o_ref, out_ref):
    kv = jnp.concatenate([k_ref[...], v_ref[...]], 0).astype(F32).T.astype(BF16)
    qkv = jnp.concatenate([q_ref[...], kv], 1)
    o = o_ref[...]
    half = o.shape[0] // 2
    out_ref[...] = jnp.concatenate([qkv[:half], o[:half], o[half:], qkv[half:]], 1)


def pack_feed(gate_ref, up_ref, down_ref, _, out_ref):
    gate_up = jnp.concatenate([gate_ref[...], up_ref[...]], 0).astype(F32).T
    rows = gate_up.shape[0]
    out_ref[:rows] = gate_up.astype(BF16)
    out_ref[rows:] = down_ref[...]


def fold_block(block):
    tail = jnp.concatenate([block[64:], jnp.zeros((8, 320), F32)], 0)
    return jnp.concatenate([block[:64], tail], 1).astype(BF16)


def unfold_block(both):
    both = both.astype(F32)
    return jnp.concatenate([both[:, :320], both[:56, 320:]], 0)


def fill_exchange(outs, buffer, d):
    outs[0][...] = fold_block(buffer[d])
    outs[1][...] = fold_block(buffer[d ^ 1])
    for i in (1, 2, 3):
        outs[i + 1][:64] = fold_block(buffer[d ^ (2 * i)])
        outs[i + 1][64:] = fold_block(buffer[d ^ (2 * i + 1)])


def place_exchanged(refs, passed, d, buffer, convert):
    buffer[d] = convert(refs[0][...])
    buffer[d ^ 1] = convert(refs[1][...])
    for i in (1, 2, 3):
        buffer[d ^ (2 * i)] = convert(refs[i + 1][:64])
        buffer[d ^ (2 * i + 1)] = convert(passed[i - 1][64:])


def exchange_shapes():
    return [shape((64, 640), BF16)] * 2 + [shape((128, 640), BF16)] * 3


def exchange(blocks):
    arrived = [blocks[0], send(blocks[1], "dp", 1)]
    return arrived + [send(blocks[i + 1], "dp", 2 * i) for i in (1, 2, 3)]


def split_down(ids, feed_ref, *rest):
    outs, buffer = rest[-6:-1], rest[-1]
    for i in range(8):
        start = 360 * (i // 2) + 240
        buffer[i] = feed_ref[start : start + 120, 320 * (i % 2) : 320 * (i % 2) + 320].astype(F32)
    fill_exchange(outs, buffer, ids[0])


def flatten_block(block):
    return jnp.concatenate([block[:40], block[40:80], block[80:]], 1)


def restore_block(rows):
    return jnp.concatenate([rows[:, :320], rows[:, 320:640], rows[:, 640:960]], 0)


def join_down(ids, own_ref, pair_ref, *rest):
    others, passed_ref, out_ref, buffer = rest[:3], rest[3], rest[-2], rest[-1]
    d = ids[0]
    buffer[d] = restore_block(own_ref[...].astype(F32)[:40])
    buffer[d ^ 1] = restore_block(pair_ref[...].astype(F32)[:40])
    passed = passed_ref[...].astype(F32)
    for i in (1, 2, 3):
        buffer[d ^ (2 * i)] = restore_block(others[i - 1][128:].astype(F32)[:40])
        buffer[d ^ (2 * i + 1)] = restore_block(passed[40 * (i - 1) : 40 * i])
    for j in range(4):
        both = jnp.concatenate([buffer[2 * j], buffer[2 * j + 1]], 1)
        out_ref[120 * j : 120 * (j + 1), :] = both.astype(BF16)


def join_lines(own_ref, got_ref, ag_ref, fg_ref, *rest):
    out_ref = rest[-1]
    half = own_ref.shape[0]
    out_ref[: 2 * half] = jnp.concatenate([own_ref[...], got_ref[...]], 0)
    gains = jnp.concatenate([ag_ref[...], fg_ref[...]], 1)
    row = pad_lanes(gains, 0, out_ref.shape[1])
    out_ref[2 * half :] = jnp.broadcast_to(row, (16, out_ref.shape[1]))


def line_blocks(buffer, f, offset):
    return [
        jnp.concatenate(
            [buffer[2 * (f ^ j) + offset][:, :120], buffer[2 * (f ^ j ^ 2) + offset][:, :120]], 1
        )
        for j in (0, 1)
    ]


def mask_bias(seg_ref):
    length = seg_ref.shape[1]
    keys = jnp.broadcast_to(seg_ref[...].astype(F32), (length, length))
    index_q = lax.broadcasted_iota(jnp.int32, (length, length), 0)
    index_k = lax.broadcasted_iota(jnp.int32, (length, length), 1)
    allowed = (keys.T == keys) & (index_q >= index_k)
    return jnp.concatenate([jnp.where(allowed, 0.0, NEGATIVE)] * GROUP, 0)


def attention_forward(
    ids, x_ref, cos_ref, sin_ref, seg_ref, *rest
):
    first = rest[:8]
    second = rest[8:16]
    (
        x2_ref, h2_ref, att_ref, qr_ref, kr_ref, vr_ref, lse_ref, gains_ref,
        hb, tb, gb,
    ) = rest[16:]
    d = ids[0]
    f = ids[1]
    length = x_ref.shape[1]
    for s in range(8):
        gb[d ^ s] = first[s][240:248, :256].astype(F32)
    gain_one = jnp.concatenate([gb[i][:, :120] for i in range(8)], 1)
    gain_two = jnp.concatenate([gb[i][:, 120:240] for i in range(8)], 1)
    gains_ref[0] = gain_one
    gains_ref[1] = gain_two
    x = x_ref[...].astype(F32).T
    scale = lax.rsqrt(jnp.mean(x * x, -1, keepdims=True) + EPS)
    h1 = (x * scale * gain_one[:1]).astype(BF16)
    for i, block in enumerate(blocks_of(h1, 120)):
        hb[i, :, :120] = block
    left = line_blocks(hb, f, 0)
    right = line_blocks(hb, f, 1)
    for s in range(8):
        a = dot(left[0], first[s][:240, 0:256]) + dot(left[1], second[s][:240, 0:256])
        b = dot(right[0], first[s][:240, 384:640]) + dot(right[1], second[s][:240, 384:640])
        tb[d ^ s, :, :200] = a[:, :200] + b[:, 56:256]
    parts = [tb[i] for i in range(8)]
    q = jnp.concatenate([p[:, :120] for p in parts], 1)
    k = jnp.concatenate([p[:, 120:160] for p in parts], 1)
    v = jnp.concatenate([p[:, 160:200] for p in parts], 1)
    cosines = cos_ref[...]
    sines = sin_ref[...]
    bias = mask_bias(seg_ref)
    heads = []
    for g in range(KV_HEADS):
        kg = k[:, g * HD : (g + 1) * HD]
        kr = (kg * cosines + turn(kg) * sines).astype(BF16)
        vr = v[:, g * HD : (g + 1) * HD].astype(BF16)
        rows = []
        for h in range(g * GROUP, (g + 1) * GROUP):
            qh = q[:, h * HD : (h + 1) * HD]
            rows.append((qh * cosines + turn(qh) * sines).astype(BF16))
        qr = jnp.concatenate(rows, 0)
        qr_ref[g] = qr
        kr_ref[g] = kr
        vr_ref[g] = vr
        scores = contract_last(qr, kr) * HD ** (-0.5) + bias
        top = jnp.max(scores, -1, keepdims=True)
        exps = jnp.exp(scores - top)
        totals = jnp.sum(exps, -1, keepdims=True)
        lse_ref[g] = top + jnp.log(totals)
        probs = (exps / totals).astype(BF16)
        out = dot(probs, vr).astype(BF16)
        heads += [out[i * length : (i + 1) * length] for i in range(GROUP)]
    attended = jnp.concatenate(heads, 1)
    att_ref[...] = attended
    for i, block in enumerate(blocks_of(attended, 120)):
        hb[i, :, :120] = block
    left = line_blocks(hb, f, 0)
    right = line_blocks(hb, f, 1)
    for s in range(8):
        a = dot(left[0], first[s][:240, 128:384]) + dot(left[1], second[s][:240, 128:384])
        b = dot(right[0], first[s][:240, 256:512]) + dot(right[1], second[s][:240, 256:512])
        tb[d ^ s, :, :120] = a[:, 72:192] + b[:, 64:184]
    x2 = x + jnp.concatenate([tb[i][:, :120] for i in range(8)], 1)
    x2_ref[...] = x2
    scale_two = lax.rsqrt(jnp.mean(x2 * x2, -1, keepdims=True) + EPS)
    h2_ref[...] = (x2 * scale_two * gain_two[:1]).astype(BF16)


def start_stack(refs, buffer, sems):
    copies = []
    for s, ref in enumerate(refs):
        rows = ref.shape[0]
        copy = pltpu.make_async_copy(ref, buffer.at[pl.ds(s * rows, rows)], sems.at[s])
        copy.start()
        copies.append(copy)
    return copies


def start_columns(refs, buffer, sems):
    copies = []
    for s, ref in enumerate(refs):
        target = buffer.at[s // 2, :, pl.ds(128 * (s % 2), 128)]
        copy = pltpu.make_async_copy(ref, target, sems.at[s])
        copy.start()
        copies.append(copy)
    return copies


def feed_critical(ids, *rest):
    h_refs, c_refs, feed_ref, down_refs = rest[:8], rest[8:16], rest[16], rest[17:22]
    even_ref, odd_ref, delta_ref, mixed_ref, dt, own_ref = rest[25:31]
    fat_refs = rest[31:34]
    hs, cs, gu, db, h_sems, c_sems = rest[34:]
    passed = rest[22:25]
    c_copies = start_columns(c_refs, cs, c_sems)
    h_copies = start_stack(h_refs, hs, h_sems)
    d = ids[0]
    for j in range(4):
        gu[240 * j : 240 * (j + 1), :] = feed_ref[360 * j : 360 * j + 240, :]
    place_exchanged(down_refs, passed, d, db, unfold_block)
    dt[...] = jnp.concatenate([db[i] for i in range(8)], 0).astype(BF16)
    for copy in c_copies + h_copies:
        copy.wait()
    units = dt.shape[1]

    def step(c, carry):
        rows = pl.ds(pl.multiple_of(c * 256, 256), 256)
        both = dot(hs[rows, :], gu[...])
        mixed_grad = contract_first(cs[c], dt[...])
        gate = both[:, :units]
        up = both[:, units:]
        sig = 1.0 / (1.0 + jnp.exp(-gate))
        silu = gate * sig
        mixed_ref[rows, :] = (silu * up).astype(BF16)
        gate_delta = (mixed_grad * up * sig * (1.0 + gate * (1.0 - sig))).astype(BF16)
        up_delta = (mixed_grad * silu).astype(BF16)
        deltas = jnp.concatenate([gate_delta, up_delta], 1)
        delta_ref[rows, :] = deltas
        back = contract_last(deltas, gu[...])
        even_ref[c] = back[:128]
        odd_ref[pl.ds(pl.multiple_of(c * 128, 128), 128), :960] = back[128:].astype(BF16)
        return carry

    lax.fori_loop(0, 4, step, 0)
    for j in range(4):
        part = jnp.zeros((240, 320), F32)
        for c in range(4):
            rows = slice(256 * c, 256 * (c + 1))
            part = part + dot(cs[c, 240 * j : 240 * (j + 1), :], mixed_ref[rows, :])
        db[2 * j] = part[:120]
        db[2 * j + 1] = part[120:]
    filler = jnp.zeros((8, 960), F32)
    own_ref[...] = jnp.concatenate([flatten_block(db[d]), filler], 0).astype(BF16)
    pair = jnp.concatenate([flatten_block(db[d ^ 1]), filler], 0)
    odd_ref[512:, :960] = pair.astype(BF16)
    for i in (1, 2, 3):
        both = [flatten_block(db[d ^ (2 * i)]), flatten_block(db[d ^ (2 * i + 1)])]
        fat_refs[i - 1][...] = jnp.concatenate(both, 0).astype(BF16)


def pair_sum_down(even_ref, odd_ref, *rest):
    fat_refs, own_ref, pair_ref = rest[:3], rest[3], rest[4]
    rows = own_ref.shape[0]
    own_ref[...] = even_ref[0] + odd_ref[:rows, :960].astype(F32)
    pair_ref[...] = odd_ref[4 * rows :, :960]
    for i, ref in enumerate(rest[5:], 1):
        total = even_ref[i] + odd_ref[rows * i : rows * (i + 1), :960].astype(F32)
        ref[:rows] = total.astype(BF16)
        ref[rows:] = fat_refs[i - 1][...]


def pair_sum(even_ref, odd_ref, *rest):
    own_ref, a_ref, b_ref, c_ref = rest[-4:]
    rows = own_ref.shape[0]
    own_ref[...] = even_ref[0] + odd_ref[:rows, :960].astype(F32)
    for i, ref in ((1, a_ref), (2, b_ref), (3, c_ref)):
        ref[...] = (even_ref[i] + odd_ref[rows * i : rows * (i + 1), :960].astype(F32)).astype(BF16)


def feed_rest(*rest):
    h_refs, dt, delta_ref, mixed_ref = rest[:8], rest[8], rest[9], rest[10]
    grad_ref, even_ref, odd_ref, hs, h_sems = rest[12:]
    for copy in start_stack(h_refs, hs, h_sems):
        copy.wait()
    for j in range(4):
        part = contract_first(hs[:, 240 * j : 240 * (j + 1)], delta_ref[...])
        grad_ref[240 * j : 240 * (j + 1), :] = part.astype(BF16)
    down = dt[...]
    for c in range(4):
        part = contract_last(mixed_ref[256 * c : 256 * (c + 1), :], down)
        even_ref[c] = part[:128]
        odd_ref[128 * c : 128 * (c + 1), :960] = part[128:].astype(BF16)


def spread_line(buffer, parts, f, offset):
    for j, part in enumerate(parts):
        buffer[2 * (f ^ j) + offset, :, :120] = part[:, :120]
        buffer[2 * (f ^ j ^ 2) + offset, :, :120] = part[:, 120:240]


def attention_backward(ids, *rest):
    own_ref, a_ref, b_ref, c_ref, cot_ref, x2_ref, x_ref, gains_ref = rest[:8]
    cos_ref, sin_ref, seg_ref, qr_ref, kr_ref, vr_ref, lse_ref = rest[8:15]
    first, second = rest[15:23], rest[23:31]
    outs = rest[-14:-6]
    grad_ref, pass_ref, fb, db, eb, gb = rest[-6:]
    d = ids[0]
    f = ids[1]
    length = x_ref.shape[1]
    gain_one = gains_ref[0, :1]
    gain_two = gains_ref[1, :1]
    dh2 = (
        own_ref[...]
        + a_ref[:128].astype(F32)
        + b_ref[:128].astype(F32)
        + c_ref[:128].astype(F32)
    )
    passed = [ref[128:].astype(F32)[40:] for ref in (a_ref, b_ref, c_ref)]
    passed = jnp.concatenate([*passed, jnp.zeros((8, 960), F32)], 0)
    pass_ref[...] = passed.astype(BF16)
    x2 = x2_ref[...]
    scale_two = lax.rsqrt(jnp.mean(x2 * x2, -1, keepdims=True) + EPS)
    unit = x2 * scale_two
    feed_gain_grad = jnp.sum(dh2 * unit, 0, keepdims=True)
    scaled = dh2 * gain_two
    dx2 = cot_ref[...].astype(F32).T + scale_two * (
        scaled - unit * jnp.mean(scaled * unit, -1, keepdims=True)
    )
    rounded = dx2.astype(BF16)
    for i, block in enumerate(blocks_of(rounded, 120)):
        db[i, :, :120] = block
    left = [jnp.zeros((length, 240), F32)] * 2
    right = [jnp.zeros((length, 240), F32)] * 2
    for s in range(8):
        mine = db[d ^ s][:, :120]
        for_left = pad_lanes(mine, 72, 256)
        for_right = pad_lanes(mine, 64, 256)
        left[0] = left[0] + contract_last(for_left, first[s][:240, 128:384])
        left[1] = left[1] + contract_last(for_left, second[s][:240, 128:384])
        right[0] = right[0] + contract_last(for_right, first[s][:240, 256:512])
        right[1] = right[1] + contract_last(for_right, second[s][:240, 256:512])
    spread_line(fb, left, f, 0)
    spread_line(fb, right, f, 1)
    grad = jnp.concatenate([fb[i][:, :120] for i in range(8)], 1).astype(BF16)
    cosines = cos_ref[...]
    sines = sin_ref[...]
    bias = mask_bias(seg_ref)
    dq, dk, dv = [], [], []
    for g in range(KV_HEADS):
        qr = qr_ref[g]
        kr = kr_ref[g]
        vr = vr_ref[g]
        grads = jnp.concatenate(
            [grad[:, h * HD : (h + 1) * HD] for h in range(g * GROUP, (g + 1) * GROUP)], 0
        )
        probs = jnp.exp(contract_last(qr, kr) * HD ** (-0.5) + bias - lse_ref[g])
        dv.append(contract_first(probs.astype(BF16), grads).astype(BF16))
        dprob = contract_last(grads, vr)
        inner = jnp.sum(probs * dprob, -1, keepdims=True)
        ds = (probs * (dprob - inner) * HD ** (-0.5)).astype(BF16)
        dqg = dot(ds, kr)
        dkg = contract_first(ds, qr)
        dk.append((dkg * cosines - turn(dkg * sines)).astype(BF16))
        for i in range(GROUP):
            part = dqg[i * length : (i + 1) * length]
            dq.append((part * cosines - turn(part * sines)).astype(BF16))
    dq = blocks_of(jnp.concatenate(dq, 1), 120)
    dk = blocks_of(jnp.concatenate(dk, 1), 40)
    dv = blocks_of(jnp.concatenate(dv, 1), 40)
    for i in range(8):
        eb[i, :, :200] = jnp.concatenate([dq[i], dk[i], dv[i]], 1)
    left = [jnp.zeros((length, 240), F32)] * 2
    right = [jnp.zeros((length, 240), F32)] * 2
    for s in range(8):
        mine = eb[d ^ s][:, :200]
        for_left = pad_lanes(mine, 0, 256)
        for_right = pad_lanes(mine, 56, 256)
        left[0] = left[0] + contract_last(for_left, first[s][:240, 0:256])
        left[1] = left[1] + contract_last(for_left, second[s][:240, 0:256])
        right[0] = right[0] + contract_last(for_right, first[s][:240, 384:640])
        right[1] = right[1] + contract_last(for_right, second[s][:240, 384:640])
    spread_line(fb, left, f, 0)
    spread_line(fb, right, f, 1)
    dh1 = jnp.concatenate([fb[i][:, :120] for i in range(8)], 1)
    x = x_ref[...].astype(F32).T
    scale_one = lax.rsqrt(jnp.mean(x * x, -1, keepdims=True) + EPS)
    unit = x * scale_one
    attention_gain_grad = jnp.sum(dh1 * unit, 0, keepdims=True)
    scaled = dh1 * gain_one
    input_grad = dx2 + scale_one * (
        scaled - unit * jnp.mean(scaled * unit, -1, keepdims=True)
    )
    grad_ref[...] = input_grad.T
    for i in range(8):
        row = jnp.concatenate(
            [feed_gain_grad[:, 120 * i : 120 * (i + 1)], attention_gain_grad[:, 120 * i : 120 * (i + 1)]], 1
        )
        gb[i] = jnp.broadcast_to(pad_lanes(row, 0, 640), (16, 640))
    half = length // 2
    for s in range(8):
        delta = eb[d ^ s][:, :200]
        mine = db[d ^ s][:, :120]
        outs[s][:half] = jnp.concatenate(
            [delta[:half], mine[:half], mine[half:], delta[half:]], 1
        )
        outs[s][half:] = gb[d ^ s].astype(BF16)


def attention_weights(ids, *rest):
    x_refs, att_ref, got, gains_ref = rest[:8], rest[8], rest[9:17], rest[17]
    own_ref, g1_ref, g2_ref, g3_ref, hs, dl, acc = rest[21:]
    d = ids[0]
    f = ids[1]
    length = 128
    half = 64
    gain_sum = jnp.zeros((8, 640), F32)
    for s in range(8):
        block = got[s][:half]
        start = pl.multiple_of(length * (d ^ s), length)
        dl[pl.ds(start, half), 0:320] = block[:, :320]
        dl[pl.ds(start + half, half), 0:320] = jnp.concatenate(
            [block[:, 440:], block[:, 320:440]], 1
        )
        gain_sum = gain_sum + got[s][half : half + 8].astype(F32)
    gain_one = gains_ref[0].T[:, :1]
    for s in range(8):
        x = x_refs[s][...].astype(F32)
        scale = lax.rsqrt(jnp.mean(x * x, 0, keepdims=True) + EPS)
        start = pl.multiple_of(length * (d ^ s), length)
        hs[:, pl.ds(start, length)] = (x * scale * gain_one).astype(BF16)
    qkv = dot(hs[...], dl[:, :200]).T
    out = contract_first(dl[:, 200:320], att_ref[...])
    both = jnp.concatenate([qkv, out], 0)
    for i in range(4):
        acc[i, :320, :240] = both[:, 240 * i : 240 * (i + 1)]
        acc[i, 320:, :240] = jnp.concatenate([gain_sum[:, :240]] * 2, 0)
    own_ref[...] = acc[f][:, :240]
    for j, ref in ((1, g1_ref), (2, g2_ref), (3, g3_ref)):
        ref[...] = acc[f ^ j][:, :240].astype(BF16)


def finish_feed(sum_ref, _, gate_ref, up_ref):
    total = sum_ref[...].astype(F32).T
    gate_ref[...] = total[:320]
    up_ref[...] = total[320:]


def finish_output(x2_ref, own_ref, a_ref, b_ref, c_ref, out_ref):
    total = (
        x2_ref[...]
        + own_ref[...]
        + a_ref[...].astype(F32)
        + b_ref[...].astype(F32)
        + c_ref[...].astype(F32)
    )
    out_ref[...] = total.T.astype(BF16)


def finish_attention(own_ref, a_ref, b_ref, c_ref, down_ref, *rest):
    q_ref, k_ref, v_ref, o_ref, ag_ref, fg_ref, down_out = rest[-7:]
    down_out[...] = down_ref[...].astype(F32)
    total = (
        own_ref[...] + a_ref[...].astype(F32) + b_ref[...].astype(F32) + c_ref[...].astype(F32)
    )
    q_ref[...] = total[:120].T
    k_ref[...] = total[120:160]
    v_ref[...] = total[160:200]
    o_ref[...] = total[200:320].T
    fg_ref[...] = total[320:321, :120]
    ag_ref[...] = total[320:321, 120:240]


def fast(
    hidden_in,
    segment_ids,
    positions,
    query_weight,
    key_weight,
    value_weight,
    output_weight,
    attention_gain,
    gate_weight,
    up_weight,
    down_weight,
    feedforward_gain,
    output_cotangent,
):
    hidden = hidden_in[0].T
    cotangent = output_cotangent[0].T
    features, length = hidden.shape
    d = lax.axis_index("dp")
    f = lax.axis_index("fsdp")
    ids = jnp.stack([d, f]).astype(jnp.int32)
    tokens = 8 * length

    (block,) = kernel_call(
        pack_attention,
        [shape((120, 640), BF16)],
        [query_weight, key_weight.T, value_weight.T, output_weight],
    )
    far = [send(cotangent, "dp", s) for s in (2, 4, 6)]
    cotangent_slots = [cotangent, send(cotangent, "dp", 1)]
    for other in far:
        cotangent_slots += [other, send(other, "dp", 1)]
    line = send(block, "fsdp", 2)
    (chunk_a,) = kernel_call(
        join_lines,
        [shape((256, 640), BF16)],
        [block, line, attention_gain[None], feedforward_gain[None], *far],
        [None] * 4 + ["any"] * 3,
    )
    chunk_b = send(chunk_a, "fsdp", 1)
    a_near, a_far = send(chunk_a, "dp", 2), send(chunk_a, "dp", 4)
    chunk_b = after(chunk_b, a_near, a_far)
    b_near, b_far = send(chunk_b, "dp", 4), send(chunk_b, "dp", 2)
    a_near, b_near = after_all([a_near, b_near])
    a_last, b_last = send(a_near, "dp", 4), send(b_near, "dp", 2)
    first, second = [], []
    for value in (chunk_a, a_near, a_far, a_last):
        first += [value, send(value, "dp", 1)]
    for value in (chunk_b, b_far, b_near, b_last):
        second += [value, send(value, "dp", 1)]

    (feed,) = kernel_call(
        pack_feed,
        [shape((360, 640), BF16)],
        [gate_weight.T, up_weight.T, down_weight.T, chunk_b],
        [None, None, None, "any"],
    )
    feed = lax.all_gather(feed, "fsdp", axis=0, tiled=True)

    cosines, sines = rotary_tables(positions[0], HD)
    x2, h2, attended, qr, kr, vr, lse, gains = kernel_call(
        attention_forward,
        [
            shape((length, features), F32),
            shape((length, features), BF16),
            shape((length, features), BF16),
            shape((KV_HEADS, GROUP * length, HD), BF16),
            shape((KV_HEADS, length, HD), BF16),
            shape((KV_HEADS, length, HD), BF16),
            shape((KV_HEADS, GROUP * length, 1), F32),
            shape((2, 8, features), F32),
        ],
        [ids, hidden, cosines, sines, segment_ids, *first, *second],
        ["smem"] + [None] * 20,
        [
            pltpu.VMEM((8, length, 128), BF16),
            pltpu.VMEM((8, length, 256), F32),
            pltpu.VMEM((8, 8, 256), F32),
        ],
        16,
        8.5,
    )
    hidden_rows = after(hidden, b_near, b_far)
    far = [send(hidden_rows, "dp", s) for s in (2, 4, 6)]
    hidden_slots = [hidden_rows, send(hidden_rows, "dp", 1)]
    for other in far:
        hidden_slots += [other, send(other, "dp", 1)]
    down_blocks = kernel_call(
        split_down,
        exchange_shapes(),
        [ids, feed, h2, *far],
        ["smem", None] + ["any"] * 4,
        [pltpu.VMEM((8, 120, 320), F32)],
    )
    down_blocks = exchange(down_blocks)
    others = after_all([send(h2, "dp", s) for s in (2, 4, 6)], *down_blocks[1:])
    down_passed = [send(value, "dp", 1) for value in down_blocks[2:]]
    h2_slots = [h2, send(h2, "dp", 1)]
    for other in others:
        h2_slots += [other, send(other, "dp", 1)]
    attended = after(attended, *others, *down_passed)
    attended = lax.all_gather(attended, "dp", axis=0, tiled=True)
    even, odd, deltas, mixed, down, own_block, *fats = kernel_call(
        feed_critical,
        [
            shape((4, length, features), F32),
            shape((4 * length + 48, 1024), BF16),
            shape((tokens, 640), BF16),
            shape((tokens, 320), BF16),
            shape((features, 320), BF16),
            shape((48, 960), BF16),
        ]
        + [shape((80, 960), BF16)] * 3,
        [ids, *h2_slots, *cotangent_slots, feed, *down_blocks, *down_passed],
        ["smem"] + ["any"] * 16 + [None] * 9,
        [
            pltpu.VMEM((tokens, features), BF16),
            pltpu.VMEM((4, features, 256), BF16),
            pltpu.VMEM((features, 640), BF16),
            pltpu.VMEM((8, 120, 320), F32),
            pltpu.SemaphoreType.DMA((8,)),
            pltpu.SemaphoreType.DMA((8,)),
        ],
        24,
        9.0,
    )

    odd = send(odd, "dp", 1)
    back_own, pair_block, back_a, back_b, back_c = kernel_call(
        pair_sum_down,
        [shape((length, features), F32), shape((48, features), BF16)]
        + [shape((length + 80, features), BF16)] * 3,
        [even, odd, *fats],
    )
    back_a, back_b, back_c = send(back_a, "dp", 2), send(back_b, "dp", 4), send(back_c, "dp", 6)
    feed_grad, f_even, f_odd = kernel_call(
        feed_rest,
        [
            shape((4 * 240, 640), BF16),
            shape((4, length, features), F32),
            shape((4 * length, 1024), BF16),
        ],
        [*h2_slots, down, deltas, mixed, back_own],
        ["any"] * 8 + [None] * 3 + ["any"],
        [
            pltpu.VMEM((tokens, features), BF16),
            pltpu.SemaphoreType.DMA((8,)),
        ],
        24,
        9.0,
    )
    feed_grad = after(feed_grad, back_a, back_b, back_c, attended)
    feed_sum = lax.psum_scatter(feed_grad, "fsdp", scatter_dimension=0, tiled=True)
    *outgoing, input_grad, passed = kernel_call(
        attention_backward,
        [shape((80, 640), BF16)] * 8
        + [shape((features, length), F32), shape((length, features), BF16)],
        [
            ids, back_own, back_a, back_b, back_c, cotangent, x2, hidden, gains,
            cosines, sines, segment_ids, qr, kr, vr, lse, *first, *second, feed_grad,
        ],
        ["smem"] + [None] * 31 + ["any"],
        [
            pltpu.VMEM((8, length, 128), F32),
            pltpu.VMEM((8, length, 128), BF16),
            pltpu.VMEM((8, length, 256), BF16),
            pltpu.VMEM((8, 16, 640), F32),
        ],
        18,
        10.5,
    )
    arrived = [outgoing[0]] + [send(outgoing[s], "dp", s) for s in range(1, 8)]
    passed = send(passed, "dp", 1)
    (down_grad,) = kernel_call(
        join_down,
        [shape((4 * 120, 640), BF16)],
        [ids, own_block, pair_block, back_a, back_b, back_c, passed],
        ["smem"] + [None] * 6,
        [pltpu.VMEM((8, 120, 320), F32)],
    )
    f_odd = send(after(f_odd, outgoing[0]), "dp", 1)
    y_own, *y_parts = kernel_call(
        pair_sum,
        [shape((length, features), F32)] + [shape((length, features), BF16)] * 3,
        [f_even, f_odd, outgoing[0]],
        [None, None, "any"],
    )
    down_sum = lax.psum_scatter(down_grad, "fsdp", scatter_dimension=0, tiled=True)
    w0, w1, w2, w3 = kernel_call(
        attention_weights,
        [shape((336, 240), F32)] + [shape((336, 240), BF16)] * 3,
        [ids, *hidden_slots, attended, *arrived, gains, y_own, down_grad, feed_sum],
        ["smem"] + [None] * 18 + ["any"] * 3,
        [
            pltpu.VMEM((features, tokens), BF16),
            pltpu.VMEM((tokens, 320), BF16),
            pltpu.VMEM((4, 336, 256), F32),
        ],
        20,
        4.5,
    )

    y_parts = after_all(y_parts, w0)
    sums = [y_own] + [send(part, "dp", 2 * i + 2) for i, part in enumerate(y_parts)]
    parts = [send(w, "fsdp", j) for j, w in ((1, w1), (2, w2), (3, w3))]
    gate_out, up_out = kernel_call(
        finish_feed, [shape((320, 240), F32)] * 2, [feed_sum, parts[0]], [None, "any"]
    )
    (block_output,) = kernel_call(
        finish_output, [shape((features, length), BF16)], [x2, *sums]
    )
    q_out, k_out, v_out, o_out, ag_out, fg_out, down_out = kernel_call(
        finish_attention,
        [
            shape((240, 120), F32),
            shape((40, 240), F32),
            shape((40, 240), F32),
            shape((240, 120), F32),
            shape((1, 120), F32),
            shape((1, 120), F32),
            shape((120, 640), F32),
        ],
        [w0, *parts, down_sum, block_output, gate_out],
        [None] * 5 + ["any"] * 2,
    )
    return (
        block_output.T[None],
        input_grad.T[None],
        q_out,
        k_out.T,
        v_out.T,
        o_out,
        ag_out[0],
        gate_out.T,
        up_out.T,
        down_out.T,
        fg_out[0],
    )


def fits(mesh_shape):
    return mesh_shape["dp"] == 8 and mesh_shape["fsdp"] == 4


def solution(mesh):
    in_specs = (
        P(("dp", "fsdp"), None, None),
        P(("dp", "fsdp"), None),
        P(("dp", "fsdp"), None),
        P("fsdp", "dp"),
        P("fsdp", "dp"),
        P("fsdp", "dp"),
        P("fsdp", "dp"),
        P("dp"),
        P("fsdp", "dp"),
        P("fsdp", "dp"),
        P("fsdp", "dp"),
        P("dp"),
        P(("dp", "fsdp"), None, None),
    )
    out_specs = (
        P(("dp", "fsdp"), None, None),
        P(("dp", "fsdp"), None, None),
        P("fsdp", "dp"),
        P("fsdp", "dp"),
        P("fsdp", "dp"),
        P("fsdp", "dp"),
        P("dp"),
        P("fsdp", "dp"),
        P("fsdp", "dp"),
        P("fsdp", "dp"),
        P("dp"),
    )
    body = fast if fits(mesh.shape) else local
    return jax.shard_map(body, mesh=mesh, in_specs=in_specs, out_specs=out_specs, check_vma=False)
```

```python
import jax
import jax.numpy as jnp
from jax import lax
from jax.experimental import pallas as pl
from jax.experimental.pallas import tpu as pltpu
from jax.sharding import PartitionSpec as P

HEADS = 15
KV_HEADS = 5
HD = 64
GROUP = HEADS // KV_HEADS


EPS = 1e-05
THETA = 100000.0
NEGATIVE = -1e30
F32 = jnp.float32
BF16 = jnp.bfloat16


def rotary_tables(position, head_dim):
    inverse = THETA ** (-jnp.arange(0, head_dim, 2).astype(F32) / head_dim)
    angles = position.astype(F32)[:, None] * inverse[None, :]
    cosines = jnp.cos(angles)
    sine_values = jnp.sin(angles)
    return (
        jnp.concatenate([cosines, cosines], -1),
        jnp.concatenate([sine_values, sine_values], -1),
    )


def rotate(values, cosines, sine_values):
    half_dim = values.shape[-1] // 2
    turned = jnp.concatenate([-values[..., half_dim:], values[..., :half_dim]], -1)
    return values * cosines[:, None, :] + turned * sine_values[:, None, :]


def rotate_back(gradient, cosines, sine_values):
    half_dim = gradient.shape[-1] // 2
    sine_scaled = gradient * sine_values[:, None, :]
    turned = jnp.concatenate([-sine_scaled[..., half_dim:], sine_scaled[..., :half_dim]], -1)
    return gradient * cosines[:, None, :] - turned


def row_scale_of(values):
    return lax.rsqrt(jnp.mean(values * values, -1, keepdims=True) + EPS)


def norm_backward(values, row_scale, gain, upstream):
    unit_rows = values * row_scale
    scaled = upstream * gain
    gain_grad = jnp.sum(upstream * unit_rows, 0)
    result = row_scale * (scaled - unit_rows * jnp.mean(scaled * unit_rows, -1, keepdims=True))
    return (result, gain_grad)


def dot(left, right):
    return jnp.dot(left, right, preferred_element_type=F32)


def contract_first(left, right):
    return lax.dot_general(left, right, (((0,), (0,)), ((), ())), preferred_element_type=F32)


def contract_last(left, right):
    return lax.dot_general(left, right, (((1,), (1,)), ((), ())), preferred_element_type=F32)


def send(values, axis, distance):
    count = lax.axis_size(axis)
    return lax.ppermute(values, axis, [(i, i ^ distance) for i in range(count)])


def pick(blocks, index):
    return lax.dynamic_index_in_dim(blocks, index, 0, keepdims=False)


def reorder(blocks, me):
    return jnp.stack([pick(blocks, me ^ s) for s in range(blocks.shape[0])])


def plane_gather(values):
    count = lax.axis_size("dp")
    if count != 8:
        return reorder(lax.all_gather(values, "dp"), lax.axis_index("dp"))
    slots = [values, send(values, "dp", 1)] + [None] * 6
    for s in (2, 4, 6):
        slots[s] = send(values, "dp", s)
        slots[s + 1] = send(slots[s], "dp", 1)
    return jnp.stack(slots)


def plane_exchange(blocks):
    count = lax.axis_size("dp")
    if count != 8:
        me = lax.axis_index("dp")
        return reorder(lax.all_to_all(reorder(blocks, me), "dp", 0, 0), me)
    return jnp.stack([blocks[0]] + [send(blocks[s], "dp", s) for s in range(1, 8)])


def plane_sum(blocks):
    count = lax.axis_size("dp")
    if count != 8:
        return jnp.sum(plane_exchange(blocks.astype(BF16)).astype(F32), 0)
    odd = send(jnp.stack([blocks[s] for s in (1, 3, 5, 7)]).astype(BF16), "dp", 1)
    pair = [blocks[2 * i] + odd[i].astype(F32) for i in range(4)]
    total = pair[0]
    for i in range(1, 4):
        total = total + send(pair[i].astype(BF16), "dp", 2 * i).astype(F32)
    return total


def line_gather(values):
    me = lax.axis_index("fsdp")
    count = lax.axis_size("fsdp")
    out = jnp.zeros((count,) + values.shape, values.dtype)
    out = lax.dynamic_update_index_in_dim(out, values, me, 0)
    for s in range(1, count):
        out = lax.dynamic_update_index_in_dim(out, send(values, "fsdp", s), me ^ s, 0)
    return out


def line_sum(blocks):
    me = lax.axis_index("fsdp")
    total = pick(blocks, me)
    for s in range(1, lax.axis_size("fsdp")):
        total = total + send(pick(blocks, me ^ s).astype(BF16), "fsdp", s).astype(F32)
    return total


def down_routes(dp_count, fsdp_count):
    ratio = dp_count // fsdp_count
    routes = []
    for m in range(ratio):
        pairs = []
        for d in range(dp_count):
            for f in range(fsdp_count):
                target = (ratio * f + (m + d) % ratio) * fsdp_count + d // ratio
                pairs.append((d * fsdp_count + f, target))
        routes.append(pairs)
    return routes


def down_pieces(down_turned, dp_count, fsdp_count):
    ratio = dp_count // fsdp_count
    d = lax.axis_index("dp")
    width = down_turned.shape[1] // ratio
    halves = jnp.stack([down_turned[:, h * width : (h + 1) * width] for h in range(ratio)])
    got = [
        lax.ppermute(pick(halves, (m + d) % ratio), ("dp", "fsdp"), pairs)
        for m, pairs in enumerate(down_routes(dp_count, fsdp_count))
    ]
    stacked = jnp.stack(got)
    ordered = [pick(stacked, (d - j) % ratio) for j in range(ratio)]
    return jnp.concatenate(ordered, 0)


def down_return(grad_turned, dp_count, fsdp_count):
    ratio = dp_count // fsdp_count
    d = lax.axis_index("dp")
    height = grad_turned.shape[0] // ratio
    pieces = grad_turned.reshape(ratio, height, grad_turned.shape[1])
    got = []
    for m, pairs in enumerate(down_routes(dp_count, fsdp_count)):
        back = [(target, source) for source, target in pairs]
        got.append(lax.ppermute(pick(pieces, (d - m) % ratio), ("dp", "fsdp"), back))
    stacked = jnp.stack(got)
    return jnp.concatenate([pick(stacked, (h - d) % ratio) for h in range(ratio)], 1)


def masked_scores(query_turned, key_turned, segment):
    length = query_turned.shape[0]
    grouped = query_turned.reshape(length, KV_HEADS, GROUP, HD)
    scores = jnp.einsum("qkgd,tkd->kgqt", grouped, key_turned, preferred_element_type=F32)
    index = jnp.arange(length)
    allowed = (segment[:, None] == segment[None, :]) & (index[:, None] >= index[None, :])
    return jnp.where(allowed, scores * HD ** (-0.5), NEGATIVE)


def attend_forward(query_turned, key_turned, value_rounded, segment):
    length = query_turned.shape[0]
    scores = masked_scores(query_turned, key_turned, segment)
    row_max = jnp.max(scores, -1, keepdims=True)
    exponentials = jnp.exp(scores - row_max)
    totals = jnp.sum(exponentials, -1, keepdims=True)
    probs_rounded = (exponentials / totals).astype(BF16)
    attended = jnp.einsum("kgqt,tkd->qkgd", probs_rounded, value_rounded, preferred_element_type=F32)
    return (attended.reshape(length, HEADS * HD).astype(BF16), row_max + jnp.log(totals))


def attend_backward(query_turned, key_turned, value_rounded, segment, log_totals, attended_grad):
    length = query_turned.shape[0]
    grouped = query_turned.reshape(length, KV_HEADS, GROUP, HD)
    grad_grouped = attended_grad.reshape(length, KV_HEADS, GROUP, HD)
    scores = masked_scores(query_turned, key_turned, segment)
    probs_again = jnp.exp(scores - log_totals)
    value_sum = jnp.einsum(
        "kgqt,qkgd->tkd", probs_again.astype(BF16), grad_grouped, preferred_element_type=F32
    )
    prob_grad = jnp.einsum(
        "qkgd,tkd->kgqt", grad_grouped, value_rounded, preferred_element_type=F32
    )
    inner_rows = jnp.sum(probs_again * prob_grad, -1, keepdims=True)
    score_grad = (probs_again * (prob_grad - inner_rows) * HD ** (-0.5)).astype(BF16)
    query_part = jnp.einsum("kgqt,tkd->qkgd", score_grad, key_turned, preferred_element_type=F32)
    key_sum = jnp.einsum("kgqt,qkgd->tkd", score_grad, grouped, preferred_element_type=F32)
    return (query_part.reshape(length, HEADS, HD), key_sum, value_sum)


def local(
    hidden_in,
    segment_ids,
    positions,
    query_weight,
    key_weight,
    value_weight,
    output_weight,
    attention_gain,
    gate_weight,
    up_weight,
    down_weight,
    feedforward_gain,
    output_cotangent,
):
    hidden = hidden_in[0]
    hidden_rows = hidden.astype(F32)
    segment = segment_ids[0]
    cotangent = output_cotangent[0]
    length, features = hidden.shape
    width = HEADS * HD
    kv_width = KV_HEADS * HD
    dp_count = lax.axis_size("dp")
    fsdp_count = lax.axis_size("fsdp")
    d = lax.axis_index("dp")
    f = lax.axis_index("fsdp")
    q_cols = width // dp_count
    kv_cols = kv_width // dp_count
    x_cols = features // dp_count
    own_rows = features // fsdp_count
    qkv_cols = q_cols + 2 * kv_cols
    all_cols = qkv_cols + x_cols
    hidden_units = gate_weight.shape[1]

    attention_block = jnp.concatenate(
        [query_weight, key_weight, value_weight, output_weight], 1
    )
    attention_rows = line_gather(attention_block).reshape(features, all_cols)
    gains = jnp.concatenate(
        [attention_gain, feedforward_gain, jnp.zeros((all_cols - 2 * x_cols,), BF16)]
    )
    gains = jnp.concatenate([gains[None], jnp.zeros((15, all_cols), BF16)])
    slots = plane_gather(jnp.concatenate([attention_rows, gains], 0))
    gains_ordered = reorder(slots[:, features, :], d)
    attention_gain_full = gains_ordered[:, :x_cols].reshape(features).astype(F32)
    feed_gain_full = gains_ordered[:, x_cols : 2 * x_cols].reshape(features).astype(F32)
    qkv_slots = slots[:, :features, :qkv_cols]
    output_slots = slots[:, :features, qkv_cols:]

    down_block = down_pieces(down_weight.T, dp_count, fsdp_count)
    feed_block = jnp.concatenate([gate_weight, up_weight, down_block], 1)
    feed = line_gather(feed_block).reshape(features, 3 * hidden_units)

    tokens = plane_gather(jnp.stack([hidden, cotangent]))
    hidden_all = tokens[:, 0].reshape(dp_count * length, features)
    cotangent_all = tokens[:, 1].reshape(dp_count * length, features)

    scale_one = row_scale_of(hidden_rows)
    normed_one = (hidden_rows * scale_one * attention_gain_full).astype(BF16)
    cosines, sine_values = rotary_tables(positions[0], HD)
    qkv = reorder(jnp.einsum("td,sdc->stc", normed_one, qkv_slots, preferred_element_type=F32), d)

    def columns(start, count):
        part = qkv[:, :, start : start + count]
        return part.transpose(1, 0, 2).reshape(length, dp_count * count)

    query_proj = columns(0, q_cols).reshape(length, HEADS, HD)
    key_proj = columns(q_cols, kv_cols).reshape(length, KV_HEADS, HD)
    value_proj = columns(q_cols + kv_cols, kv_cols).reshape(length, KV_HEADS, HD)
    query_turned = rotate(query_proj, cosines, sine_values).astype(BF16)
    key_turned = rotate(key_proj, cosines, sine_values).astype(BF16)
    value_rounded = value_proj.astype(BF16)
    attended, log_totals = attend_forward(query_turned, key_turned, value_rounded, segment)
    added = reorder(jnp.einsum("td,sdc->stc", attended, output_slots, preferred_element_type=F32), d)
    residual = hidden_rows + added.transpose(1, 0, 2).reshape(length, features)

    scale_two = row_scale_of(residual)
    normed_two = (residual * scale_two * feed_gain_full).astype(BF16)
    normed_two_all = plane_gather(normed_two).reshape(dp_count * length, features)
    gate_up = feed[:, : 2 * hidden_units]
    down_turned = feed[:, 2 * hidden_units :]
    both = dot(normed_two_all, gate_up)
    gate_proj = both[:, :hidden_units]
    up_proj = both[:, hidden_units:]
    mixed_grad = dot(cotangent_all, down_turned)
    sigmoid_gate = jax.nn.sigmoid(gate_proj)
    silu_gate = gate_proj * sigmoid_gate
    mixed = (silu_gate * up_proj).astype(BF16)
    gate_delta = (
        mixed_grad * up_proj * sigmoid_gate * (1.0 + gate_proj * (1.0 - sigmoid_gate))
    ).astype(BF16)
    up_delta = (mixed_grad * silu_gate).astype(BF16)
    deltas = jnp.concatenate([gate_delta, up_delta], 1)
    normed_two_grad = plane_sum(
        contract_last(deltas, gate_up).reshape(dp_count, length, features)
    )
    gate_up_grad = contract_first(normed_two_all, deltas)
    down_grad = contract_first(cotangent_all, mixed)
    feed_grad = jnp.concatenate([gate_up_grad, down_grad], 1).reshape(
        fsdp_count, own_rows, 3 * hidden_units
    )
    fed = plane_sum(contract_last(mixed, down_turned).reshape(dp_count, length, features))
    block_output = (residual + fed).astype(BF16)
    attended_all = plane_gather(attended).reshape(dp_count * length, width)

    residual_part, feed_gain_grad = norm_backward(
        residual, scale_two, feed_gain_full, normed_two_grad
    )
    residual_grad = cotangent.astype(F32) + residual_part
    feed_sum = line_sum(feed_grad)

    residual_rounded = residual_grad.astype(BF16)
    residual_blocks = residual_rounded.reshape(length, dp_count, x_cols).transpose(1, 0, 2)
    residual_slots = reorder(residual_blocks, d)
    attended_grad = jnp.einsum(
        "stc,sdc->td", residual_slots, output_slots, preferred_element_type=F32
    ).astype(BF16)
    query_raw, key_raw, value_raw = attend_backward(
        query_turned, key_turned, value_rounded, segment, log_totals, attended_grad
    )
    query_delta = rotate_back(query_raw, cosines, sine_values).astype(BF16)
    key_delta = rotate_back(key_raw, cosines, sine_values).astype(BF16)
    value_delta = value_raw.astype(BF16)
    qkv_delta = jnp.concatenate(
        [
            part.reshape(length, dp_count, -1).transpose(1, 0, 2)
            for part in (query_delta, key_delta, value_delta)
        ],
        2,
    )
    delta_slots = reorder(qkv_delta, d)
    normed_one_grad = jnp.einsum(
        "stc,sdc->td", delta_slots, qkv_slots, preferred_element_type=F32
    )
    input_part, attention_gain_grad = norm_backward(
        hidden_rows, scale_one, attention_gain_full, normed_one_grad
    )
    input_grad = residual_grad + input_part

    gain_rows = jnp.concatenate(
        [
            feed_gain_grad.reshape(dp_count, 1, x_cols),
            attention_gain_grad.reshape(dp_count, 1, x_cols),
            jnp.zeros((dp_count, 1, all_cols - 2 * x_cols), F32),
        ],
        2,
    ).astype(BF16)
    gain_rows = jnp.pad(reorder(gain_rows, d), ((0, 0), (0, 15), (0, 0)))
    outgoing = jnp.concatenate(
        [jnp.concatenate([delta_slots, residual_slots], 2), gain_rows], 1
    )
    arrived = plane_exchange(outgoing)
    deltas_all = arrived[:, :length].reshape(dp_count * length, all_cols)
    gain_sums = jnp.sum(arrived[:, length].astype(F32), 0)
    hidden_all_rows = hidden_all.astype(F32)
    normed_one_all = (
        hidden_all_rows * row_scale_of(hidden_all_rows) * attention_gain_full
    ).astype(BF16)
    qkv_grad = contract_first(normed_one_all, deltas_all[:, :qkv_cols])
    output_grad = contract_first(attended_all, deltas_all[:, qkv_cols:])
    attention_grad = jnp.concatenate([qkv_grad, output_grad], 1).reshape(
        fsdp_count, own_rows, all_cols
    )
    gain_block = jnp.broadcast_to(
        jnp.pad(gain_sums[None], ((0, 15), (0, 0)))[None], (fsdp_count, 16, all_cols)
    )
    attention_sum = line_sum(jnp.concatenate([attention_grad, gain_block], 1))
    down_out = down_return(feed_sum[:, 2 * hidden_units :], dp_count, fsdp_count).T

    ends = (q_cols, q_cols + kv_cols, qkv_cols)
    return (
        block_output[None],
        input_grad[None],
        attention_sum[:own_rows, : ends[0]],
        attention_sum[:own_rows, ends[0] : ends[1]],
        attention_sum[:own_rows, ends[1] : ends[2]],
        attention_sum[:own_rows, ends[2] :],
        attention_sum[own_rows, x_cols : 2 * x_cols],
        feed_sum[:, :hidden_units],
        feed_sum[:, hidden_units : 2 * hidden_units],
        down_out,
        attention_sum[own_rows, :x_cols],
    )


def vspec():
    return pl.BlockSpec(memory_space=pltpu.VMEM)


def kernel_call(body, outs, args, specs=None, scratch=(), megabytes=8, micros=1.0):
    if specs is None:
        specs = [None] * len(args)
    kinds = {
        None: pltpu.VMEM,
        "any": pl.ANY,
        "smem": pltpu.SMEM,
    }
    return pl.pallas_call(
        body,
        out_shape=outs,
        in_specs=[pl.BlockSpec(memory_space=kinds[s]) for s in specs],
        out_specs=[pl.BlockSpec(memory_space=pltpu.VMEM) for _ in outs],
        scratch_shapes=list(scratch),
        compiler_params=pltpu.CompilerParams(vmem_limit_bytes=63 * 2**20),
        cost_estimate=pl.CostEstimate(
            flops=int(micros * 1.1e9), bytes_accessed=int(micros * 3.0e6), transcendentals=0
        ),
    )(*args)


def after_all(values, *others):
    count = len(values)
    return pl.pallas_call(
        lambda *refs: None,
        out_shape=[shape(value.shape, value.dtype) for value in values],
        in_specs=[pl.BlockSpec(memory_space=pl.ANY)] * (count + len(others)),
        out_specs=[pl.BlockSpec(memory_space=pl.ANY)] * count,
        input_output_aliases={i: i for i in range(count)},
    )(*values, *others)


def after(value, *others):
    return after_all([value], *others)[0]


def shape(dims, dtype):
    return jax.ShapeDtypeStruct(dims, dtype)


def blocks_of(values, width):
    return [values[:, i : i + width] for i in range(0, values.shape[1], width)]


def turn(values):
    half = values.shape[-1] // 2
    return jnp.concatenate([-values[:, half:], values[:, :half]], 1)


def pad_lanes(values, before, total):
    rows, count = values.shape
    parts = []
    if before:
        parts.append(jnp.zeros((rows, before), values.dtype))
    parts.append(values)
    if total - before - count:
        parts.append(jnp.zeros((rows, total - before - count), values.dtype))
    return jnp.concatenate(parts, 1)


def pack_attention(q_ref, k_ref, v_ref, o_ref, out_ref):
    kv = jnp.concatenate([k_ref[...], v_ref[...]], 0).astype(F32).T.astype(BF16)
    qkv = jnp.concatenate([q_ref[...], kv], 1)
    o = o_ref[...]
    half = o.shape[0] // 2
    out_ref[...] = jnp.concatenate([qkv[:half], o[:half], o[half:], qkv[half:]], 1)


def pack_feed(gate_ref, up_ref, down_ref, _, out_ref):
    gate_up = jnp.concatenate([gate_ref[...], up_ref[...]], 0).astype(F32).T
    rows = gate_up.shape[0]
    out_ref[:rows] = gate_up.astype(BF16)
    out_ref[rows:] = down_ref[...]


def fold_block(block):
    tail = jnp.concatenate([block[64:], jnp.zeros((8, 320), F32)], 0)
    return jnp.concatenate([block[:64], tail], 1).astype(BF16)


def unfold_block(both):
    both = both.astype(F32)
    return jnp.concatenate([both[:, :320], both[:56, 320:]], 0)


def fill_exchange(outs, buffer, d):
    outs[0][...] = fold_block(buffer[d])
    outs[1][...] = fold_block(buffer[d ^ 1])
    for i in (1, 2, 3):
        outs[i + 1][:64] = fold_block(buffer[d ^ (2 * i)])
        outs[i + 1][64:] = fold_block(buffer[d ^ (2 * i + 1)])


def place_exchanged(refs, passed, d, buffer, convert):
    buffer[d] = convert(refs[0][...])
    buffer[d ^ 1] = convert(refs[1][...])
    for i in (1, 2, 3):
        buffer[d ^ (2 * i)] = convert(refs[i + 1][:64])
        buffer[d ^ (2 * i + 1)] = convert(passed[i - 1][64:])


def exchange_shapes():
    return [shape((64, 640), BF16)] * 2 + [shape((128, 640), BF16)] * 3


def exchange(blocks):
    arrived = [blocks[0], send(blocks[1], "dp", 1)]
    return arrived + [send(blocks[i + 1], "dp", 2 * i) for i in (1, 2, 3)]


def split_down(ids, feed_ref, *rest):
    outs, buffer = rest[-6:-1], rest[-1]
    for i in range(8):
        start = 360 * (i // 2) + 240
        buffer[i] = feed_ref[start : start + 120, 320 * (i % 2) : 320 * (i % 2) + 320].astype(F32)
    fill_exchange(outs, buffer, ids[0])


def flatten_block(block):
    return jnp.concatenate([block[:40], block[40:80], block[80:]], 1)


def restore_block(rows):
    return jnp.concatenate([rows[:, :320], rows[:, 320:640], rows[:, 640:960]], 0)


def join_lines(own_ref, got_ref, ag_ref, fg_ref, *rest):
    out_ref = rest[-1]
    half = own_ref.shape[0]
    out_ref[: 2 * half] = jnp.concatenate([own_ref[...], got_ref[...]], 0)
    gains = jnp.concatenate([ag_ref[...], fg_ref[...]], 1)
    row = pad_lanes(gains, 0, out_ref.shape[1])
    out_ref[2 * half :] = jnp.broadcast_to(row, (16, out_ref.shape[1]))


def line_blocks(buffer, f, offset):
    return [
        jnp.concatenate(
            [buffer[2 * (f ^ j) + offset][:, :120], buffer[2 * (f ^ j ^ 2) + offset][:, :120]], 1
        )
        for j in (0, 1)
    ]


def mask_bias(seg_ref):
    length = seg_ref.shape[1]
    keys = jnp.broadcast_to(seg_ref[...].astype(F32), (length, length))
    index_q = lax.broadcasted_iota(jnp.int32, (length, length), 0)
    index_k = lax.broadcasted_iota(jnp.int32, (length, length), 1)
    allowed = (keys.T == keys) & (index_q >= index_k)
    return jnp.concatenate([jnp.where(allowed, 0.0, NEGATIVE)] * GROUP, 0)


def attention_forward(
    ids, x_ref, cos_ref, sin_ref, seg_ref, *rest
):
    first = rest[:8]
    second = rest[8:16]
    (
        x2_ref, h2_ref, att_ref, qr_ref, kr_ref, vr_ref, probs_ref, gains_ref,
        hb, tb, gb,
    ) = rest[16:]
    d = ids[0]
    f = ids[1]
    length = x_ref.shape[1]
    for s in range(8):
        gb[d ^ s] = first[s][240:248, :256].astype(F32)
    gain_one = jnp.concatenate([gb[i][:, :120] for i in range(8)], 1)
    gain_two = jnp.concatenate([gb[i][:, 120:240] for i in range(8)], 1)
    gains_ref[0] = gain_one
    gains_ref[1] = gain_two
    x = x_ref[...].astype(F32).T
    scale = lax.rsqrt(jnp.mean(x * x, -1, keepdims=True) + EPS)
    h1 = (x * scale * gain_one[:1]).astype(BF16)
    for i, block in enumerate(blocks_of(h1, 120)):
        hb[i, :, :120] = block
    left = line_blocks(hb, f, 0)
    right = line_blocks(hb, f, 1)
    for s in range(8):
        a = dot(left[0], first[s][:240, 0:256]) + dot(left[1], second[s][:240, 0:256])
        b = dot(right[0], first[s][:240, 384:640]) + dot(right[1], second[s][:240, 384:640])
        tb[d ^ s, :, :200] = a[:, :200] + b[:, 56:256]
    parts = [tb[i] for i in range(8)]
    q = jnp.concatenate([p[:, :120] for p in parts], 1)
    k = jnp.concatenate([p[:, 120:160] for p in parts], 1)
    v = jnp.concatenate([p[:, 160:200] for p in parts], 1)
    cosines = cos_ref[...]
    sines = sin_ref[...]
    bias = mask_bias(seg_ref)
    heads = []
    for g in range(KV_HEADS):
        kg = k[:, g * HD : (g + 1) * HD]
        kr = (kg * cosines + turn(kg) * sines).astype(BF16)
        vr = v[:, g * HD : (g + 1) * HD].astype(BF16)
        rows = []
        for h in range(g * GROUP, (g + 1) * GROUP):
            qh = q[:, h * HD : (h + 1) * HD]
            rows.append((qh * cosines + turn(qh) * sines).astype(BF16))
        qr = jnp.concatenate(rows, 0)
        qr_ref[g] = qr
        kr_ref[g] = kr
        vr_ref[g] = vr
        scores = contract_last(qr, kr) * HD ** (-0.5) + bias
        top = jnp.max(scores, -1, keepdims=True)
        exps = jnp.exp(scores - top)
        totals = jnp.sum(exps, -1, keepdims=True)
        probs = exps / totals
        probs_ref[g] = probs
        probs = probs.astype(BF16)
        out = dot(probs, vr).astype(BF16)
        heads += [out[i * length : (i + 1) * length] for i in range(GROUP)]
    attended = jnp.concatenate(heads, 1)
    att_ref[...] = attended
    for i, block in enumerate(blocks_of(attended, 120)):
        hb[i, :, :120] = block
    left = line_blocks(hb, f, 0)
    right = line_blocks(hb, f, 1)
    for s in range(8):
        a = dot(left[0], first[s][:240, 128:384]) + dot(left[1], second[s][:240, 128:384])
        b = dot(right[0], first[s][:240, 256:512]) + dot(right[1], second[s][:240, 256:512])
        tb[d ^ s, :, :120] = a[:, 72:192] + b[:, 64:184]
    x2 = x + jnp.concatenate([tb[i][:, :120] for i in range(8)], 1)
    x2_ref[...] = x2
    scale_two = lax.rsqrt(jnp.mean(x2 * x2, -1, keepdims=True) + EPS)
    h2_ref[...] = (x2 * scale_two * gain_two[:1]).astype(BF16)


def start_stack(refs, buffer, sems):
    copies = []
    for s, ref in enumerate(refs):
        rows = ref.shape[0]
        copy = pltpu.make_async_copy(ref, buffer.at[pl.ds(s * rows, rows)], sems.at[s])
        copy.start()
        copies.append(copy)
    return copies


def start_columns(refs, buffer, sems):
    copies = []
    for s, ref in enumerate(refs):
        target = buffer.at[s // 2, :, pl.ds(128 * (s % 2), 128)]
        copy = pltpu.make_async_copy(ref, target, sems.at[s])
        copy.start()
        copies.append(copy)
    return copies


def feed_critical(ids, *rest):
    h_refs, c_refs, feed_ref, down_refs = rest[:8], rest[8:16], rest[16], rest[17:22]
    even_ref, odd_ref, delta_ref, mixed_ref, dt, own_ref = rest[25:31]
    fat_refs = rest[31:34]
    hs, cs, gu, db, h_sems, c_sems = rest[34:]
    passed = rest[22:25]
    c_copies = start_columns(c_refs, cs, c_sems)
    h_copies = start_stack(h_refs, hs, h_sems)
    d = ids[0]
    for j in range(4):
        gu[240 * j : 240 * (j + 1), :] = feed_ref[360 * j : 360 * j + 240, :]
    place_exchanged(down_refs, passed, d, db, unfold_block)
    dt[...] = jnp.concatenate([db[i] for i in range(8)], 0).astype(BF16)
    units = dt.shape[1]

    for c in range(4):
        for copy in h_copies[2 * c : 2 * c + 2] + c_copies[2 * c : 2 * c + 2]:
            copy.wait()
        rows = slice(256 * c, 256 * (c + 1))
        both = dot(hs[rows, :], gu[...])
        mixed_grad = contract_first(cs[c], dt[...])
        gate = both[:, :units]
        up = both[:, units:]
        sig = 1.0 / (1.0 + jnp.exp(-gate))
        silu = gate * sig
        mixed_ref[rows, :] = (silu * up).astype(BF16)
        gate_delta = (mixed_grad * up * sig * (1.0 + gate * (1.0 - sig))).astype(BF16)
        up_delta = (mixed_grad * silu).astype(BF16)
        deltas = jnp.concatenate([gate_delta, up_delta], 1)
        delta_ref[rows, :] = deltas
        back = contract_last(deltas, gu[...])
        even_ref[c] = back[:128]
        odd_ref[128 * c : 128 * (c + 1), :960] = back[128:].astype(BF16)
    for j in range(4):
        part = jnp.zeros((240, 320), F32)
        for c in range(4):
            rows = slice(256 * c, 256 * (c + 1))
            part = part + dot(cs[c, 240 * j : 240 * (j + 1), :], mixed_ref[rows, :])
        db[2 * j] = part[:120]
        db[2 * j + 1] = part[120:]
    filler = jnp.zeros((8, 960), F32)
    own_ref[...] = jnp.concatenate([flatten_block(db[d]), filler], 0).astype(BF16)
    for i in range(4):
        block = jnp.concatenate([flatten_block(db[d ^ (2 * i + 1)]), filler], 0)
        odd_ref[512 + 48 * i : 560 + 48 * i, :960] = block.astype(BF16)
    for i in (1, 2, 3):
        block = jnp.concatenate([flatten_block(db[d ^ (2 * i)]), filler], 0)
        fat_refs[i - 1][...] = block.astype(BF16)


def pair_sum_down(even_ref, odd_ref, *rest):
    fat_refs, own_ref, pair_ref = rest[:3], rest[3], rest[4]
    rows = own_ref.shape[0]
    own_ref[...] = even_ref[0] + odd_ref[:rows, :960].astype(F32)
    pair_ref[...] = odd_ref[4 * rows : 4 * rows + 48, :960]
    for i, ref in enumerate(rest[5:], 1):
        total = even_ref[i] + odd_ref[rows * i : rows * (i + 1), :960].astype(F32)
        ref[:rows] = total.astype(BF16)
        start = 4 * rows + 48 * i
        blocks = [fat_refs[i - 1][...].astype(F32)[:40], odd_ref[start : start + 48, :960].astype(F32)[:40]]
        ref[rows:] = jnp.concatenate(blocks, 0).astype(BF16)


def pair_sum(even_ref, odd_ref, *rest):
    own_ref, a_ref, b_ref, c_ref = rest[-4:]
    rows = own_ref.shape[0]
    own_ref[...] = even_ref[0] + odd_ref[:rows, :960].astype(F32)
    for i, ref in ((1, a_ref), (2, b_ref), (3, c_ref)):
        ref[...] = (even_ref[i] + odd_ref[rows * i : rows * (i + 1), :960].astype(F32)).astype(BF16)


def feed_rest(*rest):
    h_refs, dt, delta_ref, mixed_ref = rest[:8], rest[8], rest[9], rest[10]
    grad_ref, even_ref, odd_ref, hs, h_sems = rest[12:]
    for copy in start_stack(h_refs, hs, h_sems):
        copy.wait()
    for j in range(4):
        part = contract_first(hs[:, 240 * j : 240 * (j + 1)], delta_ref[...])
        grad_ref[240 * j : 240 * (j + 1), :] = part.astype(BF16)
    down = dt[...]
    for c in range(4):
        part = contract_last(mixed_ref[256 * c : 256 * (c + 1), :], down)
        even_ref[c] = part[:128]
        odd_ref[128 * c : 128 * (c + 1), :960] = part[128:].astype(BF16)


def spread_line(buffer, parts, f, offset):
    for j, part in enumerate(parts):
        buffer[2 * (f ^ j) + offset, :, :120] = part[:, :120]
        buffer[2 * (f ^ j ^ 2) + offset, :, :120] = part[:, 120:240]


def attention_backward(ids, *rest):
    own_ref, a_ref, b_ref, c_ref, cot_ref, x2_ref, x_ref, gains_ref = rest[:8]
    cos_ref, sin_ref, qr_ref, kr_ref, vr_ref, probs_ref = rest[8:14]
    first, second = rest[14:22], rest[22:30]
    block_ref, pair_ref = rest[30:32]
    outs = rest[-15:-7]
    grad_ref, down_ref, fb, db, eb, gb, jb = rest[-7:]
    d = ids[0]
    f = ids[1]
    length = x_ref.shape[1]
    gain_one = gains_ref[0, :1]
    gain_two = gains_ref[1, :1]
    dh2 = (
        own_ref[...]
        + a_ref[:128].astype(F32)
        + b_ref[:128].astype(F32)
        + c_ref[:128].astype(F32)
    )
    jb[d] = restore_block(block_ref[...].astype(F32)[:40])
    jb[d ^ 1] = restore_block(pair_ref[...].astype(F32)[:40])
    for i, ref in ((1, a_ref), (2, b_ref), (3, c_ref)):
        both = ref[128:].astype(F32)
        jb[d ^ (2 * i)] = restore_block(both[:40])
        jb[d ^ (2 * i + 1)] = restore_block(both[40:])
    for j in range(4):
        both = jnp.concatenate([jb[2 * j], jb[2 * j + 1]], 1)
        down_ref[120 * j : 120 * (j + 1), :] = both.astype(BF16)
    x2 = x2_ref[...]
    scale_two = lax.rsqrt(jnp.mean(x2 * x2, -1, keepdims=True) + EPS)
    unit = x2 * scale_two
    feed_gain_grad = jnp.sum(dh2 * unit, 0, keepdims=True)
    scaled = dh2 * gain_two
    dx2 = cot_ref[...].astype(F32).T + scale_two * (
        scaled - unit * jnp.mean(scaled * unit, -1, keepdims=True)
    )
    rounded = dx2.astype(BF16)
    for i, block in enumerate(blocks_of(rounded, 120)):
        db[i, :, :120] = block
    left = [jnp.zeros((length, 240), F32)] * 2
    right = [jnp.zeros((length, 240), F32)] * 2
    for s in range(8):
        mine = db[d ^ s][:, :120]
        for_left = pad_lanes(mine, 72, 256)
        for_right = pad_lanes(mine, 64, 256)
        left[0] = left[0] + contract_last(for_left, first[s][:240, 128:384])
        left[1] = left[1] + contract_last(for_left, second[s][:240, 128:384])
        right[0] = right[0] + contract_last(for_right, first[s][:240, 256:512])
        right[1] = right[1] + contract_last(for_right, second[s][:240, 256:512])
    spread_line(fb, left, f, 0)
    spread_line(fb, right, f, 1)
    grad = jnp.concatenate([fb[i][:, :120] for i in range(8)], 1).astype(BF16)
    cosines = cos_ref[...]
    sines = sin_ref[...]
    dq, dk, dv = [], [], []
    for g in range(KV_HEADS):
        qr = qr_ref[g]
        kr = kr_ref[g]
        vr = vr_ref[g]
        grads = jnp.concatenate(
            [grad[:, h * HD : (h + 1) * HD] for h in range(g * GROUP, (g + 1) * GROUP)], 0
        )
        probs = probs_ref[g]
        dv.append(contract_first(probs.astype(BF16), grads).astype(BF16))
        dprob = contract_last(grads, vr)
        inner = jnp.sum(probs * dprob, -1, keepdims=True)
        ds = (probs * (dprob - inner) * HD ** (-0.5)).astype(BF16)
        dqg = dot(ds, kr)
        dkg = contract_first(ds, qr)
        dk.append((dkg * cosines - turn(dkg * sines)).astype(BF16))
        for i in range(GROUP):
            part = dqg[i * length : (i + 1) * length]
            dq.append((part * cosines - turn(part * sines)).astype(BF16))
    dq = blocks_of(jnp.concatenate(dq, 1), 120)
    dk = blocks_of(jnp.concatenate(dk, 1), 40)
    dv = blocks_of(jnp.concatenate(dv, 1), 40)
    for i in range(8):
        eb[i, :, :200] = jnp.concatenate([dq[i], dk[i], dv[i]], 1)
    left = [jnp.zeros((length, 240), F32)] * 2
    right = [jnp.zeros((length, 240), F32)] * 2
    for s in range(8):
        mine = eb[d ^ s][:, :200]
        for_left = pad_lanes(mine, 0, 256)
        for_right = pad_lanes(mine, 56, 256)
        left[0] = left[0] + contract_last(for_left, first[s][:240, 0:256])
        left[1] = left[1] + contract_last(for_left, second[s][:240, 0:256])
        right[0] = right[0] + contract_last(for_right, first[s][:240, 384:640])
        right[1] = right[1] + contract_last(for_right, second[s][:240, 384:640])
    spread_line(fb, left, f, 0)
    spread_line(fb, right, f, 1)
    dh1 = jnp.concatenate([fb[i][:, :120] for i in range(8)], 1)
    x = x_ref[...].astype(F32).T
    scale_one = lax.rsqrt(jnp.mean(x * x, -1, keepdims=True) + EPS)
    unit = x * scale_one
    attention_gain_grad = jnp.sum(dh1 * unit, 0, keepdims=True)
    scaled = dh1 * gain_one
    input_grad = dx2 + scale_one * (
        scaled - unit * jnp.mean(scaled * unit, -1, keepdims=True)
    )
    grad_ref[...] = input_grad.T
    for i in range(8):
        row = jnp.concatenate(
            [feed_gain_grad[:, 120 * i : 120 * (i + 1)], attention_gain_grad[:, 120 * i : 120 * (i + 1)]], 1
        )
        gb[i] = jnp.broadcast_to(pad_lanes(row, 0, 640), (16, 640))
    half = length // 2
    for s in range(8):
        delta = eb[d ^ s][:, :200]
        mine = db[d ^ s][:, :120]
        outs[s][:half] = jnp.concatenate(
            [delta[:half], mine[:half], mine[half:], delta[half:]], 1
        )
        outs[s][half:] = gb[d ^ s].astype(BF16)


def attention_weights(ids, *rest):
    x_refs, att_ref, got, gains_ref = rest[:8], rest[8], rest[9:17], rest[17]
    own_ref, g1_ref, g2_ref, g3_ref, hs, dl, acc = rest[21:]
    d = ids[0]
    f = ids[1]
    length = 128
    half = 64
    gain_sum = jnp.zeros((8, 640), F32)
    for s in range(8):
        block = got[s][:half]
        start = pl.multiple_of(length * (d ^ s), length)
        dl[pl.ds(start, half), 0:320] = block[:, :320]
        dl[pl.ds(start + half, half), 0:320] = jnp.concatenate(
            [block[:, 440:], block[:, 320:440]], 1
        )
        gain_sum = gain_sum + got[s][half : half + 8].astype(F32)
    gain_one = gains_ref[0].T[:, :1]
    for s in range(8):
        x = x_refs[s][...].astype(F32)
        scale = lax.rsqrt(jnp.mean(x * x, 0, keepdims=True) + EPS)
        start = pl.multiple_of(length * (d ^ s), length)
        hs[:, pl.ds(start, length)] = (x * scale * gain_one).astype(BF16)
    qkv = dot(hs[...], dl[:, :200]).T
    out = contract_first(dl[:, 200:320], att_ref[...])
    both = jnp.concatenate([qkv, out], 0)
    for i in range(4):
        acc[i, :320, :240] = both[:, 240 * i : 240 * (i + 1)]
        acc[i, 320:, :240] = jnp.concatenate([gain_sum[:, :240]] * 2, 0)
    own_ref[...] = acc[f][:, :240]
    for j, ref in ((1, g1_ref), (2, g2_ref), (3, g3_ref)):
        ref[...] = acc[f ^ j][:, :240].astype(BF16)


def finish_feed(sum_ref, _, gate_ref, up_ref):
    total = sum_ref[...].astype(F32).T
    gate_ref[...] = total[:320]
    up_ref[...] = total[320:]


def finish_output(x2_ref, own_ref, a_ref, b_ref, c_ref, out_ref):
    total = (
        x2_ref[...]
        + own_ref[...]
        + a_ref[...].astype(F32)
        + b_ref[...].astype(F32)
        + c_ref[...].astype(F32)
    )
    out_ref[...] = total.T.astype(BF16)


def finish_attention(own_ref, a_ref, b_ref, c_ref, down_ref, *rest):
    q_ref, k_ref, v_ref, o_ref, ag_ref, fg_ref, down_out = rest[-7:]
    down_out[...] = down_ref[...].astype(F32)
    total = (
        own_ref[...] + a_ref[...].astype(F32) + b_ref[...].astype(F32) + c_ref[...].astype(F32)
    )
    q_ref[...] = total[:120].T
    k_ref[...] = total[120:160]
    v_ref[...] = total[160:200]
    o_ref[...] = total[200:320].T
    fg_ref[...] = total[320:321, :120]
    ag_ref[...] = total[320:321, 120:240]


def fast(
    hidden_in,
    segment_ids,
    positions,
    query_weight,
    key_weight,
    value_weight,
    output_weight,
    attention_gain,
    gate_weight,
    up_weight,
    down_weight,
    feedforward_gain,
    output_cotangent,
):
    hidden = hidden_in[0].T
    cotangent = output_cotangent[0].T
    features, length = hidden.shape
    d = lax.axis_index("dp")
    f = lax.axis_index("fsdp")
    ids = jnp.stack([d, f]).astype(jnp.int32)
    tokens = 8 * length

    (block,) = kernel_call(
        pack_attention,
        [shape((120, 640), BF16)],
        [query_weight, key_weight.T, value_weight.T, output_weight],
    )
    far = [send(cotangent, "dp", s) for s in (2, 4, 6)]
    cotangent_slots = [cotangent, send(cotangent, "dp", 1)]
    for other in far:
        cotangent_slots += [other, send(other, "dp", 1)]
    line = send(block, "fsdp", 2)
    (chunk_a,) = kernel_call(
        join_lines,
        [shape((256, 640), BF16)],
        [block, line, attention_gain[None], feedforward_gain[None], *far],
        [None] * 4 + ["any"] * 3,
    )
    chunk_b = send(chunk_a, "fsdp", 1)
    a_near, a_far = send(chunk_a, "dp", 2), send(chunk_a, "dp", 4)
    chunk_b = after(chunk_b, a_near, a_far)
    b_near, b_far = send(chunk_b, "dp", 4), send(chunk_b, "dp", 2)
    a_near, b_near = after_all([a_near, b_near])
    a_last, b_last = send(a_near, "dp", 4), send(b_near, "dp", 2)
    first, second = [], []
    for value in (chunk_a, a_near, a_far, a_last):
        first += [value, send(value, "dp", 1)]
    for value in (chunk_b, b_far, b_near, b_last):
        second += [value, send(value, "dp", 1)]

    (feed,) = kernel_call(
        pack_feed,
        [shape((360, 640), BF16)],
        [gate_weight.T, up_weight.T, down_weight.T, chunk_b],
        [None, None, None, "any"],
    )
    feed = lax.all_gather(feed, "fsdp", axis=0, tiled=True)

    cosines, sines = rotary_tables(positions[0], HD)
    x2, h2, attended, qr, kr, vr, probs, gains = kernel_call(
        attention_forward,
        [
            shape((length, features), F32),
            shape((length, features), BF16),
            shape((length, features), BF16),
            shape((KV_HEADS, GROUP * length, HD), BF16),
            shape((KV_HEADS, length, HD), BF16),
            shape((KV_HEADS, length, HD), BF16),
            shape((KV_HEADS, GROUP * length, length), F32),
            shape((2, 8, features), F32),
        ],
        [ids, hidden, cosines, sines, segment_ids, *first, *second],
        ["smem"] + [None] * 20,
        [
            pltpu.VMEM((8, length, 128), BF16),
            pltpu.VMEM((8, length, 256), F32),
            pltpu.VMEM((8, 8, 256), F32),
        ],
        16,
        10.0,
    )
    hidden_rows = after(hidden, b_near, b_far)
    far = [send(hidden_rows, "dp", s) for s in (2, 4, 6)]
    hidden_slots = [hidden_rows, send(hidden_rows, "dp", 1)]
    for other in far:
        hidden_slots += [other, send(other, "dp", 1)]
    down_blocks = kernel_call(
        split_down,
        exchange_shapes(),
        [ids, feed, h2, *far],
        ["smem", None] + ["any"] * 4,
        [pltpu.VMEM((8, 120, 320), F32)],
    )
    down_blocks = exchange(down_blocks)
    others = after_all([send(h2, "dp", s) for s in (2, 4, 6)], *down_blocks[1:])
    down_passed = [send(value, "dp", 1) for value in down_blocks[2:]]
    h2_slots = [h2, send(h2, "dp", 1)]
    for other in others:
        h2_slots += [other, send(other, "dp", 1)]
    attended = after(attended, *others, *down_passed)
    attended = lax.all_gather(attended, "dp", axis=0, tiled=True)
    even, odd, deltas, mixed, down, own_block, *fats = kernel_call(
        feed_critical,
        [
            shape((4, length, features), F32),
            shape((4 * length + 192, 1024), BF16),
            shape((tokens, 640), BF16),
            shape((tokens, 320), BF16),
            shape((features, 320), BF16),
            shape((48, 960), BF16),
        ]
        + [shape((48, 960), BF16)] * 3,
        [ids, *h2_slots, *cotangent_slots, feed, *down_blocks, *down_passed],
        ["smem"] + ["any"] * 16 + [None] * 9,
        [
            pltpu.VMEM((tokens, features), BF16),
            pltpu.VMEM((4, features, 256), BF16),
            pltpu.VMEM((features, 640), BF16),
            pltpu.VMEM((8, 120, 320), F32),
            pltpu.SemaphoreType.DMA((8,)),
            pltpu.SemaphoreType.DMA((8,)),
        ],
        24,
        11.0,
    )

    odd = send(odd, "dp", 1)
    back_own, pair_block, back_a, back_b, back_c = kernel_call(
        pair_sum_down,
        [shape((length, features), F32), shape((48, features), BF16)]
        + [shape((length + 80, features), BF16)] * 3,
        [even, odd, *fats],
    )
    back_a, back_b, back_c = send(back_a, "dp", 2), send(back_b, "dp", 4), send(back_c, "dp", 6)
    feed_grad, f_even, f_odd = kernel_call(
        feed_rest,
        [
            shape((4 * 240, 640), BF16),
            shape((4, length, features), F32),
            shape((4 * length, 1024), BF16),
        ],
        [*h2_slots, down, deltas, mixed, back_own],
        ["any"] * 8 + [None] * 3 + ["any"],
        [
            pltpu.VMEM((tokens, features), BF16),
            pltpu.SemaphoreType.DMA((8,)),
        ],
        24,
        4.0,
    )
    feed_grad = after(feed_grad, back_a, back_b, back_c, attended)
    feed_sum = lax.psum_scatter(feed_grad, "fsdp", scatter_dimension=0, tiled=True)
    *outgoing, input_grad, down_grad = kernel_call(
        attention_backward,
        [shape((80, 640), BF16)] * 8
        + [shape((features, length), F32), shape((4 * 120, 640), BF16)],
        [
            ids, back_own, back_a, back_b, back_c, cotangent, x2, hidden, gains,
            cosines, sines, qr, kr, vr, probs, *first, *second, own_block,
            pair_block, feed_grad,
        ],
        ["smem"] + [None] * 32 + ["any"],
        [
            pltpu.VMEM((8, length, 128), F32),
            pltpu.VMEM((8, length, 128), BF16),
            pltpu.VMEM((8, length, 256), BF16),
            pltpu.VMEM((8, 16, 640), F32),
            pltpu.VMEM((8, 120, 320), F32),
        ],
        18,
        12.0,
    )
    arrived = [outgoing[0]] + [send(outgoing[s], "dp", s) for s in range(1, 8)]
    f_odd = send(f_odd, "dp", 1)
    y_own, *y_parts = kernel_call(
        pair_sum,
        [shape((length, features), F32)] + [shape((length, features), BF16)] * 3,
        [f_even, f_odd, outgoing[0]],
        [None, None, "any"],
    )
    down_sum = lax.psum_scatter(down_grad, "fsdp", scatter_dimension=0, tiled=True)
    w0, w1, w2, w3 = kernel_call(
        attention_weights,
        [shape((336, 240), F32)] + [shape((336, 240), BF16)] * 3,
        [ids, *hidden_slots, attended, *arrived, gains, y_own, down_grad, feed_sum],
        ["smem"] + [None] * 18 + ["any"] * 3,
        [
            pltpu.VMEM((features, tokens), BF16),
            pltpu.VMEM((tokens, 320), BF16),
            pltpu.VMEM((4, 336, 256), F32),
        ],
        20,
        6.5,
    )

    y_parts = after_all(y_parts, w0)
    sums = [y_own] + [send(part, "dp", 2 * i + 2) for i, part in enumerate(y_parts)]
    parts = [send(w, "fsdp", j) for j, w in ((1, w1), (2, w2), (3, w3))]
    gate_out, up_out = kernel_call(
        finish_feed, [shape((320, 240), F32)] * 2, [feed_sum, parts[0]], [None, "any"]
    )
    (block_output,) = kernel_call(
        finish_output, [shape((features, length), BF16)], [x2, *sums]
    )
    q_out, k_out, v_out, o_out, ag_out, fg_out, down_out = kernel_call(
        finish_attention,
        [
            shape((240, 120), F32),
            shape((40, 240), F32),
            shape((40, 240), F32),
            shape((240, 120), F32),
            shape((1, 120), F32),
            shape((1, 120), F32),
            shape((120, 640), F32),
        ],
        [w0, *parts, down_sum, block_output, gate_out],
        [None] * 5 + ["any"] * 2,
    )
    return (
        block_output.T[None],
        input_grad.T[None],
        q_out,
        k_out.T,
        v_out.T,
        o_out,
        ag_out[0],
        gate_out.T,
        up_out.T,
        down_out.T,
        fg_out[0],
    )


def fits(mesh_shape):
    return mesh_shape["dp"] == 8 and mesh_shape["fsdp"] == 4


def solution(mesh):
    in_specs = (
        P(("dp", "fsdp"), None, None),
        P(("dp", "fsdp"), None),
        P(("dp", "fsdp"), None),
        P("fsdp", "dp"),
        P("fsdp", "dp"),
        P("fsdp", "dp"),
        P("fsdp", "dp"),
        P("dp"),
        P("fsdp", "dp"),
        P("fsdp", "dp"),
        P("fsdp", "dp"),
        P("dp"),
        P(("dp", "fsdp"), None, None),
    )
    out_specs = (
        P(("dp", "fsdp"), None, None),
        P(("dp", "fsdp"), None, None),
        P("fsdp", "dp"),
        P("fsdp", "dp"),
        P("fsdp", "dp"),
        P("fsdp", "dp"),
        P("dp"),
        P("fsdp", "dp"),
        P("fsdp", "dp"),
        P("fsdp", "dp"),
        P("dp"),
    )
    body = fast if fits(mesh.shape) else local
    return jax.shard_map(body, mesh=mesh, in_specs=in_specs, out_specs=out_specs, check_vma=False)
```

```python
import jax
import jax.numpy as jnp
from jax import lax
from jax.experimental import pallas as pl
from jax.experimental.pallas import tpu as pltpu
from jax.sharding import PartitionSpec as P

HEADS = 15
KV_HEADS = 5
HD = 64
GROUP = HEADS // KV_HEADS


EPS = 1e-05
THETA = 100000.0
NEGATIVE = -1e30
F32 = jnp.float32
BF16 = jnp.bfloat16


def rotary_tables(position, head_dim):
    inverse = THETA ** (-jnp.arange(0, head_dim, 2).astype(F32) / head_dim)
    angles = position.astype(F32)[:, None] * inverse[None, :]
    cosines = jnp.cos(angles)
    sine_values = jnp.sin(angles)
    return (
        jnp.concatenate([cosines, cosines], -1),
        jnp.concatenate([sine_values, sine_values], -1),
    )


def rotate(values, cosines, sine_values):
    half_dim = values.shape[-1] // 2
    turned = jnp.concatenate([-values[..., half_dim:], values[..., :half_dim]], -1)
    return values * cosines[:, None, :] + turned * sine_values[:, None, :]


def rotate_back(gradient, cosines, sine_values):
    half_dim = gradient.shape[-1] // 2
    sine_scaled = gradient * sine_values[:, None, :]
    turned = jnp.concatenate([-sine_scaled[..., half_dim:], sine_scaled[..., :half_dim]], -1)
    return gradient * cosines[:, None, :] - turned


def row_scale_of(values):
    return lax.rsqrt(jnp.mean(values * values, -1, keepdims=True) + EPS)


def norm_backward(values, row_scale, gain, upstream):
    unit_rows = values * row_scale
    scaled = upstream * gain
    gain_grad = jnp.sum(upstream * unit_rows, 0)
    result = row_scale * (scaled - unit_rows * jnp.mean(scaled * unit_rows, -1, keepdims=True))
    return (result, gain_grad)


def dot(left, right):
    return jnp.dot(left, right, preferred_element_type=F32)


def contract_first(left, right):
    return lax.dot_general(left, right, (((0,), (0,)), ((), ())), preferred_element_type=F32)


def contract_last(left, right):
    return lax.dot_general(left, right, (((1,), (1,)), ((), ())), preferred_element_type=F32)


def send(values, axis, distance):
    count = lax.axis_size(axis)
    return lax.ppermute(values, axis, [(i, i ^ distance) for i in range(count)])


def pick(blocks, index):
    return lax.dynamic_index_in_dim(blocks, index, 0, keepdims=False)


def reorder(blocks, me):
    return jnp.stack([pick(blocks, me ^ s) for s in range(blocks.shape[0])])


def plane_gather(values):
    count = lax.axis_size("dp")
    if count != 8:
        return reorder(lax.all_gather(values, "dp"), lax.axis_index("dp"))
    slots = [values, send(values, "dp", 1)] + [None] * 6
    for s in (2, 4, 6):
        slots[s] = send(values, "dp", s)
        slots[s + 1] = send(slots[s], "dp", 1)
    return jnp.stack(slots)


def plane_exchange(blocks):
    count = lax.axis_size("dp")
    if count != 8:
        me = lax.axis_index("dp")
        return reorder(lax.all_to_all(reorder(blocks, me), "dp", 0, 0), me)
    return jnp.stack([blocks[0]] + [send(blocks[s], "dp", s) for s in range(1, 8)])


def plane_sum(blocks):
    count = lax.axis_size("dp")
    if count != 8:
        return jnp.sum(plane_exchange(blocks.astype(BF16)).astype(F32), 0)
    odd = send(jnp.stack([blocks[s] for s in (1, 3, 5, 7)]).astype(BF16), "dp", 1)
    pair = [blocks[2 * i] + odd[i].astype(F32) for i in range(4)]
    total = pair[0]
    for i in range(1, 4):
        total = total + send(pair[i].astype(BF16), "dp", 2 * i).astype(F32)
    return total


def line_gather(values):
    me = lax.axis_index("fsdp")
    count = lax.axis_size("fsdp")
    out = jnp.zeros((count,) + values.shape, values.dtype)
    out = lax.dynamic_update_index_in_dim(out, values, me, 0)
    for s in range(1, count):
        out = lax.dynamic_update_index_in_dim(out, send(values, "fsdp", s), me ^ s, 0)
    return out


def line_sum(blocks):
    me = lax.axis_index("fsdp")
    total = pick(blocks, me)
    for s in range(1, lax.axis_size("fsdp")):
        total = total + send(pick(blocks, me ^ s).astype(BF16), "fsdp", s).astype(F32)
    return total


def down_routes(dp_count, fsdp_count):
    ratio = dp_count // fsdp_count
    routes = []
    for m in range(ratio):
        pairs = []
        for d in range(dp_count):
            for f in range(fsdp_count):
                target = (ratio * f + (m + d) % ratio) * fsdp_count + d // ratio
                pairs.append((d * fsdp_count + f, target))
        routes.append(pairs)
    return routes


def down_pieces(down_turned, dp_count, fsdp_count):
    ratio = dp_count // fsdp_count
    d = lax.axis_index("dp")
    width = down_turned.shape[1] // ratio
    halves = jnp.stack([down_turned[:, h * width : (h + 1) * width] for h in range(ratio)])
    got = [
        lax.ppermute(pick(halves, (m + d) % ratio), ("dp", "fsdp"), pairs)
        for m, pairs in enumerate(down_routes(dp_count, fsdp_count))
    ]
    stacked = jnp.stack(got)
    ordered = [pick(stacked, (d - j) % ratio) for j in range(ratio)]
    return jnp.concatenate(ordered, 0)


def down_return(grad_turned, dp_count, fsdp_count):
    ratio = dp_count // fsdp_count
    d = lax.axis_index("dp")
    height = grad_turned.shape[0] // ratio
    pieces = grad_turned.reshape(ratio, height, grad_turned.shape[1])
    got = []
    for m, pairs in enumerate(down_routes(dp_count, fsdp_count)):
        back = [(target, source) for source, target in pairs]
        got.append(lax.ppermute(pick(pieces, (d - m) % ratio), ("dp", "fsdp"), back))
    stacked = jnp.stack(got)
    return jnp.concatenate([pick(stacked, (h - d) % ratio) for h in range(ratio)], 1)


def masked_scores(query_turned, key_turned, segment):
    length = query_turned.shape[0]
    grouped = query_turned.reshape(length, KV_HEADS, GROUP, HD)
    scores = jnp.einsum("qkgd,tkd->kgqt", grouped, key_turned, preferred_element_type=F32)
    index = jnp.arange(length)
    allowed = (segment[:, None] == segment[None, :]) & (index[:, None] >= index[None, :])
    return jnp.where(allowed, scores * HD ** (-0.5), NEGATIVE)


def attend_forward(query_turned, key_turned, value_rounded, segment):
    length = query_turned.shape[0]
    scores = masked_scores(query_turned, key_turned, segment)
    row_max = jnp.max(scores, -1, keepdims=True)
    exponentials = jnp.exp(scores - row_max)
    totals = jnp.sum(exponentials, -1, keepdims=True)
    probs_rounded = (exponentials / totals).astype(BF16)
    attended = jnp.einsum("kgqt,tkd->qkgd", probs_rounded, value_rounded, preferred_element_type=F32)
    return (attended.reshape(length, HEADS * HD).astype(BF16), row_max + jnp.log(totals))


def attend_backward(query_turned, key_turned, value_rounded, segment, log_totals, attended_grad):
    length = query_turned.shape[0]
    grouped = query_turned.reshape(length, KV_HEADS, GROUP, HD)
    grad_grouped = attended_grad.reshape(length, KV_HEADS, GROUP, HD)
    scores = masked_scores(query_turned, key_turned, segment)
    probs_again = jnp.exp(scores - log_totals)
    value_sum = jnp.einsum(
        "kgqt,qkgd->tkd", probs_again.astype(BF16), grad_grouped, preferred_element_type=F32
    )
    prob_grad = jnp.einsum(
        "qkgd,tkd->kgqt", grad_grouped, value_rounded, preferred_element_type=F32
    )
    inner_rows = jnp.sum(probs_again * prob_grad, -1, keepdims=True)
    score_grad = (probs_again * (prob_grad - inner_rows) * HD ** (-0.5)).astype(BF16)
    query_part = jnp.einsum("kgqt,tkd->qkgd", score_grad, key_turned, preferred_element_type=F32)
    key_sum = jnp.einsum("kgqt,qkgd->tkd", score_grad, grouped, preferred_element_type=F32)
    return (query_part.reshape(length, HEADS, HD), key_sum, value_sum)


def local(
    hidden_in,
    segment_ids,
    positions,
    query_weight,
    key_weight,
    value_weight,
    output_weight,
    attention_gain,
    gate_weight,
    up_weight,
    down_weight,
    feedforward_gain,
    output_cotangent,
):
    hidden = hidden_in[0]
    hidden_rows = hidden.astype(F32)
    segment = segment_ids[0]
    cotangent = output_cotangent[0]
    length, features = hidden.shape
    width = HEADS * HD
    kv_width = KV_HEADS * HD
    dp_count = lax.axis_size("dp")
    fsdp_count = lax.axis_size("fsdp")
    d = lax.axis_index("dp")
    f = lax.axis_index("fsdp")
    q_cols = width // dp_count
    kv_cols = kv_width // dp_count
    x_cols = features // dp_count
    own_rows = features // fsdp_count
    qkv_cols = q_cols + 2 * kv_cols
    all_cols = qkv_cols + x_cols
    hidden_units = gate_weight.shape[1]

    attention_block = jnp.concatenate(
        [query_weight, key_weight, value_weight, output_weight], 1
    )
    attention_rows = line_gather(attention_block).reshape(features, all_cols)
    gains = jnp.concatenate(
        [attention_gain, feedforward_gain, jnp.zeros((all_cols - 2 * x_cols,), BF16)]
    )
    gains = jnp.concatenate([gains[None], jnp.zeros((15, all_cols), BF16)])
    slots = plane_gather(jnp.concatenate([attention_rows, gains], 0))
    gains_ordered = reorder(slots[:, features, :], d)
    attention_gain_full = gains_ordered[:, :x_cols].reshape(features).astype(F32)
    feed_gain_full = gains_ordered[:, x_cols : 2 * x_cols].reshape(features).astype(F32)
    qkv_slots = slots[:, :features, :qkv_cols]
    output_slots = slots[:, :features, qkv_cols:]

    down_block = down_pieces(down_weight.T, dp_count, fsdp_count)
    feed_block = jnp.concatenate([gate_weight, up_weight, down_block], 1)
    feed = line_gather(feed_block).reshape(features, 3 * hidden_units)

    tokens = plane_gather(jnp.stack([hidden, cotangent]))
    hidden_all = tokens[:, 0].reshape(dp_count * length, features)
    cotangent_all = tokens[:, 1].reshape(dp_count * length, features)

    scale_one = row_scale_of(hidden_rows)
    normed_one = (hidden_rows * scale_one * attention_gain_full).astype(BF16)
    cosines, sine_values = rotary_tables(positions[0], HD)
    qkv = reorder(jnp.einsum("td,sdc->stc", normed_one, qkv_slots, preferred_element_type=F32), d)

    def columns(start, count):
        part = qkv[:, :, start : start + count]
        return part.transpose(1, 0, 2).reshape(length, dp_count * count)

    query_proj = columns(0, q_cols).reshape(length, HEADS, HD)
    key_proj = columns(q_cols, kv_cols).reshape(length, KV_HEADS, HD)
    value_proj = columns(q_cols + kv_cols, kv_cols).reshape(length, KV_HEADS, HD)
    query_turned = rotate(query_proj, cosines, sine_values).astype(BF16)
    key_turned = rotate(key_proj, cosines, sine_values).astype(BF16)
    value_rounded = value_proj.astype(BF16)
    attended, log_totals = attend_forward(query_turned, key_turned, value_rounded, segment)
    added = reorder(jnp.einsum("td,sdc->stc", attended, output_slots, preferred_element_type=F32), d)
    residual = hidden_rows + added.transpose(1, 0, 2).reshape(length, features)

    scale_two = row_scale_of(residual)
    normed_two = (residual * scale_two * feed_gain_full).astype(BF16)
    normed_two_all = plane_gather(normed_two).reshape(dp_count * length, features)
    gate_up = feed[:, : 2 * hidden_units]
    down_turned = feed[:, 2 * hidden_units :]
    both = dot(normed_two_all, gate_up)
    gate_proj = both[:, :hidden_units]
    up_proj = both[:, hidden_units:]
    mixed_grad = dot(cotangent_all, down_turned)
    sigmoid_gate = jax.nn.sigmoid(gate_proj)
    silu_gate = gate_proj * sigmoid_gate
    mixed = (silu_gate * up_proj).astype(BF16)
    gate_delta = (
        mixed_grad * up_proj * sigmoid_gate * (1.0 + gate_proj * (1.0 - sigmoid_gate))
    ).astype(BF16)
    up_delta = (mixed_grad * silu_gate).astype(BF16)
    deltas = jnp.concatenate([gate_delta, up_delta], 1)
    normed_two_grad = plane_sum(
        contract_last(deltas, gate_up).reshape(dp_count, length, features)
    )
    gate_up_grad = contract_first(normed_two_all, deltas)
    down_grad = contract_first(cotangent_all, mixed)
    feed_grad = jnp.concatenate([gate_up_grad, down_grad], 1).reshape(
        fsdp_count, own_rows, 3 * hidden_units
    )
    fed = plane_sum(contract_last(mixed, down_turned).reshape(dp_count, length, features))
    block_output = (residual + fed).astype(BF16)
    attended_all = plane_gather(attended).reshape(dp_count * length, width)

    residual_part, feed_gain_grad = norm_backward(
        residual, scale_two, feed_gain_full, normed_two_grad
    )
    residual_grad = cotangent.astype(F32) + residual_part
    feed_sum = line_sum(feed_grad)

    residual_rounded = residual_grad.astype(BF16)
    residual_blocks = residual_rounded.reshape(length, dp_count, x_cols).transpose(1, 0, 2)
    residual_slots = reorder(residual_blocks, d)
    attended_grad = jnp.einsum(
        "stc,sdc->td", residual_slots, output_slots, preferred_element_type=F32
    ).astype(BF16)
    query_raw, key_raw, value_raw = attend_backward(
        query_turned, key_turned, value_rounded, segment, log_totals, attended_grad
    )
    query_delta = rotate_back(query_raw, cosines, sine_values).astype(BF16)
    key_delta = rotate_back(key_raw, cosines, sine_values).astype(BF16)
    value_delta = value_raw.astype(BF16)
    qkv_delta = jnp.concatenate(
        [
            part.reshape(length, dp_count, -1).transpose(1, 0, 2)
            for part in (query_delta, key_delta, value_delta)
        ],
        2,
    )
    delta_slots = reorder(qkv_delta, d)
    normed_one_grad = jnp.einsum(
        "stc,sdc->td", delta_slots, qkv_slots, preferred_element_type=F32
    )
    input_part, attention_gain_grad = norm_backward(
        hidden_rows, scale_one, attention_gain_full, normed_one_grad
    )
    input_grad = residual_grad + input_part

    gain_rows = jnp.concatenate(
        [
            feed_gain_grad.reshape(dp_count, 1, x_cols),
            attention_gain_grad.reshape(dp_count, 1, x_cols),
            jnp.zeros((dp_count, 1, all_cols - 2 * x_cols), F32),
        ],
        2,
    ).astype(BF16)
    gain_rows = jnp.pad(reorder(gain_rows, d), ((0, 0), (0, 15), (0, 0)))
    outgoing = jnp.concatenate(
        [jnp.concatenate([delta_slots, residual_slots], 2), gain_rows], 1
    )
    arrived = plane_exchange(outgoing)
    deltas_all = arrived[:, :length].reshape(dp_count * length, all_cols)
    gain_sums = jnp.sum(arrived[:, length].astype(F32), 0)
    hidden_all_rows = hidden_all.astype(F32)
    normed_one_all = (
        hidden_all_rows * row_scale_of(hidden_all_rows) * attention_gain_full
    ).astype(BF16)
    qkv_grad = contract_first(normed_one_all, deltas_all[:, :qkv_cols])
    output_grad = contract_first(attended_all, deltas_all[:, qkv_cols:])
    attention_grad = jnp.concatenate([qkv_grad, output_grad], 1).reshape(
        fsdp_count, own_rows, all_cols
    )
    gain_block = jnp.broadcast_to(
        jnp.pad(gain_sums[None], ((0, 15), (0, 0)))[None], (fsdp_count, 16, all_cols)
    )
    attention_sum = line_sum(jnp.concatenate([attention_grad, gain_block], 1))
    down_out = down_return(feed_sum[:, 2 * hidden_units :], dp_count, fsdp_count).T

    ends = (q_cols, q_cols + kv_cols, qkv_cols)
    return (
        block_output[None],
        input_grad[None],
        attention_sum[:own_rows, : ends[0]],
        attention_sum[:own_rows, ends[0] : ends[1]],
        attention_sum[:own_rows, ends[1] : ends[2]],
        attention_sum[:own_rows, ends[2] :],
        attention_sum[own_rows, x_cols : 2 * x_cols],
        feed_sum[:, :hidden_units],
        feed_sum[:, hidden_units : 2 * hidden_units],
        down_out,
        attention_sum[own_rows, :x_cols],
    )


def vspec():
    return pl.BlockSpec(memory_space=pltpu.VMEM)


def kernel_call(body, outs, args, specs=None, scratch=(), megabytes=8, micros=1.0):
    if specs is None:
        specs = [None] * len(args)
    kinds = {
        None: pltpu.VMEM,
        "any": pl.ANY,
        "smem": pltpu.SMEM,
    }
    return pl.pallas_call(
        body,
        out_shape=outs,
        in_specs=[pl.BlockSpec(memory_space=kinds[s]) for s in specs],
        out_specs=[pl.BlockSpec(memory_space=pltpu.VMEM) for _ in outs],
        scratch_shapes=list(scratch),
        compiler_params=pltpu.CompilerParams(vmem_limit_bytes=63 * 2**20),
        cost_estimate=pl.CostEstimate(
            flops=int(micros * 1.1e9), bytes_accessed=int(micros * 3.0e6), transcendentals=0
        ),
    )(*args)


def after_all(values, *others):
    count = len(values)
    return pl.pallas_call(
        lambda *refs: None,
        out_shape=[shape(value.shape, value.dtype) for value in values],
        in_specs=[pl.BlockSpec(memory_space=pl.ANY)] * (count + len(others)),
        out_specs=[pl.BlockSpec(memory_space=pl.ANY)] * count,
        input_output_aliases={i: i for i in range(count)},
    )(*values, *others)


def after(value, *others):
    return after_all([value], *others)[0]


def shape(dims, dtype):
    return jax.ShapeDtypeStruct(dims, dtype)


def blocks_of(values, width):
    return [values[:, i : i + width] for i in range(0, values.shape[1], width)]


def turn(values):
    half = values.shape[-1] // 2
    return jnp.concatenate([-values[:, half:], values[:, :half]], 1)


def pad_lanes(values, before, total):
    rows, count = values.shape
    parts = []
    if before:
        parts.append(jnp.zeros((rows, before), values.dtype))
    parts.append(values)
    if total - before - count:
        parts.append(jnp.zeros((rows, total - before - count), values.dtype))
    return jnp.concatenate(parts, 1)


def pack_attention(q_ref, k_ref, v_ref, o_ref, out_ref):
    kv = jnp.concatenate([k_ref[...], v_ref[...]], 0).astype(F32).T.astype(BF16)
    qkv = jnp.concatenate([q_ref[...], kv], 1)
    o = o_ref[...]
    half = o.shape[0] // 2
    out_ref[...] = jnp.concatenate([qkv[:half], o[:half], o[half:], qkv[half:]], 1)


def pack_feed(gate_ref, up_ref, down_ref, _, out_ref):
    gate_up = jnp.concatenate([gate_ref[...], up_ref[...]], 0).astype(F32).T
    rows = gate_up.shape[0]
    out_ref[:rows] = gate_up.astype(BF16)
    out_ref[rows:] = down_ref[...]


def fold_block(block):
    tail = jnp.concatenate([block[64:], jnp.zeros((8, 320), F32)], 0)
    return jnp.concatenate([block[:64], tail], 1).astype(BF16)


def unfold_block(both):
    both = both.astype(F32)
    return jnp.concatenate([both[:, :320], both[:56, 320:]], 0)


def fill_exchange(outs, buffer, d):
    outs[0][...] = fold_block(buffer[d])
    outs[1][...] = fold_block(buffer[d ^ 1])
    for i in (1, 2, 3):
        outs[i + 1][:64] = fold_block(buffer[d ^ (2 * i)])
        outs[i + 1][64:] = fold_block(buffer[d ^ (2 * i + 1)])


def place_exchanged(refs, passed, d, buffer, convert):
    buffer[d] = convert(refs[0][...])
    buffer[d ^ 1] = convert(refs[1][...])
    for i in (1, 2, 3):
        buffer[d ^ (2 * i)] = convert(refs[i + 1][:64])
        buffer[d ^ (2 * i + 1)] = convert(passed[i - 1][64:])


def exchange_shapes():
    return [shape((64, 640), BF16)] * 2 + [shape((128, 640), BF16)] * 3


def exchange(blocks):
    arrived = [blocks[0], send(blocks[1], "dp", 1)]
    return arrived + [send(blocks[i + 1], "dp", 2 * i) for i in (1, 2, 3)]


def split_down(ids, feed_ref, *rest):
    outs, buffer = rest[-6:-1], rest[-1]
    for i in range(8):
        start = 360 * (i // 2) + 240
        buffer[i] = feed_ref[start : start + 120, 320 * (i % 2) : 320 * (i % 2) + 320].astype(F32)
    fill_exchange(outs, buffer, ids[0])


def flatten_block(block):
    return jnp.concatenate([block[:40], block[40:80], block[80:]], 1)


def restore_block(rows):
    return jnp.concatenate([rows[:, :320], rows[:, 320:640], rows[:, 640:960]], 0)


def join_lines(own_ref, got_ref, ag_ref, fg_ref, *rest):
    out_ref = rest[-1]
    half = own_ref.shape[0]
    out_ref[: 2 * half] = jnp.concatenate([own_ref[...], got_ref[...]], 0)
    gains = jnp.concatenate([ag_ref[...], fg_ref[...]], 1)
    row = pad_lanes(gains, 0, out_ref.shape[1])
    out_ref[2 * half :] = jnp.broadcast_to(row, (16, out_ref.shape[1]))


def line_blocks(buffer, f, offset):
    return [
        jnp.concatenate(
            [buffer[2 * (f ^ j) + offset][:, :120], buffer[2 * (f ^ j ^ 2) + offset][:, :120]], 1
        )
        for j in (0, 1)
    ]


def mask_bias(seg_ref):
    length = seg_ref.shape[1]
    keys = jnp.broadcast_to(seg_ref[...].astype(F32), (length, length))
    index_q = lax.broadcasted_iota(jnp.int32, (length, length), 0)
    index_k = lax.broadcasted_iota(jnp.int32, (length, length), 1)
    allowed = (keys.T == keys) & (index_q >= index_k)
    return jnp.concatenate([jnp.where(allowed, 0.0, NEGATIVE)] * GROUP, 0)


def attention_forward(
    ids, x_ref, cos_ref, sin_ref, seg_ref, *rest
):
    first = rest[:8]
    second = rest[8:16]
    (
        x2_ref, h2_ref, att_ref, qr_ref, kr_ref, vr_ref, probs_ref, gains_ref,
        hb, tb, gb,
    ) = rest[16:]
    d = ids[0]
    f = ids[1]
    length = x_ref.shape[1]
    for s in range(8):
        gb[d ^ s] = first[s][240:248, :256].astype(F32)
    gain_one = jnp.concatenate([gb[i][:, :120] for i in range(8)], 1)
    gain_two = jnp.concatenate([gb[i][:, 120:240] for i in range(8)], 1)
    gains_ref[0] = gain_one
    gains_ref[1] = gain_two
    x = x_ref[...].astype(F32).T
    scale = lax.rsqrt(jnp.mean(x * x, -1, keepdims=True) + EPS)
    h1 = (x * scale * gain_one[:1]).astype(BF16)
    for i, block in enumerate(blocks_of(h1, 120)):
        hb[i, :, :120] = block
    left = line_blocks(hb, f, 0)
    right = line_blocks(hb, f, 1)
    for s in range(8):
        a = dot(left[0], first[s][:240, 0:256]) + dot(left[1], second[s][:240, 0:256])
        b = dot(right[0], first[s][:240, 384:640]) + dot(right[1], second[s][:240, 384:640])
        tb[d ^ s, :, :200] = a[:, :200] + b[:, 56:256]
    parts = [tb[i] for i in range(8)]
    q = jnp.concatenate([p[:, :120] for p in parts], 1)
    k = jnp.concatenate([p[:, 120:160] for p in parts], 1)
    v = jnp.concatenate([p[:, 160:200] for p in parts], 1)
    cosines = cos_ref[...]
    sines = sin_ref[...]
    bias = mask_bias(seg_ref)
    heads = []
    for g in range(KV_HEADS):
        kg = k[:, g * HD : (g + 1) * HD]
        kr = (kg * cosines + turn(kg) * sines).astype(BF16)
        vr = v[:, g * HD : (g + 1) * HD].astype(BF16)
        rows = []
        for h in range(g * GROUP, (g + 1) * GROUP):
            qh = q[:, h * HD : (h + 1) * HD]
            rows.append((qh * cosines + turn(qh) * sines).astype(BF16))
        qr = jnp.concatenate(rows, 0)
        qr_ref[g] = qr
        kr_ref[g] = kr
        vr_ref[g] = vr
        scores = contract_last(qr, kr) * HD ** (-0.5) + bias
        top = jnp.max(scores, -1, keepdims=True)
        exps = jnp.exp(scores - top)
        totals = jnp.sum(exps, -1, keepdims=True)
        probs = exps / totals
        probs_ref[g] = probs
        probs = probs.astype(BF16)
        out = dot(probs, vr).astype(BF16)
        heads += [out[i * length : (i + 1) * length] for i in range(GROUP)]
    attended = jnp.concatenate(heads, 1)
    att_ref[...] = attended
    for i, block in enumerate(blocks_of(attended, 120)):
        hb[i, :, :120] = block
    left = line_blocks(hb, f, 0)
    right = line_blocks(hb, f, 1)
    for s in range(8):
        a = dot(left[0], first[s][:240, 128:384]) + dot(left[1], second[s][:240, 128:384])
        b = dot(right[0], first[s][:240, 256:512]) + dot(right[1], second[s][:240, 256:512])
        tb[d ^ s, :, :120] = a[:, 72:192] + b[:, 64:184]
    x2 = x + jnp.concatenate([tb[i][:, :120] for i in range(8)], 1)
    x2_ref[...] = x2
    scale_two = lax.rsqrt(jnp.mean(x2 * x2, -1, keepdims=True) + EPS)
    h2_ref[...] = (x2 * scale_two * gain_two[:1]).astype(BF16)


def start_stack(refs, buffer, sems):
    copies = []
    for s, ref in enumerate(refs):
        rows = ref.shape[0]
        copy = pltpu.make_async_copy(ref, buffer.at[pl.ds(s * rows, rows)], sems.at[s])
        copy.start()
        copies.append(copy)
    return copies


def start_columns(refs, buffer, sems):
    copies = []
    for s, ref in enumerate(refs):
        target = buffer.at[s // 2, :, pl.ds(128 * (s % 2), 128)]
        copy = pltpu.make_async_copy(ref, target, sems.at[s])
        copy.start()
        copies.append(copy)
    return copies


def feed_critical(ids, *rest):
    h_refs, c_refs, feed_ref, down_refs = rest[:8], rest[8:16], rest[16], rest[17:22]
    even_ref, odd_ref, delta_ref, mixed_ref, dt, own_ref = rest[25:31]
    fat_refs = rest[31:34]
    hs, cs, gu, db, h_sems, c_sems = rest[34:]
    passed = rest[22:25]
    c_copies = start_columns(c_refs, cs, c_sems)
    h_copies = start_stack(h_refs, hs, h_sems)
    d = ids[0]
    for j in range(4):
        gu[240 * j : 240 * (j + 1), :] = feed_ref[360 * j : 360 * j + 240, :]
    place_exchanged(down_refs, passed, d, db, unfold_block)
    dt[...] = jnp.concatenate([db[i] for i in range(8)], 0).astype(BF16)
    units = dt.shape[1]

    for c in range(4):
        for copy in h_copies[2 * c : 2 * c + 2] + c_copies[2 * c : 2 * c + 2]:
            copy.wait()
        rows = slice(256 * c, 256 * (c + 1))
        both = dot(hs[rows, :], gu[...])
        mixed_grad = contract_first(cs[c], dt[...])
        gate = both[:, :units]
        up = both[:, units:]
        sig = 1.0 / (1.0 + jnp.exp(-gate))
        silu = gate * sig
        mixed_ref[rows, :] = (silu * up).astype(BF16)
        gate_delta = (mixed_grad * up * sig * (1.0 + gate * (1.0 - sig))).astype(BF16)
        up_delta = (mixed_grad * silu).astype(BF16)
        deltas = jnp.concatenate([gate_delta, up_delta], 1)
        delta_ref[rows, :] = deltas
        back = contract_last(deltas, gu[...])
        even_ref[c] = back[:128]
        odd_ref[128 * c : 128 * (c + 1), :960] = back[128:].astype(BF16)
    for j in range(4):
        part = jnp.zeros((240, 320), F32)
        for c in range(4):
            rows = slice(256 * c, 256 * (c + 1))
            part = part + dot(cs[c, 240 * j : 240 * (j + 1), :], mixed_ref[rows, :])
        db[2 * j] = part[:120]
        db[2 * j + 1] = part[120:]
    filler = jnp.zeros((8, 960), F32)
    own_ref[...] = jnp.concatenate([flatten_block(db[d]), filler], 0).astype(BF16)
    for i in range(4):
        block = jnp.concatenate([flatten_block(db[d ^ (2 * i + 1)]), filler], 0)
        odd_ref[512 + 48 * i : 560 + 48 * i, :960] = block.astype(BF16)
    for i in (1, 2, 3):
        block = jnp.concatenate([flatten_block(db[d ^ (2 * i)]), filler], 0)
        fat_refs[i - 1][...] = block.astype(BF16)


def pair_sum_down(even_ref, odd_ref, *rest):
    fat_refs, own_ref, pair_ref = rest[:3], rest[3], rest[4]
    rows = own_ref.shape[0]
    own_ref[...] = even_ref[0] + odd_ref[:rows, :960].astype(F32)
    pair_ref[...] = odd_ref[4 * rows : 4 * rows + 48, :960]
    for i, ref in enumerate(rest[5:], 1):
        total = even_ref[i] + odd_ref[rows * i : rows * (i + 1), :960].astype(F32)
        ref[:rows] = total.astype(BF16)
        start = 4 * rows + 48 * i
        blocks = [fat_refs[i - 1][...].astype(F32)[:40], odd_ref[start : start + 48, :960].astype(F32)[:40]]
        ref[rows:] = jnp.concatenate(blocks, 0).astype(BF16)


def pair_sum(even_ref, odd_ref, *rest):
    own_ref, a_ref, b_ref, c_ref = rest[-4:]
    rows = own_ref.shape[0]
    own_ref[...] = even_ref[0] + odd_ref[:rows, :960].astype(F32)
    for i, ref in ((1, a_ref), (2, b_ref), (3, c_ref)):
        ref[...] = (even_ref[i] + odd_ref[rows * i : rows * (i + 1), :960].astype(F32)).astype(BF16)


def feed_rest(*rest):
    h_refs, dt, delta_ref, mixed_ref = rest[:8], rest[8], rest[9], rest[10]
    grad_ref, even_ref, odd_ref, hs, h_sems = rest[12:]
    for copy in start_stack(h_refs, hs, h_sems):
        copy.wait()
    for j in range(4):
        part = contract_first(hs[:, 240 * j : 240 * (j + 1)], delta_ref[...])
        grad_ref[240 * j : 240 * (j + 1), :] = part.astype(BF16)
    down = dt[...]
    for c in range(4):
        part = contract_last(mixed_ref[256 * c : 256 * (c + 1), :], down)
        even_ref[c] = part[:128]
        odd_ref[128 * c : 128 * (c + 1), :960] = part[128:].astype(BF16)


def spread_line(buffer, parts, f, offset):
    for j, part in enumerate(parts):
        buffer[2 * (f ^ j) + offset, :, :120] = part[:, :120]
        buffer[2 * (f ^ j ^ 2) + offset, :, :120] = part[:, 120:240]


def attention_backward(ids, *rest):
    own_ref, a_ref, b_ref, c_ref, cot_ref, x2_ref, x_ref, gains_ref = rest[:8]
    cos_ref, sin_ref, qr_ref, kr_ref, vr_ref, probs_ref = rest[8:14]
    first, second = rest[14:22], rest[22:30]
    block_ref, pair_ref = rest[30:32]
    outs = rest[-15:-7]
    grad_ref, down_ref, fb, db, eb, gb, jb = rest[-7:]
    d = ids[0]
    f = ids[1]
    length = x_ref.shape[1]
    gain_one = gains_ref[0, :1]
    gain_two = gains_ref[1, :1]
    dh2 = (
        own_ref[...]
        + a_ref[:128].astype(F32)
        + b_ref[:128].astype(F32)
        + c_ref[:128].astype(F32)
    )
    jb[d] = restore_block(block_ref[...].astype(F32)[:40])
    jb[d ^ 1] = restore_block(pair_ref[...].astype(F32)[:40])
    for i, ref in ((1, a_ref), (2, b_ref), (3, c_ref)):
        both = ref[128:].astype(F32)
        jb[d ^ (2 * i)] = restore_block(both[:40])
        jb[d ^ (2 * i + 1)] = restore_block(both[40:])
    for j in range(4):
        both = jnp.concatenate([jb[2 * j], jb[2 * j + 1]], 1)
        down_ref[120 * j : 120 * (j + 1), :] = both.astype(BF16)
    x2 = x2_ref[...]
    scale_two = lax.rsqrt(jnp.mean(x2 * x2, -1, keepdims=True) + EPS)
    unit = x2 * scale_two
    feed_gain_grad = jnp.sum(dh2 * unit, 0, keepdims=True)
    scaled = dh2 * gain_two
    dx2 = cot_ref[...].astype(F32).T + scale_two * (
        scaled - unit * jnp.mean(scaled * unit, -1, keepdims=True)
    )
    rounded = dx2.astype(BF16)
    for i, block in enumerate(blocks_of(rounded, 120)):
        db[i, :, :120] = block
    left = [jnp.zeros((length, 240), F32)] * 2
    right = [jnp.zeros((length, 240), F32)] * 2
    for s in range(8):
        mine = db[d ^ s][:, :120]
        for_left = pad_lanes(mine, 72, 256)
        for_right = pad_lanes(mine, 64, 256)
        left[0] = left[0] + contract_last(for_left, first[s][:240, 128:384])
        left[1] = left[1] + contract_last(for_left, second[s][:240, 128:384])
        right[0] = right[0] + contract_last(for_right, first[s][:240, 256:512])
        right[1] = right[1] + contract_last(for_right, second[s][:240, 256:512])
    spread_line(fb, left, f, 0)
    spread_line(fb, right, f, 1)
    grad = jnp.concatenate([fb[i][:, :120] for i in range(8)], 1).astype(BF16)
    cosines = cos_ref[...]
    sines = sin_ref[...]
    dq, dk, dv = [], [], []
    for g in range(KV_HEADS):
        qr = qr_ref[g]
        kr = kr_ref[g]
        vr = vr_ref[g]
        grads = jnp.concatenate(
            [grad[:, h * HD : (h + 1) * HD] for h in range(g * GROUP, (g + 1) * GROUP)], 0
        )
        probs = probs_ref[g]
        dv.append(contract_first(probs.astype(BF16), grads).astype(BF16))
        dprob = contract_last(grads, vr)
        inner = jnp.sum(probs * dprob, -1, keepdims=True)
        ds = (probs * (dprob - inner) * HD ** (-0.5)).astype(BF16)
        dqg = dot(ds, kr)
        dkg = contract_first(ds, qr)
        dk.append((dkg * cosines - turn(dkg * sines)).astype(BF16))
        for i in range(GROUP):
            part = dqg[i * length : (i + 1) * length]
            dq.append((part * cosines - turn(part * sines)).astype(BF16))
    dq = blocks_of(jnp.concatenate(dq, 1), 120)
    dk = blocks_of(jnp.concatenate(dk, 1), 40)
    dv = blocks_of(jnp.concatenate(dv, 1), 40)
    for i in range(8):
        eb[i, :, :200] = jnp.concatenate([dq[i], dk[i], dv[i]], 1)
    left = [jnp.zeros((length, 240), F32)] * 2
    right = [jnp.zeros((length, 240), F32)] * 2
    for s in range(8):
        mine = eb[d ^ s][:, :200]
        for_left = pad_lanes(mine, 0, 256)
        for_right = pad_lanes(mine, 56, 256)
        left[0] = left[0] + contract_last(for_left, first[s][:240, 0:256])
        left[1] = left[1] + contract_last(for_left, second[s][:240, 0:256])
        right[0] = right[0] + contract_last(for_right, first[s][:240, 384:640])
        right[1] = right[1] + contract_last(for_right, second[s][:240, 384:640])
    spread_line(fb, left, f, 0)
    spread_line(fb, right, f, 1)
    dh1 = jnp.concatenate([fb[i][:, :120] for i in range(8)], 1)
    x = x_ref[...].astype(F32).T
    scale_one = lax.rsqrt(jnp.mean(x * x, -1, keepdims=True) + EPS)
    unit = x * scale_one
    attention_gain_grad = jnp.sum(dh1 * unit, 0, keepdims=True)
    scaled = dh1 * gain_one
    input_grad = dx2 + scale_one * (
        scaled - unit * jnp.mean(scaled * unit, -1, keepdims=True)
    )
    grad_ref[...] = input_grad.T
    for i in range(8):
        row = jnp.concatenate(
            [feed_gain_grad[:, 120 * i : 120 * (i + 1)], attention_gain_grad[:, 120 * i : 120 * (i + 1)]], 1
        )
        gb[i] = jnp.broadcast_to(pad_lanes(row, 0, 640), (16, 640))
    half = length // 2
    for s in range(8):
        delta = eb[d ^ s][:, :200]
        mine = db[d ^ s][:, :120]
        outs[s][:half] = jnp.concatenate(
            [delta[:half], mine[:half], mine[half:], delta[half:]], 1
        )
        outs[s][half:] = gb[d ^ s].astype(BF16)


def attention_weights(ids, *rest):
    x_refs, att_ref, got, gains_ref = rest[:8], rest[8], rest[9:17], rest[17]
    own_ref, g1_ref, g2_ref, g3_ref, hs, dl, acc = rest[21:]
    d = ids[0]
    f = ids[1]
    length = 128
    half = 64
    gain_sum = jnp.zeros((8, 640), F32)
    for s in range(8):
        block = got[s][:half]
        start = pl.multiple_of(length * (d ^ s), length)
        dl[pl.ds(start, half), 0:320] = block[:, :320]
        dl[pl.ds(start + half, half), 0:320] = jnp.concatenate(
            [block[:, 440:], block[:, 320:440]], 1
        )
        gain_sum = gain_sum + got[s][half : half + 8].astype(F32)
    gain_one = gains_ref[0].T[:, :1]
    for s in range(8):
        x = x_refs[s][...].astype(F32)
        scale = lax.rsqrt(jnp.mean(x * x, 0, keepdims=True) + EPS)
        start = pl.multiple_of(length * (d ^ s), length)
        hs[:, pl.ds(start, length)] = (x * scale * gain_one).astype(BF16)
    qkv = dot(hs[...], dl[:, :200]).T
    out = contract_first(dl[:, 200:320], att_ref[...])
    both = jnp.concatenate([qkv, out], 0)
    for i in range(4):
        acc[i, :320, :240] = both[:, 240 * i : 240 * (i + 1)]
        acc[i, 320:, :240] = jnp.concatenate([gain_sum[:, :240]] * 2, 0)
    own_ref[...] = acc[f][:, :240]
    for j, ref in ((1, g1_ref), (2, g2_ref), (3, g3_ref)):
        ref[...] = acc[f ^ j][:, :240].astype(BF16)


def finish_feed(sum_ref, _, gate_ref, up_ref):
    total = sum_ref[...].astype(F32).T
    gate_ref[...] = total[:320]
    up_ref[...] = total[320:]


def finish_output(x2_ref, own_ref, a_ref, b_ref, c_ref, out_ref):
    total = (
        x2_ref[...]
        + own_ref[...]
        + a_ref[...].astype(F32)
        + b_ref[...].astype(F32)
        + c_ref[...].astype(F32)
    )
    out_ref[...] = total.T.astype(BF16)


def finish_attention(own_ref, a_ref, b_ref, c_ref, down_ref, *rest):
    q_ref, k_ref, v_ref, o_ref, ag_ref, fg_ref, down_out = rest[-7:]
    down_out[...] = down_ref[...].astype(F32)
    total = (
        own_ref[...] + a_ref[...].astype(F32) + b_ref[...].astype(F32) + c_ref[...].astype(F32)
    )
    q_ref[...] = total[:120].T
    k_ref[...] = total[120:160]
    v_ref[...] = total[160:200]
    o_ref[...] = total[200:320].T
    fg_ref[...] = total[320:321, :120]
    ag_ref[...] = total[320:321, 120:240]


def fast(
    hidden_in,
    segment_ids,
    positions,
    query_weight,
    key_weight,
    value_weight,
    output_weight,
    attention_gain,
    gate_weight,
    up_weight,
    down_weight,
    feedforward_gain,
    output_cotangent,
):
    hidden = hidden_in[0].T
    cotangent = output_cotangent[0].T
    features, length = hidden.shape
    d = lax.axis_index("dp")
    f = lax.axis_index("fsdp")
    ids = jnp.stack([d, f]).astype(jnp.int32)
    tokens = 8 * length

    (block,) = kernel_call(
        pack_attention,
        [shape((120, 640), BF16)],
        [query_weight, key_weight.T, value_weight.T, output_weight],
    )
    far = [send(cotangent, "dp", s) for s in (2, 4, 6)]
    cotangent_slots = [cotangent, send(cotangent, "dp", 1)]
    for other in far:
        cotangent_slots += [other, send(other, "dp", 1)]
    line = send(block, "fsdp", 2)
    (chunk_a,) = kernel_call(
        join_lines,
        [shape((256, 640), BF16)],
        [block, line, attention_gain[None], feedforward_gain[None], *far],
        [None] * 4 + ["any"] * 3,
    )
    chunk_b = send(chunk_a, "fsdp", 1)
    a_near, a_far = send(chunk_a, "dp", 2), send(chunk_a, "dp", 4)
    chunk_b = after(chunk_b, a_near, a_far)
    b_near, b_far = send(chunk_b, "dp", 4), send(chunk_b, "dp", 2)
    a_near, b_near = after_all([a_near, b_near])
    a_last, b_last = send(a_near, "dp", 4), send(b_near, "dp", 2)
    first, second = [], []
    for value in (chunk_a, a_near, a_far, a_last):
        first += [value, send(value, "dp", 1)]
    for value in (chunk_b, b_far, b_near, b_last):
        second += [value, send(value, "dp", 1)]

    (feed,) = kernel_call(
        pack_feed,
        [shape((360, 640), BF16)],
        [gate_weight.T, up_weight.T, down_weight.T, chunk_b],
        [None, None, None, "any"],
    )
    feed = lax.all_gather(feed, "fsdp", axis=0, tiled=True)

    cosines, sines = rotary_tables(positions[0], HD)
    x2, h2, attended, qr, kr, vr, probs, gains = kernel_call(
        attention_forward,
        [
            shape((length, features), F32),
            shape((length, features), BF16),
            shape((length, features), BF16),
            shape((KV_HEADS, GROUP * length, HD), BF16),
            shape((KV_HEADS, length, HD), BF16),
            shape((KV_HEADS, length, HD), BF16),
            shape((KV_HEADS, GROUP * length, length), F32),
            shape((2, 8, features), F32),
        ],
        [ids, hidden, cosines, sines, segment_ids, *first, *second],
        ["smem"] + [None] * 20,
        [
            pltpu.VMEM((8, length, 128), BF16),
            pltpu.VMEM((8, length, 256), F32),
            pltpu.VMEM((8, 8, 256), F32),
        ],
        16,
        10.0,
    )
    hidden_rows = after(hidden, b_near, b_far)
    far = [send(hidden_rows, "dp", s) for s in (2, 4, 6)]
    hidden_slots = [hidden_rows, send(hidden_rows, "dp", 1)]
    for other in far:
        hidden_slots += [other, send(other, "dp", 1)]
    down_blocks = kernel_call(
        split_down,
        exchange_shapes(),
        [ids, feed, h2, *far],
        ["smem", None] + ["any"] * 4,
        [pltpu.VMEM((8, 120, 320), F32)],
    )
    down_blocks = exchange(down_blocks)
    near = send(h2, "dp", 2)
    others = after_all([near, send(h2, "dp", 4), send(near, "dp", 4)], *down_blocks[1:])
    down_passed = [send(value, "dp", 1) for value in down_blocks[2:]]
    h2_slots = [h2, send(h2, "dp", 1)]
    for other in others:
        h2_slots += [other, send(other, "dp", 1)]
    attended = after(attended, *others, *down_passed)
    attended = lax.all_gather(attended, "dp", axis=0, tiled=True)
    even, odd, deltas, mixed, down, own_block, *fats = kernel_call(
        feed_critical,
        [
            shape((4, length, features), F32),
            shape((4 * length + 192, 1024), BF16),
            shape((tokens, 640), BF16),
            shape((tokens, 320), BF16),
            shape((features, 320), BF16),
            shape((48, 960), BF16),
        ]
        + [shape((48, 960), BF16)] * 3,
        [ids, *h2_slots, *cotangent_slots, feed, *down_blocks, *down_passed],
        ["smem"] + ["any"] * 16 + [None] * 9,
        [
            pltpu.VMEM((tokens, features), BF16),
            pltpu.VMEM((4, features, 256), BF16),
            pltpu.VMEM((features, 640), BF16),
            pltpu.VMEM((8, 120, 320), F32),
            pltpu.SemaphoreType.DMA((8,)),
            pltpu.SemaphoreType.DMA((8,)),
        ],
        24,
        11.0,
    )

    odd = send(odd, "dp", 1)
    back_own, pair_block, back_a, back_b, back_c = kernel_call(
        pair_sum_down,
        [shape((length, features), F32), shape((48, features), BF16)]
        + [shape((length + 80, features), BF16)] * 3,
        [even, odd, *fats],
    )
    back_a, back_b, back_c = send(back_a, "dp", 2), send(back_b, "dp", 4), send(back_c, "dp", 6)
    feed_grad, f_even, f_odd = kernel_call(
        feed_rest,
        [
            shape((4 * 240, 640), BF16),
            shape((4, length, features), F32),
            shape((4 * length, 1024), BF16),
        ],
        [*h2_slots, down, deltas, mixed, back_own],
        ["any"] * 8 + [None] * 3 + ["any"],
        [
            pltpu.VMEM((tokens, features), BF16),
            pltpu.SemaphoreType.DMA((8,)),
        ],
        24,
        4.0,
    )
    feed_grad = after(feed_grad, back_a, back_b, back_c, attended)
    feed_sum = lax.psum_scatter(feed_grad, "fsdp", scatter_dimension=0, tiled=True)
    *outgoing, input_grad, down_grad = kernel_call(
        attention_backward,
        [shape((80, 640), BF16)] * 8
        + [shape((features, length), F32), shape((4 * 120, 640), BF16)],
        [
            ids, back_own, back_a, back_b, back_c, cotangent, x2, hidden, gains,
            cosines, sines, qr, kr, vr, probs, *first, *second, own_block,
            pair_block, feed_grad,
        ],
        ["smem"] + [None] * 32 + ["any"],
        [
            pltpu.VMEM((8, length, 128), F32),
            pltpu.VMEM((8, length, 128), BF16),
            pltpu.VMEM((8, length, 256), BF16),
            pltpu.VMEM((8, 16, 640), F32),
            pltpu.VMEM((8, 120, 320), F32),
        ],
        18,
        12.0,
    )
    arrived = [outgoing[0]] + [send(outgoing[s], "dp", s) for s in range(1, 8)]
    f_odd = send(f_odd, "dp", 1)
    y_own, *y_parts = kernel_call(
        pair_sum,
        [shape((length, features), F32)] + [shape((length, features), BF16)] * 3,
        [f_even, f_odd, outgoing[0]],
        [None, None, "any"],
    )
    down_sum = lax.psum_scatter(down_grad, "fsdp", scatter_dimension=0, tiled=True)
    w0, w1, w2, w3 = kernel_call(
        attention_weights,
        [shape((336, 240), F32)] + [shape((336, 240), BF16)] * 3,
        [ids, *hidden_slots, attended, *arrived, gains, y_own, down_grad, feed_sum],
        ["smem"] + [None] * 18 + ["any"] * 3,
        [
            pltpu.VMEM((features, tokens), BF16),
            pltpu.VMEM((tokens, 320), BF16),
            pltpu.VMEM((4, 336, 256), F32),
        ],
        20,
        6.5,
    )

    y_parts = after_all(y_parts, w0)
    sums = [y_own] + [send(part, "dp", 2 * i + 2) for i, part in enumerate(y_parts)]
    parts = [send(w, "fsdp", j) for j, w in ((1, w1), (2, w2), (3, w3))]
    gate_out, up_out = kernel_call(
        finish_feed, [shape((320, 240), F32)] * 2, [feed_sum, parts[0]], [None, "any"]
    )
    (block_output,) = kernel_call(
        finish_output, [shape((features, length), BF16)], [x2, *sums]
    )
    q_out, k_out, v_out, o_out, ag_out, fg_out, down_out = kernel_call(
        finish_attention,
        [
            shape((240, 120), F32),
            shape((40, 240), F32),
            shape((40, 240), F32),
            shape((240, 120), F32),
            shape((1, 120), F32),
            shape((1, 120), F32),
            shape((120, 640), F32),
        ],
        [w0, *parts, down_sum, block_output, gate_out],
        [None] * 5 + ["any"] * 2,
    )
    return (
        block_output.T[None],
        input_grad.T[None],
        q_out,
        k_out.T,
        v_out.T,
        o_out,
        ag_out[0],
        gate_out.T,
        up_out.T,
        down_out.T,
        fg_out[0],
    )


def fits(mesh_shape):
    return mesh_shape["dp"] == 8 and mesh_shape["fsdp"] == 4


def solution(mesh):
    in_specs = (
        P(("dp", "fsdp"), None, None),
        P(("dp", "fsdp"), None),
        P(("dp", "fsdp"), None),
        P("fsdp", "dp"),
        P("fsdp", "dp"),
        P("fsdp", "dp"),
        P("fsdp", "dp"),
        P("dp"),
        P("fsdp", "dp"),
        P("fsdp", "dp"),
        P("fsdp", "dp"),
        P("dp"),
        P(("dp", "fsdp"), None, None),
    )
    out_specs = (
        P(("dp", "fsdp"), None, None),
        P(("dp", "fsdp"), None, None),
        P("fsdp", "dp"),
        P("fsdp", "dp"),
        P("fsdp", "dp"),
        P("fsdp", "dp"),
        P("dp"),
        P("fsdp", "dp"),
        P("fsdp", "dp"),
        P("fsdp", "dp"),
        P("dp"),
    )
    body = fast if fits(mesh.shape) else local
    return jax.shard_map(body, mesh=mesh, in_specs=in_specs, out_specs=out_specs, check_vma=False)
```
